512 devices in a mesh: seq: 32 (over y, x), mp: 16 (over z, core).
Axes of the slice: x: 4, y: 8, z: 8, core: 2. Of those that a mesh axis runs over, the one named last changes fastest.
Arguments:
- frames: bfloat16 [16384, 1024], P('seq', 'mp'), may hold values from -40 to 40
- cotangent: bfloat16 [16384, 1024], P('seq', 'mp'), may hold values from -6 to 6
- query_weight: bfloat16 [1024, 1024], P('mp'), may hold values from -2 to 2
- key_weight: bfloat16 [1024, 1024], P('mp'), may hold values from -2 to 2
- value_weight: bfloat16 [1024, 1024], P('mp'), may hold values from -0.1875 to 0.1875
- out_weight: bfloat16 [1024, 1024], P('mp'), may hold values from -0.1875 to 0.1875
- turn_blocks: int32 [32, 32, 2], replicated, may hold values from -1 to 127, as said below
Outputs:
- attended: bfloat16 [16384, 1024], P('seq', 'mp')
- grad_frames: bfloat16 [16384, 1024], P('seq', 'mp')
- grad_query: float32 [1024, 1024], P('mp')
- grad_key: float32 [1024, 1024], P('mp')
- grad_value: float32 [1024, 1024], P('mp')
- grad_out: float32 [1024, 1024], P('mp')
The draws below stay inside these ranges and needn't reach their ends.
Inputs may be any that keep to these rules, and one draw needn't show every extreme that they name: turn_blocks[d, e, c] is -1 or a block of device d (blocks d * 4 to (d + 1) * 4 - 1); slot c of devices d and e joins block turn_blocks[d, e, c] with block turn_blocks[e, d, c], and the two are -1 together; used slots come before unused ones, the blocks of one (d, e) differ, d = e is all -1; some pair of devices uses all 2 slots.
All inputs are finite; a program needn't handle non-finite values.
Results may differ from the reference program's by a relative error of at most 0.025.
The reference program's roundings to bfloat16 on the way count: a program that leaves them out, or rounds other values in their place, can miss the bound.
Values may be sent and summed in bfloat16 or wider, within the bound.
A program may use at most 128 MiB of HBM per device.

```python
import math
import jax
import jax.numpy as jnp
from jax import lax

D = 1024
HEADS = 16
BLK = 128
BAND = 2
CAP = 2
BLK_DEV = 4
FRAMES = 16384
PEERS = 32


def shared_projection(key):
    return jax.random.normal(key, (D, D), jnp.float32)


def draw_query_weight(key, part):
    common = shared_projection(key)
    key = jax.random.fold_in(key, 5)
    jitter = jax.random.normal(key, (D, D), jnp.float32)
    mixed = 0.98 * common + 0.2 * jitter
    return (mixed * (2.0 / math.sqrt(D))).astype(jnp.bfloat16)


def draw_key_weight(key, part):
    key = jax.random.fold_in(key, 6)
    private = jax.random.normal(key, (D, D), jnp.float32)
    mixed = private
    return (mixed * (1.5 / math.sqrt(D))).astype(jnp.bfloat16)


def draw_frames(key, part):
    key = jax.random.fold_in(key, 7)
    base = jax.random.normal(jax.random.fold_in(key, 1), (FRAMES, D), jnp.float32)
    result = base
    return result.astype(jnp.bfloat16)


def draw_turn_blocks(key, part):
    key = jax.random.fold_in(key, 11)
    peer_count = PEERS
    first_peer = jax.random.randint(jax.random.fold_in(key, 1), (), 0, peer_count)
    other_peer = (first_peer + 1 + jax.random.randint(jax.random.fold_in(key, 2), (), 0, peer_count - 1)) % peer_count
    forced = jnp.minimum(first_peer, other_peer) * peer_count + jnp.maximum(first_peer, other_peer)

    def pair_entry(holder, partner):
        pair_index = jnp.minimum(holder, partner) * peer_count + jnp.maximum(holder, partner)
        pair_key = jax.random.fold_in(key, 100 + pair_index)
        amount = jax.random.randint(jax.random.fold_in(pair_key, 0), (), 0, CAP + 1)
        amount = jnp.where(pair_index == forced, CAP, amount)
        side_pick = jnp.where(holder < partner, 1, 2)
        block_order = jax.random.permutation(jax.random.fold_in(pair_key, side_pick), BLK_DEV)
        slot_index = jnp.arange(CAP)
        chosen = holder * BLK_DEV + block_order[:CAP]
        slot_live = (slot_index < amount) & (holder != partner)
        return jnp.where(slot_live, chosen, -1).astype(jnp.int32)
    holders = jnp.arange(peer_count)
    return jax.vmap(lambda holder: jax.vmap(lambda partner: pair_entry(holder, partner))(holders))(holders)


def levels(stream_key, dims, cuts, least, largest):
    level = 1.0
    for axis_at, parts in cuts:
        steps = jax.random.uniform(jax.random.fold_in(jax.random.fold_in(stream_key, 6), axis_at), (parts,), jnp.float32, least / len(cuts), largest / len(cuts))
        level = level * jnp.repeat(jnp.exp(steps), dims[axis_at] // parts).reshape((-1,) + (1,) * (len(dims) - 1 - axis_at))
    return level


def scatter_about(rng, dims, width, limit, pieces=(), held_as=jnp.bfloat16):
    entries = width * jax.random.normal(rng, dims, jnp.float32)
    if pieces:
        entries = entries * levels(rng, dims, pieces, -0.22, 0.18)
    return jnp.clip(entries, -limit, limit).astype(held_as)


def setup_inputs(seed: int = 0) -> dict:
    key_of = jax.random.split(jax.random.key(seed), 8)
    frames = draw_frames(jax.random.fold_in(key_of[7], 71), 0)
    cotangent = scatter_about(key_of[1], (FRAMES, D), 1.0, 6.0, ((0, 32), (1, 16)))
    query_weight = draw_query_weight(jax.random.fold_in(key_of[7], 71), 0)
    key_weight = draw_key_weight(jax.random.fold_in(key_of[7], 71), 0)
    value_weight = scatter_about(key_of[4], (D, D), D ** -0.5, 0.1875, ((0, 16),))
    out_weight = scatter_about(key_of[5], (D, D), D ** -0.5, 0.1875, ((0, 16),))
    turn_blocks = draw_turn_blocks(jax.random.fold_in(key_of[7], 71), 0)
    return {"frames": frames, "cotangent": cotangent, "query_weight": query_weight, "key_weight": key_weight, "value_weight": value_weight, "out_weight": out_weight, "turn_blocks": turn_blocks}


def heads_view(tensor, head_count):
    return tensor.reshape(tensor.shape[:-1] + (head_count, tensor.shape[-1] // head_count))

def round_trip(tensor):
    return lax.optimization_barrier(tensor.astype(jnp.bfloat16)).astype(jnp.float32)

def device_attention(query_heads, key_window, value_window, band_valid, query_slots, key_slots, value_slots, far_valid, slot_block, slot_used, grad_heads, grad_slots, score_scale):
    highest = lax.Precision.HIGHEST
    block_count = query_heads.shape[0]
    select = ((slot_block[:, None] == jnp.arange(block_count, dtype=jnp.int32)[None, :]) & slot_used[:, None]).astype(jnp.float32)
    band_scores = jnp.einsum('jqhe,jkhe->jhqk', query_heads, key_window) * score_scale
    band_scores = jnp.where(band_valid[:, None, None, :], band_scores, -jnp.inf)
    far_scores = jnp.einsum('sqhe,skhe->shqk', query_slots, key_slots) * score_scale
    far_scores = jnp.where(far_valid[:, None, None, None], far_scores, -jnp.inf)
    far_top = lax.optimization_barrier(jnp.max(jnp.where(select[:, :, None, None] > 0, lax.optimization_barrier(jnp.max(far_scores, axis=-1))[:, None], -jnp.inf), axis=0))
    row_top = jnp.maximum(lax.optimization_barrier(jnp.max(band_scores, axis=-1)), far_top)
    slot_top = jnp.einsum('sj,jhq->shq', select, row_top, precision=highest)
    band_weight = jnp.exp(band_scores - row_top[..., None])
    far_weight = jnp.exp(far_scores - slot_top[..., None])
    row_total = lax.optimization_barrier(jnp.sum(band_weight, axis=-1)) + jnp.einsum('sj,shq->jhq', select, lax.optimization_barrier(jnp.sum(far_weight, axis=-1)), precision=highest)
    far_part = jnp.einsum('shqk,skhe->sqhe', round_trip(far_weight), value_slots)
    row_sum = jnp.einsum('jhqk,jkhe->jqhe', round_trip(band_weight), value_window) + jnp.einsum('sj,sqhe->jqhe', select, far_part, precision=highest)
    output = row_sum / jnp.transpose(row_total, (0, 2, 1))[..., None]
    row_drift = jnp.transpose(lax.optimization_barrier(jnp.sum(grad_heads * output, axis=-1)), (0, 2, 1))
    band_prob = band_weight / row_total[..., None]
    band_slope = round_trip(band_prob * (jnp.einsum('jqhe,jkhe->jhqk', grad_heads, value_window) - row_drift[..., None]))
    slot_total = jnp.where(slot_used[:, None, None], jnp.einsum('sj,jhq->shq', select, row_total, precision=highest), 1.0)
    slot_drift = jnp.einsum('sj,jhq->shq', select, row_drift, precision=highest)
    far_prob = far_weight / slot_total[..., None]
    far_slope = round_trip(far_prob * (jnp.einsum('sqhe,skhe->shqk', grad_slots, value_slots) - slot_drift[..., None]))
    far_query = jnp.einsum('shqk,skhe->sqhe', far_slope, key_slots)
    query_grad = (jnp.einsum('jhqk,jkhe->jqhe', band_slope, key_window) + jnp.einsum('sj,sqhe->jqhe', select, far_query, precision=highest)) * score_scale
    key_window_grad = jnp.einsum('jhqk,jqhe->jkhe', band_slope, query_heads) * score_scale
    value_window_grad = jnp.einsum('jhqk,jqhe->jkhe', round_trip(band_prob), grad_heads)
    key_slot_grad = jnp.einsum('shqk,sqhe->skhe', far_slope, query_slots) * score_scale
    value_slot_grad = jnp.einsum('shqk,sqhe->skhe', round_trip(far_prob), grad_slots)
    return (output, query_grad, key_window_grad, value_window_grad, key_slot_grad, value_slot_grad)

def reference(frames, cotangent, query_weight, key_weight, value_weight, out_weight, turn_blocks):
    peer_count = turn_blocks.shape[0]
    block_count = BLK_DEV
    all_blocks = block_count * peer_count
    window = 2 * BAND + 1
    head_size = D // HEADS
    score_scale = 1.0 / math.sqrt(head_size)
    joint_weight = jnp.concatenate([query_weight, key_weight, value_weight], axis=0)
    projected = jnp.dot(frames, joint_weight.T, preferred_element_type=jnp.float32).astype(jnp.bfloat16)
    query_blocks = projected[:, :D].reshape(all_blocks, BLK, D)
    keyval_blocks = projected[:, D:].reshape(all_blocks, BLK, 2 * D)
    keyval_padded = jnp.pad(keyval_blocks, ((BAND, BAND), (0, 0), (0, 0)))
    context_grad = jnp.dot(cotangent, out_weight.T, preferred_element_type=jnp.float32).astype(jnp.bfloat16)
    grad_blocks = context_grad.reshape(all_blocks, BLK, D)

    def one_device(grad_store, device):
        first_block = device * block_count
        query_local = lax.dynamic_slice_in_dim(query_blocks, first_block, block_count, 0).astype(jnp.float32)
        grad_local = lax.dynamic_slice_in_dim(grad_blocks, first_block, block_count, 0).astype(jnp.float32)
        region = lax.dynamic_slice_in_dim(keyval_padded, first_block, block_count + 2 * BAND, 0)
        windows = jnp.stack([region[offset:offset + block_count] for offset in range(window)], axis=1)
        windows = windows.reshape(block_count, window * BLK, 2 * D).astype(jnp.float32)
        placed = first_block + jnp.arange(block_count, dtype=jnp.int32)[:, None] + jnp.arange(window, dtype=jnp.int32)[None, :] - BAND
        band_valid = jnp.repeat((placed >= 0) & (placed < all_blocks), BLK, axis=1)
        own_list = lax.dynamic_index_in_dim(turn_blocks, device, 0, keepdims=False).reshape(-1)
        their_list = lax.dynamic_index_in_dim(turn_blocks, device, 1, keepdims=False).reshape(-1)
        slot_used = own_list >= 0
        far_valid = slot_used & (jnp.abs(own_list - their_list) > BAND)
        own_safe = jnp.clip(own_list, 0, all_blocks - 1).astype(jnp.int32)
        their_safe = jnp.clip(their_list, 0, all_blocks - 1).astype(jnp.int32)
        query_slots = query_blocks[own_safe].astype(jnp.float32)
        keyval_slots = keyval_blocks[their_safe].astype(jnp.float32)
        grad_slots = grad_blocks[own_safe].astype(jnp.float32)
        results = device_attention(heads_view(query_local, HEADS), heads_view(windows[..., :D], HEADS), heads_view(windows[..., D:], HEADS), band_valid, heads_view(query_slots, HEADS), heads_view(keyval_slots[..., :D], HEADS), heads_view(keyval_slots[..., D:], HEADS), far_valid, (own_list - first_block).astype(jnp.int32), slot_used, heads_view(grad_local, HEADS), heads_view(grad_slots, HEADS), score_scale)
        output, query_grad, key_window_grad, value_window_grad, key_slot_grad, value_slot_grad = results
        window_grad = jnp.concatenate([key_window_grad.reshape(block_count, window, BLK, D), value_window_grad.reshape(block_count, window, BLK, D)], axis=-1)
        grad_region = lax.dynamic_slice_in_dim(grad_store, first_block, block_count + 2 * BAND, 0)
        for offset in range(window):
            grad_region = grad_region.at[offset:offset + block_count].add(window_grad[:, offset])
        grad_store = lax.dynamic_update_slice_in_dim(grad_store, grad_region, first_block, 0)
        slot_grad = jnp.concatenate([key_slot_grad.reshape(-1, BLK, D), value_slot_grad.reshape(-1, BLK, D)], axis=-1)
        grad_store = grad_store.at[their_safe + BAND].add(jnp.where(slot_used[:, None, None], slot_grad, 0.0))
        return (grad_store, (output.reshape(block_count * BLK, D).astype(jnp.bfloat16), query_grad.reshape(block_count * BLK, D)))
    empty_store = jnp.zeros((all_blocks + 2 * BAND, BLK, 2 * D), jnp.float32)
    grad_store, per_device = lax.scan(one_device, empty_store, jnp.arange(peer_count, dtype=jnp.int32))
    context = per_device[0].reshape(-1, D)
    query_grad = per_device[1].reshape(-1, D)
    keyval_grad = grad_store[BAND:BAND + all_blocks].reshape(-1, 2 * D)
    attended = jnp.dot(context, out_weight, preferred_element_type=jnp.float32).astype(jnp.bfloat16)
    grad_out = jnp.dot(context.T, cotangent, preferred_element_type=jnp.float32)
    joint_grad = jnp.concatenate([query_grad, keyval_grad], axis=1).astype(jnp.bfloat16)
    grad_frames = jnp.dot(joint_grad, joint_weight, preferred_element_type=jnp.float32).astype(jnp.bfloat16)
    weight_grad = jnp.dot(joint_grad.T, frames, preferred_element_type=jnp.float32)
    return (attended, grad_frames, weight_grad[:D], weight_grad[D:2 * D], weight_grad[2 * D:], grad_out)
```

```python
import functools
import math

import jax
import jax.numpy as jnp
from jax import lax
from jax.experimental import pallas as pl
from jax.experimental.pallas import tpu as pltpu
from jax.sharding import PartitionSpec as P

D = 1024
HEADS = 16
BLK = 128
BAND = 2
RING_X = 4
HEAD = D // HEADS
PAIR = 2 * HEAD
UNROLL = 4
SCALE = 1.0 / math.sqrt(HEAD)
EXP2_SCALE = SCALE * math.log2(math.e)
MESH = pl.DeviceIdType.MESH
VMEM = pl.BlockSpec(memory_space=pltpu.VMEM)
SMEM = pl.BlockSpec(memory_space=pltpu.SMEM)
ANY = pl.BlockSpec(memory_space=pl.ANY)
LIMIT = 50 * 1024 * 1024


def wrap(index, count):
    return lax.rem(index + count, count)


def greet(devices):
    barrier = pltpu.get_barrier_semaphore()
    for device in devices:
        pl.semaphore_signal(barrier, inc=1, device_id=device, device_id_type=MESH)
    pl.semaphore_wait(barrier, len(devices))


def remote(source, target, send, recv, device):
    return pltpu.make_async_remote_copy(
        source, target, send, recv, device_id=device, device_id_type=MESH
    )


def take(process, count):
    for _ in range(count):
        next(process, None)


def finish(process):
    for _ in process:
        pass


def fill_weights(refs, whole):
    for index, ref in enumerate(refs):
        whole[index * HEAD : (index + 1) * HEAD] = ref[...]


def places():
    me_mp, me = lax.axis_index("mp"), lax.axis_index("seq")
    chips, count_y = lax.axis_size("mp") // 2, lax.axis_size("seq") // RING_X
    return lax.div(me_mp, 2), lax.rem(me_mp, 2), lax.div(me, RING_X), lax.rem(me, RING_X), chips, count_y


def neighbours(at_y, at_x, count_y):
    return {
        ("x", 1): {"seq": at_y * RING_X + wrap(at_x + 1, RING_X)},
        ("x", -1): {"seq": at_y * RING_X + wrap(at_x - 1, RING_X)},
        ("y", 1): {"seq": wrap(at_y + 1, count_y) * RING_X + at_x},
        ("y", -1): {"seq": wrap(at_y - 1, count_y) * RING_X + at_x},
    }


@functools.cache
def ring_plan(count_y, count_x):
    sizes = {"x": count_x, "y": count_y}
    timed = []

    def ring(kind, axis, at, begin):
        count = sizes[axis]
        for hop in range(1, count // 2 + 1):
            for way in (1, -1):
                far = -way * (hop - 1)
                spot = (far, at) if axis == "x" else (at, far)
                half = None if hop < count // 2 else (0 if way == 1 else 1)
                timed.append((begin + hop - 1, kind, axis, way, spot[0], spot[1], half))

    def steps(count):
        near = [(sign * hop, hop) for hop in range(1, count // 2) for sign in (-1, 1)]
        return [(0, 0)] + near + [(count // 2, count // 2)]

    ring(0, "x", 0, 0)
    ring(1, "y", 0, 0)
    for dx, begin in steps(count_x):
        ring(0, "y", dx, begin)
    for dy, begin in steps(count_y):
        ring(1, "x", dy, begin)
    timed.sort(key=lambda step: step[0])
    plan = []
    for _, kind, axis, way, dx, dy, half in timed:
        plan.append((kind, axis, way, dx % count_x, dy % count_y, half))
    return tuple(plan)


def ring_gather(own, store, local, send, recv):
    _, _, at_y, at_x, _, count_y = places()
    near = neighbours(at_y, at_x, count_y)
    half_rows = store.shape[1] // 2
    plan = ring_plan(count_y, RING_X)

    def part(ref, kind, half):
        if half is None:
            return ref.at[pl.ds(kind * half_rows, half_rows)]
        quarter = half_rows // 2
        return ref.at[pl.ds(kind * half_rows + half * quarter, quarter)]

    def spot(kind, dx, dy, half):
        slot = wrap(at_y + dy, count_y) * RING_X + wrap(at_x + dx, RING_X)
        return part(store.at[slot], kind, half)

    def copy_of(index, source, target):
        _, axis, way, _, _, _ = plan[index]
        return remote(source, target, send.at[index], recv.at[index], near[axis, way])

    def outgoing(index):
        kind, _, _, dx, dy, half = plan[index]
        target = spot(kind, dx, dy, half)
        return copy_of(index, target if dx or dy else part(own, kind, half), target)

    def tile_in(index):
        kind, axis, way, dx, dy, _ = plan[index]
        if axis == "x":
            return kind, (dx - way) % RING_X, dy
        return kind, dx, (dy - way) % count_y

    def incoming(index):
        target = spot(*tile_in(index), plan[index][-1])
        return copy_of(index, target, target)

    arrivals = {}
    for index in range(len(plan)):
        arrivals.setdefault(tile_in(index), []).append(index)
    keep = pltpu.make_async_copy(own, store.at[at_y * RING_X + at_x], local)
    waited = set()
    for index, (kind, _, _, dx, dy, _) in enumerate(plan):
        if dx or dy:
            for before in arrivals[kind, dx, dy]:
                if before not in waited:
                    waited.add(before)
                    incoming(before).wait_recv()
        outgoing(index).start()
        if index == 0:
            keep.start()
        yield
    for index in range(len(plan)):
        if index not in waited:
            incoming(index).wait_recv()
    yield
    for index in range(len(plan)):
        outgoing(index).wait_send()
    keep.wait()


def ring_sems():
    steps = len(ring_plan(lax.axis_size("seq") // RING_X, RING_X))
    return [
        pltpu.SemaphoreType.DMA,
        pltpu.SemaphoreType.DMA((steps,)),
        pltpu.SemaphoreType.DMA((steps,)),
    ]


def sum_over_mp(partial, out_ref, mine, gift, theirs, chip_sum, tiles, done, pair_send, pair_recv, z_send, z_recv, swap_send, swap_recv):
    chip, core, _, _, chips, _ = places()
    sibling = {"mp": 2 * chip + 1 - core}
    half = mine.shape[1]

    def give(step):
        return remote(gift.at[step], theirs.at[step], pair_send.at[step], pair_recv.at[step], sibling)

    def post(step):
        target = {"mp": 2 * lax.rem(chip + step, chips) + core}
        return remote(chip_sum.at[step], tiles.at[step], z_send.at[step - 1], z_recv.at[step - 1], target)

    order = sorted(range(1, chips), key=lambda step: -min(step, chips - step)) + [0]
    for step in order:
        tile = lax.rem(chip + step, chips)
        gift[step] = partial(tile, 1 - core).astype(jnp.bfloat16)
        give(step).start()
        mine[step] = partial(tile, core)
        yield
    for step in order:
        give(step).wait_recv()
        mine[step] += theirs[step].astype(jnp.float32)
        if step:
            chip_sum[step] = mine[step].astype(jnp.bfloat16)
            post(step).start()
        yield
    total = mine[0]
    for step in reversed(order[:-1]):
        post(step).wait_recv()
        total += tiles[step].astype(jnp.float32)
    done[...] = jnp.transpose(total).astype(jnp.bfloat16)
    columns = pl.ds(pl.multiple_of(core * half, half), half)
    other_columns = pl.ds(pl.multiple_of((1 - core) * half, half), half)
    own_rows = pl.ds(pl.multiple_of(core * HEAD, HEAD), HEAD)
    swap = remote(
        done.at[pl.ds(pl.multiple_of((1 - core) * HEAD, HEAD), HEAD)],
        out_ref.at[:, columns],
        swap_send,
        swap_recv,
        sibling,
    )
    swap.start()
    out_ref[:, columns] = done[own_rows]
    yield
    remote(done.at[own_rows], out_ref.at[:, other_columns], swap_send, swap_recv, sibling).wait_recv()
    swap.wait_send()
    for step in order:
        give(step).wait_send()
        if step:
            post(step).wait_send()


def sum_scratch(rows):
    chips = lax.axis_size("mp") // 2
    half = rows // 2
    dma = pltpu.SemaphoreType.DMA
    some = pltpu.VMEM((chips, half, PAIR), jnp.bfloat16)
    return [
        pltpu.VMEM((chips, half, PAIR), jnp.float32),
        some,
        some,
        some,
        some,
        pltpu.VMEM((PAIR, half), jnp.bfloat16),
        dma((chips,)),
        dma((chips,)),
        dma((chips - 1,)),
        dma((chips - 1,)),
        dma,
        dma,
    ]


def mp_partners(chip, core, chips):
    return [{"mp": 2 * chip + 1 - core}] + [
        {"mp": 2 * lax.rem(chip + step, chips) + core} for step in range(1, chips)
    ]


def seq_partners(at_y, at_x, count_y):
    along_x = [{"seq": at_y * RING_X + lax.rem(at_x + step, RING_X)} for step in range(1, RING_X)]
    along_y = [{"seq": lax.rem(at_y + step, count_y) * RING_X + at_x} for step in range(1, count_y)]
    return along_x, along_y


def half_rows_of(ref, half):
    rows = ref.shape[0] // 2
    return ref[pl.ds(pl.multiple_of(half * rows, rows), rows)]


def project_kernel(
    frames_ref,
    grad_ref,
    key_w,
    value_w,
    query_w,
    out_w,
    features,
    own,
    kv_ref,
    weights,
    mine,
    other,
    pair_send,
    pair_recv,
    z_send,
    z_recv,
    share_send,
    share_recv,
    *ring,
):
    chip, core, at_y, at_x, chips, count_y = places()
    hops = chips // 2
    rows = features.shape[0]
    half, width = rows // 2, chips * PAIR
    sibling = {"mp": 2 * chip + 1 - core}
    right = {"mp": 2 * wrap(chip + 1, chips) + core}
    left = {"mp": 2 * wrap(chip - 1, chips) + core}
    greet([sibling, right, left] + list(neighbours(at_y, at_x, count_y).values()))

    mine[:HEAD] = frames_ref[...]
    mine[HEAD:] = grad_ref[...]
    swap = remote(mine, other, pair_send, pair_recv, sibling)
    swap.start()
    fill_weights((key_w, value_w, query_w, out_w), weights)
    swap.wait()
    column = pl.multiple_of(chip * PAIR, PAIR)
    here, there = mine[...].astype(jnp.float32), other[...].astype(jnp.float32)
    even = jnp.where(core == 0, here, there)
    odd = jnp.where(core == 0, there, here)
    for kind in (0, 1):
        side = slice(kind * HEAD, (kind + 1) * HEAD)
        tile = jnp.transpose(jnp.concatenate([even[side], odd[side]], axis=0))
        features[:, pl.ds(kind * width + column, PAIR)] = tile.astype(jnp.bfloat16)

    def place(kind, tile, whose, way, hop):
        start = pl.multiple_of(kind * width + wrap(tile, chips) * PAIR, PAIR)
        count = half if hop < hops else half // 2
        first = whose * half + (0 if hop < hops else way * count)
        return features.at[pl.ds(pl.multiple_of(first, count), count), pl.ds(start, PAIR)]

    def sent(kind, way, hop):
        spot = place(kind, chip + (1 - hop if way == 0 else hop - 1), core, way, hop)
        at = (kind, way, hop - 1)
        return remote(spot, spot, z_send.at[at], z_recv.at[at], right if way == 0 else left)

    def landed(kind, way, hop):
        spot = place(kind, chip + (-hop if way == 0 else hop), core, way, hop)
        at = (kind, way, hop - 1)
        return remote(spot, spot, z_send.at[at], z_recv.at[at], right if way == 0 else left)

    def shared(kind, way, hop, whose):
        spot = place(kind, chip + (-hop if way == 0 else hop), whose, way, hop)
        at = (kind, way, hop - 1)
        return remote(spot, spot, share_send.at[at], share_recv.at[at], sibling)

    def advance(kind, hop):
        for way in (0, 1):
            landed(kind, way, hop).wait_recv()
            if hop < hops:
                sent(kind, way, hop + 1).start()
            shared(kind, way, hop, core).start()

    for kind in (0, 1):
        for way in (0, 1):
            sent(kind, way, 1).start()
    advance(0, 1)
    for hop in range(2, hops + 1):
        advance(0, hop)
        advance(1, hop - 1)
    steps = [(way, hop) for hop in range(1, hops + 1) for way in (0, 1)]
    for way, hop in steps:
        shared(0, way, hop, 1 - core).wait_recv()

    lane = lax.broadcasted_iota(jnp.int32, (BLK, PAIR), 1)
    blocks = [slice(start, start + BLK) for start in range(0, rows, BLK)]
    against = (((1,), (1,)), ((), ()))
    for block in blocks:
        product = lax.dot_general(
            features[block, :width], weights[...], against, preferred_element_type=jnp.float32
        )
        own[block, :PAIR] = product[:, :PAIR].astype(jnp.bfloat16)
        own[block, PAIR:] = product[:, PAIR:].astype(jnp.bfloat16)
    gather = ring_gather(own.at[:, pl.ds(0, PAIR)], kv_ref, *ring)
    take(gather, 8)
    advance(1, hops)
    for way, hop in steps:
        shared(1, way, hop, 1 - core).wait_recv()
    for block in blocks:
        product = lax.dot_general(
            features[block, width:], weights[PAIR:], against, preferred_element_type=jnp.float32
        )
        own[block, PAIR:] = jnp.where(lane < HEAD, own[block, PAIR:], product.astype(jnp.bfloat16))
        take(gather, 4)
    finish(gather)
    for kind in (0, 1):
        for way, hop in steps:
            sent(kind, way, hop).wait_send()
            shared(kind, way, hop, core).wait_send()


def project(frames, cotangent, weights):
    cores, peers = lax.axis_size("mp"), lax.axis_size("seq")
    rows = frames.shape[0]
    dma = pltpu.SemaphoreType.DMA
    sems = dma((2, 2, cores // 4))
    return pl.pallas_call(
        project_kernel,
        out_shape=(
            jax.ShapeDtypeStruct((rows, cores * PAIR), jnp.bfloat16),
            jax.ShapeDtypeStruct((rows, 2 * PAIR), jnp.bfloat16),
            jax.ShapeDtypeStruct((peers, rows, PAIR), jnp.bfloat16),
        ),
        in_specs=[VMEM] * 6,
        out_specs=(VMEM, VMEM, ANY),
        scratch_shapes=[
            pltpu.VMEM((4 * HEAD, D), jnp.bfloat16),
            pltpu.VMEM((PAIR, rows), jnp.bfloat16),
            pltpu.VMEM((PAIR, rows), jnp.bfloat16),
            dma,
            dma,
            sems,
            sems,
            sems,
            sems,
        ]
        + ring_sems(),
        compiler_params=pltpu.CompilerParams(
            collective_id=0, has_side_effects=True, vmem_limit_bytes=LIMIT
        ),
        name="project",
    )(frames.T, cotangent.T, *weights)


def exchange_stats(own_ref, all_ref, x_send, x_recv, y_send, y_recv):
    _, _, at_y, at_x, _, count_y = places()
    along_x, along_y = seq_partners(at_y, at_x, count_y)

    def over_x(step, slot):
        return remote(own_ref, all_ref.at[slot], x_send.at[step], x_recv.at[step], along_x[step])

    def over_y(step, row):
        part = all_ref.at[pl.ds(row * RING_X, RING_X)]
        return remote(part, part, y_send.at[step], y_recv.at[step], along_y[step])

    for step in range(len(along_x)):
        over_x(step, at_y * RING_X + at_x).start()
    all_ref[at_y * RING_X + at_x] = own_ref[...]
    yield
    for step in range(len(along_x)):
        over_x(step, at_y * RING_X + wrap(at_x - step - 1, RING_X)).wait_recv()
    for step in range(len(along_y)):
        over_y(step, at_y).start()
    yield
    for step in range(len(along_y)):
        over_y(step, wrap(at_y - step - 1, count_y)).wait_recv()
    for step in range(len(along_x)):
        over_x(step, at_y * RING_X + at_x).wait_send()
    for step in range(len(along_y)):
        over_y(step, at_y).wait_send()


def share_kernel(
    own,
    stats,
    query_side,
    key_w,
    value_w,
    query_w,
    out_w,
    qg_ref,
    all_stats,
    attended,
    lhs,
    weights,
    local,
    send,
    recv,
    x_send,
    x_recv,
    y_send,
    y_recv,
    *sum_refs,
):
    chip, core, at_y, at_x, chips, count_y = places()
    along_x, along_y = seq_partners(at_y, at_x, count_y)
    greet(along_x + along_y + mp_partners(chip, core, chips))
    table = exchange_stats(stats, all_stats, x_send, x_recv, y_send, y_recv)
    take(table, 1)
    gather = ring_gather(own.at[:, pl.ds(PAIR, PAIR)], qg_ref, local, send, recv)
    take(gather, 8)
    weights[:HEAD] = query_w[...]
    weights[HEAD:] = out_w[...]
    lane = lax.broadcasted_iota(jnp.int32, lhs.shape, 1)
    lhs[...] = jnp.where(lane < HEAD, jnp.zeros_like(lhs[...]), query_side[...])

    def partial(tile, half):
        columns = pl.ds(pl.multiple_of(tile * PAIR, PAIR), PAIR)
        return jnp.dot(half_rows_of(lhs, half), weights[:, columns], preferred_element_type=jnp.float32)

    total = sum_over_mp(partial, attended, *sum_refs)
    take(total, 4)
    take(table, 1)
    for _ in range(2 * chips):
        take(total, 1)
        take(gather, 3)
    finish(gather)
    finish(total)
    finish(table)


def share(own, stats, query_side, weights):
    peers = lax.axis_size("seq")
    rows = own.shape[0]
    dma = pltpu.SemaphoreType.DMA
    x_sems, y_sems = dma((RING_X - 1,)), dma((peers // RING_X - 1,))
    return pl.pallas_call(
        share_kernel,
        out_shape=(
            jax.ShapeDtypeStruct((peers, rows, PAIR), jnp.bfloat16),
            jax.ShapeDtypeStruct((peers,) + stats.shape, jnp.float32),
            jax.ShapeDtypeStruct((HEAD, rows), jnp.bfloat16),
        ),
        in_specs=[ANY] + [VMEM] * 6,
        out_specs=(ANY, VMEM, VMEM),
        scratch_shapes=[
            pltpu.VMEM((rows, PAIR), jnp.bfloat16),
            pltpu.VMEM((2 * HEAD, D), jnp.bfloat16),
        ]
        + ring_sems()
        + [x_sems, x_sems, y_sems, y_sems]
        + sum_scratch(rows),
        compiler_params=pltpu.CompilerParams(
            collective_id=1, has_side_effects=True, vmem_limit_bytes=LIMIT
        ),
        name="share",
    )(own, stats, query_side, *weights)


def list_pairs(peers, blocks, device, turn_ref, own_ref, far_ref):
    first = device * blocks
    total = blocks * peers
    count = jnp.int32(0)
    for block in range(blocks):
        for offset in range(-BAND, BAND + 1):
            key = first + block + offset
            own_ref[count] = block
            far_ref[count] = jnp.clip(key, 0, total - 1)
            count += ((key >= 0) & (key < total)).astype(jnp.int32)
    slots = turn_ref.shape[1]

    def visit(peer, count):
        for slot in range(slots):
            own = turn_ref[device, slot, peer]
            far = turn_ref[peer, slot, device]
            own_ref[count] = jnp.clip(own - first, 0, blocks - 1)
            far_ref[count] = jnp.clip(far, 0, total - 1)
            count += ((own >= 0) & (jnp.abs(own - far) > BAND)).astype(jnp.int32)
        return count

    count = lax.fori_loop(0, peers, visit, count)
    for pad in range(UNROLL):
        own_ref[count + pad] = 0
        far_ref[count + pad] = first
    return count


def most_pairs(peers, blocks, slots):
    return blocks * (2 * BAND + 1) + slots * peers + UNROLL


def query_kernel(
    peers,
    turn_ref,
    own_ref,
    kv_ref,
    out_ref,
    stats_ref,
    own_list,
    far_list,
    rhs,
    score,
    slope,
    top,
    total,
    mixed,
    query,
):
    blocks = own_ref.shape[0] // BLK
    count = list_pairs(peers, blocks, lax.axis_index("seq"), turn_ref, own_list, far_list)
    rounds = lax.div(count + UNROLL - 1, UNROLL)
    lane = lax.broadcasted_iota(jnp.int32, (BLK, PAIR), 1)
    zero = jnp.zeros((BLK, PAIR), jnp.bfloat16)
    for block in range(blocks):
        pair = own_ref[block * BLK : (block + 1) * BLK, PAIR:]
        rhs[block, :BLK] = jnp.where(lane < HEAD, pair, zero)
        rhs[block, BLK:] = jnp.where(lane < HEAD, zero, pair)
    top[...] = jnp.full_like(top, -jnp.inf)
    total[...] = jnp.zeros_like(total)
    mixed[...] = jnp.zeros_like(mixed)
    query[...] = jnp.zeros_like(query)

    def tiles(step):
        return [(step * UNROLL + u, own_list[step * UNROLL + u], far_list[step * UNROLL + u]) for u in range(UNROLL)]

    def score_step(step, carry):
        now = tiles(step)
        both = [
            lax.dot_general(
                rhs[own], kv_ref[far], (((1,), (1,)), ((), ())), preferred_element_type=jnp.float32
            )
            for _, own, far in now
        ]
        scaled = []
        for (tile, _, _), product in zip(now, both):
            masked = product[:BLK] * EXP2_SCALE + jnp.where(tile < count, 0.0, -jnp.inf)
            score[tile] = masked
            slope[tile] = product[BLK:]
            scaled.append(masked)
        for (_, own, _), masked in zip(now, scaled):
            top[own] = jnp.maximum(top[own], masked)
        return carry

    lax.fori_loop(0, rounds, score_step, 0)
    for block in range(blocks):
        top[block] = jnp.broadcast_to(jnp.max(top[block], axis=1, keepdims=True), (BLK, PAIR))

    def weight_step(step, carry):
        now = tiles(step)
        weights = []
        for tile, own, _ in now:
            weight = jnp.exp2(score[tile] - top[own])
            weights.append(weight)
        sums = [
            jnp.dot(weight.astype(jnp.bfloat16), kv_ref[far], preferred_element_type=jnp.float32)
            for weight, (_, _, far) in zip(weights, now)
        ]
        for (tile, own, _), weight, part in zip(now, weights, sums):
            score[tile] = weight
            total[own] += weight
            mixed[own] += part
        return carry

    lax.fori_loop(0, rounds, weight_step, 0)
    column = jnp.zeros((BLK, PAIR), jnp.float32)
    for block in range(blocks):
        inverse = 1.0 / jnp.sum(total[block], axis=1, keepdims=True)
        output = mixed[block] * inverse
        mixed[block] = output
        pair = own_ref[block * BLK : (block + 1) * BLK, PAIR:].astype(jnp.float32)
        drift = jnp.sum(jnp.where(lane < HEAD, 0.0, pair * output), axis=1, keepdims=True)
        column = jnp.where(lane == block, top[block], column)
        column = jnp.where(lane == blocks + block, inverse, column)
        column = jnp.where(lane == 2 * blocks + block, drift, column)
        total[block] = jnp.broadcast_to(inverse, (BLK, PAIR))
        top[block] = jnp.broadcast_to(drift, (BLK, PAIR))
    stats_ref[...] = jnp.transpose(column)[: stats_ref.shape[0]]

    def slope_step(step, carry):
        now = tiles(step)
        slopes = []
        for tile, own, _ in now:
            prob = score[tile] * total[own]
            slopes.append((prob * (slope[tile] - top[own])).astype(jnp.bfloat16))
        parts = [
            jnp.dot(value, kv_ref[far], preferred_element_type=jnp.float32)
            for value, (_, _, far) in zip(slopes, now)
        ]
        for (_, own, _), part in zip(now, parts):
            query[own] += part
        return carry

    lax.fori_loop(0, rounds, slope_step, 0)
    for block in range(blocks):
        out_ref[block * BLK : (block + 1) * BLK] = jnp.where(
            lane < HEAD, query[block] * SCALE, mixed[block]
        ).astype(jnp.bfloat16)


def attend_queries(turns, projected, kv):
    peers = lax.axis_size("seq")
    rows = projected.shape[0]
    blocks = rows // BLK
    most = most_pairs(peers, blocks, turns.shape[1])
    square = pltpu.VMEM((blocks, BLK, PAIR), jnp.float32)
    flops = most * 4 * 2 * 2 * BLK * BLK * PAIR // 2
    return pl.pallas_call(
        functools.partial(query_kernel, peers),
        out_shape=(
            jax.ShapeDtypeStruct((rows, PAIR), jnp.bfloat16),
            jax.ShapeDtypeStruct((4 * blocks, BLK), jnp.float32),
        ),
        in_specs=[SMEM, VMEM, VMEM],
        out_specs=(VMEM, VMEM),
        scratch_shapes=[
            pltpu.SMEM((most,), jnp.int32),
            pltpu.SMEM((most,), jnp.int32),
            pltpu.VMEM((blocks, 2 * BLK, PAIR), jnp.bfloat16),
            pltpu.VMEM((most, BLK, BLK), jnp.float32),
            pltpu.VMEM((most, BLK, BLK), jnp.float32),
            square,
            square,
            square,
            square,
        ],
        compiler_params=pltpu.CompilerParams(vmem_limit_bytes=LIMIT),
        cost_estimate=pl.CostEstimate(flops=flops, bytes_accessed=kv.size * 2, transcendentals=most * BLK * BLK),
        name="attend_queries",
    )(turns, projected, kv.reshape(-1, BLK, PAIR))


def key_kernel(peers, turn_ref, own_ref, qg_ref, stats_ref, out_ref, own_list, far_list, lhs, grads):
    blocks = own_ref.shape[0] // BLK
    count = list_pairs(peers, blocks, lax.axis_index("seq"), turn_ref, own_list, far_list)
    rounds = lax.div(count + UNROLL - 1, UNROLL)
    lane = lax.broadcasted_iota(jnp.int32, (BLK, PAIR), 1)
    zero = jnp.zeros((BLK, PAIR), jnp.bfloat16)
    for block in range(blocks):
        pair = own_ref[block * BLK : (block + 1) * BLK, :PAIR]
        lhs[block, :BLK] = jnp.where(lane < HEAD, pair, zero)
        lhs[block, BLK:] = jnp.where(lane < HEAD, zero, pair)
    grads[...] = jnp.zeros_like(grads)

    def step_of(step, carry):
        now = []
        for u in range(UNROLL):
            tile = step * UNROLL + u
            now.append((tile, own_list[tile], far_list[tile]))
        both = [
            lax.dot_general(
                lhs[own], qg_ref[far], (((1,), (1,)), ((), ())), preferred_element_type=jnp.float32
            )
            for _, own, far in now
        ]
        factors = []
        for (tile, _, far), product in zip(now, both):
            peer, block = lax.div(far, blocks), lax.rem(far, blocks)
            top, inverse, drift = (
                stats_ref[peer, pl.ds(kind * blocks + block, 1), :] for kind in range(3)
            )
            masked = product[:BLK] * EXP2_SCALE + jnp.where(tile < count, 0.0, -jnp.inf)
            prob = jnp.exp2(masked - top) * inverse
            factors.append(
                jnp.concatenate([prob * (product[BLK:] - drift), prob], axis=0).astype(jnp.bfloat16)
            )
        parts = [
            jnp.dot(factor, qg_ref[far], preferred_element_type=jnp.float32)
            for factor, (_, _, far) in zip(factors, now)
        ]
        for (_, own, _), part in zip(now, parts):
            grads[own] += part
        return carry

    lax.fori_loop(0, rounds, step_of, 0)
    for block in range(blocks):
        out_ref[block * BLK : (block + 1) * BLK] = jnp.where(
            lane < HEAD, grads[block, :BLK] * SCALE, grads[block, BLK:]
        ).astype(jnp.bfloat16)


def attend_keys(turns, projected, qg, stats):
    peers = lax.axis_size("seq")
    rows = projected.shape[0]
    blocks = rows // BLK
    most = most_pairs(peers, blocks, turns.shape[1])
    flops = most * 4 * 2 * 2 * BLK * BLK * PAIR // 2
    return pl.pallas_call(
        functools.partial(key_kernel, peers),
        out_shape=jax.ShapeDtypeStruct((rows, PAIR), jnp.bfloat16),
        in_specs=[SMEM, VMEM, VMEM, VMEM],
        out_specs=VMEM,
        scratch_shapes=[
            pltpu.SMEM((most,), jnp.int32),
            pltpu.SMEM((most,), jnp.int32),
            pltpu.VMEM((blocks, 2 * BLK, PAIR), jnp.bfloat16),
            pltpu.VMEM((blocks, 2 * BLK, PAIR), jnp.float32),
        ],
        compiler_params=pltpu.CompilerParams(vmem_limit_bytes=LIMIT),
        cost_estimate=pl.CostEstimate(flops=flops, bytes_accessed=qg.size * 2, transcendentals=most * BLK * BLK),
        name="attend_keys",
    )(turns, projected, qg.reshape(-1, BLK, PAIR), stats)


def sum_over_seq(grads, sums_ref, from_x, x_sum, from_y, piece, totals, sems):
    _, _, at_y, at_x, _, count_y = places()
    along_x, along_y = seq_partners(at_y, at_x, count_y)
    width = totals.shape[1]
    xs, ys = range(len(along_x)), range(len(along_y))

    def weight(index):
        column = pl.multiple_of(jnp.where(index == RING_X - 1, width, 0), PAIR)
        return grads.at[pl.ds(pl.multiple_of(index * HEAD, HEAD), HEAD), pl.ds(column, width)]

    def columns(index):
        return pl.ds(pl.multiple_of(index * PAIR, PAIR), PAIR)

    def rows(index):
        return pl.ds(pl.multiple_of(index * HEAD, HEAD), HEAD)

    def in_x(step):
        source = weight(lax.rem(at_x + step + 1, RING_X))
        return remote(source, from_x.at[step], sems[0].at[step], sems[1].at[step], along_x[step])

    def in_y(step):
        source = x_sum.at[:, columns(lax.rem(at_y + step + 1, count_y))]
        return remote(source, from_y.at[step], sems[2].at[step], sems[3].at[step], along_y[step])

    def out_y(step, owner):
        target = totals.at[rows(at_x), columns(owner)]
        return remote(piece, target, sems[4].at[step], sems[5].at[step], along_y[step])

    def out_x(step, owner):
        part = totals.at[rows(owner)]
        return remote(part, part, sems[6].at[step], sems[7].at[step], along_x[step])

    for step in xs:
        in_x(step).start()
    yield
    total = weight(at_x)[...].astype(jnp.float32)
    for step in xs:
        in_x(step).wait_recv()
        total += from_x[step].astype(jnp.float32)
    x_sum[...] = total.astype(jnp.bfloat16)
    for step in ys:
        in_y(step).start()
    yield
    total = x_sum[:, columns(at_y)].astype(jnp.float32)
    for step in ys:
        in_y(step).wait_recv()
        total += from_y[step].astype(jnp.float32)
    piece[...] = total.astype(jnp.bfloat16)
    for step in ys:
        out_y(step, at_y).start()
    totals[rows(at_x), columns(at_y)] = piece[...]
    yield
    for step in ys:
        out_y(step, wrap(at_y - step - 1, count_y)).wait_recv()
    for step in xs:
        out_x(step, at_x).start()
    yield
    for step in xs:
        out_x(step, wrap(at_x - step - 1, RING_X)).wait_recv()
    sums_ref[...] = totals[...].astype(jnp.float32)
    for step in xs:
        in_x(step).wait_send()
        out_x(step, at_x).wait_send()
    for step in ys:
        in_y(step).wait_send()
        out_y(step, at_y).wait_send()


def finish_kernel(
    key_side,
    query_side,
    grads,
    key_w,
    value_w,
    query_w,
    out_w,
    grad_frames,
    sums_ref,
    lhs,
    weights,
    from_x,
    x_sum,
    from_y,
    piece,
    totals,
    *refs,
):
    chip, core, at_y, at_x, chips, count_y = places()
    along_x, along_y = seq_partners(at_y, at_x, count_y)
    greet(along_x + along_y + mp_partners(chip, core, chips))
    over_seq = sum_over_seq(grads, sums_ref, from_x, x_sum, from_y, piece, totals, refs[:8])
    take(over_seq, 1)
    fill_weights((key_w, value_w, query_w, out_w), weights)
    lane = lax.broadcasted_iota(jnp.int32, query_side.shape, 1)
    lhs[:, :PAIR] = key_side[...]
    lhs[:, PAIR:] = jnp.where(lane < HEAD, query_side[...], jnp.zeros_like(query_side[...]))

    def partial(tile, half):
        columns = pl.ds(pl.multiple_of(tile * PAIR, PAIR), PAIR)
        return jnp.dot(half_rows_of(lhs, half), weights[:, columns], preferred_element_type=jnp.float32)

    over_mp = sum_over_mp(partial, grad_frames, *refs[8:])
    take(over_mp, 2 * chips)
    take(over_seq, 2)
    take(over_mp, 1)
    finish(over_seq)
    finish(over_mp)


def finish_sums(key_side, query_side, grads, weights):
    peers = lax.axis_size("seq")
    rows = key_side.shape[0]
    height, width = 4 * HEAD, D
    dma = pltpu.SemaphoreType.DMA
    x_sems, y_sems = dma((RING_X - 1,)), dma((peers // RING_X - 1,))
    return pl.pallas_call(
        finish_kernel,
        out_shape=(
            jax.ShapeDtypeStruct((HEAD, rows), jnp.bfloat16),
            jax.ShapeDtypeStruct((height, width), jnp.float32),
        ),
        in_specs=[VMEM] * 7,
        out_specs=(VMEM, VMEM),
        scratch_shapes=[
            pltpu.VMEM((rows, 2 * PAIR), jnp.bfloat16),
            pltpu.VMEM((height, width), jnp.bfloat16),
            pltpu.VMEM((RING_X - 1, HEAD, width), jnp.bfloat16),
            pltpu.VMEM((HEAD, width), jnp.bfloat16),
            pltpu.VMEM((peers // RING_X - 1, HEAD, PAIR), jnp.bfloat16),
            pltpu.VMEM((HEAD, PAIR), jnp.bfloat16),
            pltpu.VMEM((height, width), jnp.bfloat16),
            x_sems,
            x_sems,
            y_sems,
            y_sems,
            y_sems,
            y_sems,
            x_sems,
            x_sems,
        ]
        + sum_scratch(rows),
        compiler_params=pltpu.CompilerParams(
            collective_id=2, has_side_effects=True, vmem_limit_bytes=LIMIT
        ),
        name="finish_sums",
    )(key_side, query_side, grads, *weights)


def on_device(frames, cotangent, query_weight, key_weight, value_weight, out_weight, turn_blocks):
    turns = jnp.transpose(turn_blocks, (0, 2, 1))
    weights = (key_weight, value_weight, query_weight, out_weight)
    features, projected, kv = project(frames, cotangent, weights)
    query_side, stats = attend_queries(turns, projected, kv)
    qg, all_stats, attended = share(projected, stats, query_side, weights)
    key_side = attend_keys(turns, projected, qg, all_stats)
    joint = jnp.concatenate([key_side, query_side], axis=1)
    products = lax.dot_general(
        joint, features, (((0,), (0,)), ((), ())), preferred_element_type=jnp.float32
    )
    grad_frames, sums = finish_sums(key_side, query_side, products.astype(jnp.bfloat16), weights)
    grad_key, grad_value, grad_query, grad_out = (
        sums[index * HEAD : (index + 1) * HEAD] for index in range(4)
    )
    return attended.T, grad_frames.T, grad_query, grad_key, grad_value, grad_out


def solution(mesh):
    return jax.shard_map(
        on_device,
        mesh=mesh,
        in_specs=(
            P("seq", "mp"),
            P("seq", "mp"),
            P("mp", None),
            P("mp", None),
            P("mp", None),
            P("mp", None),
            P(),
        ),
        out_specs=(
            P("seq", "mp"),
            P("seq", "mp"),
            P("mp", None),
            P("mp", None),
            P("mp", None),
            P("mp", None),
        ),
        check_vma=False,
    )
```

```python
import functools
import math

import jax
import jax.numpy as jnp
from jax import lax
from jax.experimental import pallas as pl
from jax.experimental.pallas import tpu as pltpu
from jax.sharding import PartitionSpec as P

D = 1024
HEADS = 16
BLK = 128
BAND = 2
RING_X = 4
HEAD = D // HEADS
PAIR = 2 * HEAD
UNROLL = 4
SCALE = 1.0 / math.sqrt(HEAD)
EXP2_SCALE = SCALE * math.log2(math.e)
MESH = pl.DeviceIdType.MESH
VMEM = pl.BlockSpec(memory_space=pltpu.VMEM)
SMEM = pl.BlockSpec(memory_space=pltpu.SMEM)
ANY = pl.BlockSpec(memory_space=pl.ANY)
LIMIT = 60 * 1024 * 1024


def wrap(index, count):
    return lax.rem(index + count, count)


def greet(devices):
    barrier = pltpu.get_barrier_semaphore()
    for device in devices:
        pl.semaphore_signal(barrier, inc=1, device_id=device, device_id_type=MESH)
    pl.semaphore_wait(barrier, len(devices))


def remote(source, target, send, recv, device):
    return pltpu.make_async_remote_copy(
        source, target, send, recv, device_id=device, device_id_type=MESH
    )


def take(process, count):
    for _ in range(count):
        next(process, None)


def finish(process):
    for _ in process:
        pass


def stack_rows(refs, whole, sems):
    copies = []
    for index, ref in enumerate(refs):
        target = whole.at[pl.ds(index * HEAD, HEAD)]
        copies.append(pltpu.make_async_copy(ref, target, sems.at[index]))
    return copies


def places():
    me_mp, me = lax.axis_index("mp"), lax.axis_index("seq")
    chips, count_y = lax.axis_size("mp") // 2, lax.axis_size("seq") // RING_X
    return lax.div(me_mp, 2), lax.rem(me_mp, 2), lax.div(me, RING_X), lax.rem(me, RING_X), chips, count_y


def neighbours(at_y, at_x, count_y):
    return {
        ("x", 1): {"seq": at_y * RING_X + wrap(at_x + 1, RING_X)},
        ("x", -1): {"seq": at_y * RING_X + wrap(at_x - 1, RING_X)},
        ("y", 1): {"seq": wrap(at_y + 1, count_y) * RING_X + at_x},
        ("y", -1): {"seq": wrap(at_y - 1, count_y) * RING_X + at_x},
    }


@functools.cache
def ring_messages(count_y, count_x):
    messages = []
    for phase, count, split in (("x", count_x, False), ("y", count_y, False), ("row", count_y, True), ("col", count_x, True)):
        for hop in range(1, count // 2 + 1):
            for way in (0, 1):
                if hop == count // 2:
                    messages.append((phase, way, hop, way))
                elif split:
                    messages += [(phase, way, hop, 0), (phase, way, hop, 1)]
                else:
                    messages.append((phase, way, hop, None))
    return tuple(messages)


def ring_gather(own, store, local, send, recv):
    _, _, at_y, at_x, _, count_y = places()
    near = neighbours(at_y, at_x, count_y)
    half_rows = store.shape[2] // 2
    quarter = half_rows // 2
    messages = ring_messages(count_y, RING_X)

    def rows(phase, part):
        base = 0 if phase in ("x", "row") else half_rows
        return pl.ds(base, half_rows) if part is None else pl.ds(base + part * quarter, quarter)

    def region(phase, offset, part):
        if phase in ("x", "col"):
            column = wrap(at_x + offset, RING_X)
            return store.at[at_y if phase == "x" else slice(None), column, rows(phase, part)]
        row = wrap(at_y + offset, count_y)
        return store.at[row, at_x if phase == "y" else slice(None), rows(phase, part)]

    def copy_of(message, arriving):
        phase, way, hop, part = message
        sign = -1 if way == 0 else 1
        target = region(phase, sign * (hop if arriving else hop - 1), part)
        source = target
        if hop == 1 and phase in ("x", "y") and not arriving:
            source = own.at[rows(phase, part)]
        index = messages.index(message)
        axis = "x" if phase in ("x", "col") else "y"
        return remote(source, target, send.at[index], recv.at[index], near[axis, 1 if way == 0 else -1])

    def of(phase, hop):
        found = [message for message in messages if message[0] == phase and message[2] == hop]
        return sorted(found, key=lambda message: (message[3] or 0, message[1]))

    waited = []

    def await_all(arrived):
        for message in arrived:
            if message not in waited:
                waited.append(message)
                copy_of(message, True).wait_recv()

    def start_hop(phase, hop):
        for message in of(phase, hop):
            _, way, _, part = message
            if hop > 1:
                await_all([m for m in of(phase, hop - 1) if m[1] == way and m[3] in (None, part)])
            copy_of(message, False).start()
            yield

    keep = pltpu.make_async_copy(own, store.at[at_y, at_x], local)
    yield from start_hop("x", 1)
    yield from start_hop("y", 1)
    keep.start()
    yield from start_hop("x", 2)
    yield from start_hop("y", 2)
    keep.wait()
    for hop in range(1, RING_X // 2 + 1):
        await_all(of("x", hop))
    yield from start_hop("row", 1)
    for hop in range(3, count_y // 2 + 1):
        yield from start_hop("y", hop)
    yield from start_hop("row", 2)
    for hop in range(1, count_y // 2 + 1):
        await_all(of("y", hop))
    yield from start_hop("col", 1)
    yield from start_hop("row", 3)
    yield from start_hop("col", 2)
    for hop in range(4, count_y // 2 + 1):
        yield from start_hop("row", hop)
    await_all(messages)
    yield
    for message in messages:
        copy_of(message, False).wait_send()


def ring_sems():
    steps = len(ring_messages(lax.axis_size("seq") // RING_X, RING_X))
    return [
        pltpu.SemaphoreType.DMA,
        pltpu.SemaphoreType.DMA((steps,)),
        pltpu.SemaphoreType.DMA((steps,)),
    ]


def sum_over_mp(partial, out_ref, mine, gift, theirs, chip_sum, tiles, done, pair_send, pair_recv, z_send, z_recv, swap_send, swap_recv):
    chip, core, _, _, chips, _ = places()
    sibling = {"mp": 2 * chip + 1 - core}
    half = mine.shape[1]

    def give(step):
        return remote(gift.at[step], theirs.at[step], pair_send.at[step], pair_recv.at[step], sibling)

    def post(step):
        target = {"mp": 2 * lax.rem(chip + step, chips) + core}
        return remote(chip_sum.at[step], tiles.at[step], z_send.at[step - 1], z_recv.at[step - 1], target)

    order = sorted(range(1, chips), key=lambda step: -min(step, chips - step)) + [0]
    for step in order:
        tile = lax.rem(chip + step, chips)
        gift[step] = partial(tile, 1 - core).astype(jnp.bfloat16)
        give(step).start()
        mine[step] = partial(tile, core)
        yield
    for step in order:
        give(step).wait_recv()
        mine[step] += theirs[step].astype(jnp.float32)
        if step:
            chip_sum[step] = mine[step].astype(jnp.bfloat16)
            post(step).start()
        yield
    total = mine[0]
    for step in reversed(order[:-1]):
        post(step).wait_recv()
        total += tiles[step].astype(jnp.float32)
    done[...] = jnp.transpose(total).astype(jnp.bfloat16)
    columns = pl.ds(pl.multiple_of(core * half, half), half)
    other_columns = pl.ds(pl.multiple_of((1 - core) * half, half), half)
    own_rows = pl.ds(pl.multiple_of(core * HEAD, HEAD), HEAD)
    swap = remote(
        done.at[pl.ds(pl.multiple_of((1 - core) * HEAD, HEAD), HEAD)],
        out_ref.at[:, columns],
        swap_send,
        swap_recv,
        sibling,
    )
    swap.start()
    out_ref[:, columns] = done[own_rows]
    yield
    remote(done.at[own_rows], out_ref.at[:, other_columns], swap_send, swap_recv, sibling).wait_recv()
    swap.wait_send()
    for step in order:
        give(step).wait_send()
        if step:
            post(step).wait_send()


def sum_scratch(rows):
    chips = lax.axis_size("mp") // 2
    half = rows // 2
    dma = pltpu.SemaphoreType.DMA
    some = pltpu.VMEM((chips, half, PAIR), jnp.bfloat16)
    return [
        pltpu.VMEM((chips, half, PAIR), jnp.float32),
        some,
        some,
        some,
        some,
        pltpu.VMEM((PAIR, half), jnp.bfloat16),
        dma((chips,)),
        dma((chips,)),
        dma((chips - 1,)),
        dma((chips - 1,)),
        dma,
        dma,
    ]


def mp_partners(chip, core, chips):
    return [{"mp": 2 * chip + 1 - core}] + [
        {"mp": 2 * lax.rem(chip + step, chips) + core} for step in range(1, chips)
    ]


def seq_partners(at_y, at_x, count_y):
    along_x = [{"seq": at_y * RING_X + lax.rem(at_x + step, RING_X)} for step in range(1, RING_X)]
    along_y = [{"seq": lax.rem(at_y + step, count_y) * RING_X + at_x} for step in range(1, count_y)]
    return along_x, along_y


def half_rows_of(ref, half):
    rows = ref.shape[0] // 2
    return ref[pl.ds(pl.multiple_of(half * rows, rows), rows)]


def project_kernel(
    frames_ref,
    grad_ref,
    key_w,
    value_w,
    query_w,
    out_w,
    features,
    own,
    kv_ref,
    weights,
    mine,
    other,
    loaded,
    filled,
    pair_send,
    pair_recv,
    z_send,
    z_recv,
    share_send,
    share_recv,
    *ring,
):
    chip, core, at_y, at_x, chips, count_y = places()
    hops = chips // 2
    rows = features.shape[0]
    half, width = rows // 2, chips * PAIR
    sibling = {"mp": 2 * chip + 1 - core}
    right = {"mp": 2 * wrap(chip + 1, chips) + core}
    left = {"mp": 2 * wrap(chip - 1, chips) + core}
    inputs = stack_rows((frames_ref, grad_ref), mine, loaded)
    fill = stack_rows((key_w, value_w, query_w, out_w), weights, filled)
    for copy in inputs + fill:
        copy.start()
    greet([sibling, right, left] + list(neighbours(at_y, at_x, count_y).values()))
    for copy in inputs:
        copy.wait()

    def side(whose):
        return pl.ds(pl.multiple_of(whose * half, half), half)

    swap = remote(mine.at[:, side(1 - core)], other, pair_send, pair_recv, sibling)
    swap.start()
    swap.wait_recv()
    here, there = mine[:, side(core)].astype(jnp.float32), other[...].astype(jnp.float32)
    even = jnp.where(core == 0, here, there)
    odd = jnp.where(core == 0, there, here)
    for kind in (0, 1):
        part = slice(kind * HEAD, (kind + 1) * HEAD)
        tile = jnp.transpose(jnp.concatenate([even[part], odd[part]], axis=0))
        column = pl.multiple_of(kind * width + chip * PAIR, PAIR)
        features[side(core), pl.ds(column, PAIR)] = tile.astype(jnp.bfloat16)

    def place(kind, tile, way, hop):
        start = pl.multiple_of(kind * width + wrap(tile, chips) * PAIR, PAIR)
        count = half if hop < hops else half // 2
        first = core * half + (0 if hop < hops else way * count)
        return features.at[pl.ds(pl.multiple_of(first, count), count), pl.ds(start, PAIR)]

    def along_z(kind, way, hop, moved):
        spot = place(kind, chip + (-moved if way == 0 else moved), way, hop)
        at = (kind, way, hop - 1)
        return remote(spot, spot, z_send.at[at], z_recv.at[at], right if way == 0 else left)

    def sent(kind, way, hop):
        return along_z(kind, way, hop, hop - 1)

    def landed(kind, way, hop):
        return along_z(kind, way, hop, hop)

    def shared(kind, whose):
        spot = features.at[side(whose), pl.ds(kind * width, width)]
        return remote(spot, spot, share_send.at[kind], share_recv.at[kind], sibling)

    def advance(kind, hop):
        for way in (0, 1):
            landed(kind, way, hop).wait_recv()
            if hop < hops:
                sent(kind, way, hop + 1).start()
        if hop == hops:
            shared(kind, core).start()

    for kind in (0, 1):
        for way in (0, 1):
            sent(kind, way, 1).start()
    advance(0, 1)
    for hop in range(2, hops + 1):
        advance(0, hop)
        advance(1, hop - 1)
    for copy in fill:
        copy.wait()
    shared(0, 1 - core).wait_recv()

    lane = lax.broadcasted_iota(jnp.int32, (BLK, PAIR), 1)
    blocks = [slice(start, start + BLK) for start in range(0, rows, BLK)]
    against = (((1,), (1,)), ((), ()))
    for block in blocks:
        product = lax.dot_general(
            features[block, :width], weights[...], against, preferred_element_type=jnp.float32
        )
        own[block, :PAIR] = product[:, :PAIR].astype(jnp.bfloat16)
        own[block, PAIR:] = product[:, PAIR:].astype(jnp.bfloat16)
    gather = ring_gather(own.at[:, pl.ds(0, PAIR)], kv_ref, *ring)
    take(gather, 4)
    advance(1, hops)
    shared(1, 1 - core).wait_recv()
    for block in blocks:
        product = lax.dot_general(
            features[block, width:], weights[PAIR:], against, preferred_element_type=jnp.float32
        )
        own[block, PAIR:] = jnp.where(lane < HEAD, own[block, PAIR:], product.astype(jnp.bfloat16))
        take(gather, 4)
    finish(gather)
    swap.wait_send()
    for kind in (0, 1):
        shared(kind, core).wait_send()
        for hop in range(1, hops + 1):
            for way in (0, 1):
                sent(kind, way, hop).wait_send()


def project(frames, cotangent, weights):
    cores, peers = lax.axis_size("mp"), lax.axis_size("seq")
    rows = frames.shape[0]
    dma = pltpu.SemaphoreType.DMA
    sems = dma((2, 2, cores // 4))
    return pl.pallas_call(
        project_kernel,
        out_shape=(
            jax.ShapeDtypeStruct((rows, cores * PAIR), jnp.bfloat16),
            jax.ShapeDtypeStruct((rows, 2 * PAIR), jnp.bfloat16),
            jax.ShapeDtypeStruct((peers // RING_X, RING_X, rows, PAIR), jnp.bfloat16),
        ),
        in_specs=[ANY] * 6,
        out_specs=(VMEM, VMEM, ANY),
        scratch_shapes=[
            pltpu.VMEM((4 * HEAD, D), jnp.bfloat16),
            pltpu.VMEM((PAIR, rows), jnp.bfloat16),
            pltpu.VMEM((PAIR, rows // 2), jnp.bfloat16),
            dma((2,)),
            dma((4,)),
            dma,
            dma,
            sems,
            sems,
            dma((2,)),
            dma((2,)),
        ]
        + ring_sems(),
        compiler_params=pltpu.CompilerParams(
            collective_id=0, has_side_effects=True, vmem_limit_bytes=LIMIT
        ),
        name="project",
    )(frames.T, cotangent.T, *weights)


def exchange_stats(own_ref, all_ref, x_send, x_recv, y_send, y_recv):
    _, _, at_y, at_x, _, count_y = places()
    along_x, along_y = seq_partners(at_y, at_x, count_y)

    def over_x(step, slot):
        return remote(own_ref, all_ref.at[slot], x_send.at[step], x_recv.at[step], along_x[step])

    def over_y(step, row):
        part = all_ref.at[pl.ds(row * RING_X, RING_X)]
        return remote(part, part, y_send.at[step], y_recv.at[step], along_y[step])

    for step in range(len(along_x)):
        over_x(step, at_y * RING_X + at_x).start()
    all_ref[at_y * RING_X + at_x] = own_ref[...]
    yield
    for step in range(len(along_x)):
        over_x(step, at_y * RING_X + wrap(at_x - step - 1, RING_X)).wait_recv()
    for step in range(len(along_y)):
        over_y(step, at_y).start()
    yield
    for step in range(len(along_y)):
        over_y(step, wrap(at_y - step - 1, count_y)).wait_recv()
    for step in range(len(along_x)):
        over_x(step, at_y * RING_X + at_x).wait_send()
    for step in range(len(along_y)):
        over_y(step, at_y).wait_send()


def share_kernel(
    own,
    stats,
    query_side,
    query_w,
    out_w,
    qg_ref,
    all_stats,
    attended,
    lhs,
    weights,
    filled,
    local,
    send,
    recv,
    x_send,
    x_recv,
    y_send,
    y_recv,
    *sum_refs,
):
    chip, core, at_y, at_x, chips, count_y = places()
    along_x, along_y = seq_partners(at_y, at_x, count_y)
    fill = stack_rows((query_w, out_w), weights, filled)
    for copy in fill:
        copy.start()
    greet(along_x + along_y + mp_partners(chip, core, chips))
    table = exchange_stats(stats, all_stats, x_send, x_recv, y_send, y_recv)
    take(table, 1)
    gather = ring_gather(own.at[:, pl.ds(PAIR, PAIR)], qg_ref, local, send, recv)
    take(gather, 4)
    for copy in fill:
        copy.wait()
    lane = lax.broadcasted_iota(jnp.int32, lhs.shape, 1)
    lhs[...] = jnp.where(lane < HEAD, jnp.zeros_like(lhs[...]), query_side[...])

    def partial(tile, half):
        columns = pl.ds(pl.multiple_of(tile * PAIR, PAIR), PAIR)
        return jnp.dot(half_rows_of(lhs, half), weights[:, columns], preferred_element_type=jnp.float32)

    total = sum_over_mp(partial, attended, *sum_refs)
    take(total, 4)
    take(table, 1)
    for _ in range(2 * chips):
        take(total, 1)
        take(gather, 2)
    finish(gather)
    finish(total)
    finish(table)


def share(own, stats, query_side, weights):
    peers = lax.axis_size("seq")
    rows = own.shape[0]
    dma = pltpu.SemaphoreType.DMA
    x_sems, y_sems = dma((RING_X - 1,)), dma((peers // RING_X - 1,))
    return pl.pallas_call(
        share_kernel,
        out_shape=(
            jax.ShapeDtypeStruct((peers // RING_X, RING_X, rows, PAIR), jnp.bfloat16),
            jax.ShapeDtypeStruct((peers,) + stats.shape, jnp.float32),
            jax.ShapeDtypeStruct((HEAD, rows), jnp.bfloat16),
        ),
        in_specs=[ANY, VMEM, VMEM, ANY, ANY],
        out_specs=(ANY, VMEM, VMEM),
        scratch_shapes=[
            pltpu.VMEM((rows, PAIR), jnp.bfloat16),
            pltpu.VMEM((2 * HEAD, D), jnp.bfloat16),
            dma((2,)),
        ]
        + ring_sems()
        + [x_sems, x_sems, y_sems, y_sems]
        + sum_scratch(rows),
        compiler_params=pltpu.CompilerParams(
            collective_id=1, has_side_effects=True, vmem_limit_bytes=LIMIT
        ),
        name="share",
    )(own, stats, query_side, *weights[2:])


def list_pairs(peers, blocks, device, turn_ref, own_ref, far_ref):
    first = device * blocks
    total = blocks * peers
    count = jnp.int32(0)
    for block in range(blocks):
        for offset in range(-BAND, BAND + 1):
            key = first + block + offset
            own_ref[count] = block
            far_ref[count] = jnp.clip(key, 0, total - 1)
            count += ((key >= 0) & (key < total)).astype(jnp.int32)
    slots = turn_ref.shape[1]

    def visit(peer, count):
        for slot in range(slots):
            own = turn_ref[device, slot, peer]
            far = turn_ref[peer, slot, device]
            own_ref[count] = jnp.clip(own - first, 0, blocks - 1)
            far_ref[count] = jnp.clip(far, 0, total - 1)
            count += ((own >= 0) & (jnp.abs(own - far) > BAND)).astype(jnp.int32)
        return count

    count = lax.fori_loop(0, peers, visit, count)
    for pad in range(UNROLL):
        own_ref[count + pad] = 0
        far_ref[count + pad] = first
    return count


def most_pairs(peers, blocks, slots):
    return blocks * (2 * BAND + 1) + slots * peers + UNROLL


def query_kernel(
    peers,
    turn_ref,
    own_ref,
    kv_ref,
    out_ref,
    stats_ref,
    own_list,
    far_list,
    rhs,
    score,
    slope,
    top,
    total,
    mixed,
    query,
):
    blocks = own_ref.shape[0] // BLK
    count = list_pairs(peers, blocks, lax.axis_index("seq"), turn_ref, own_list, far_list)
    rounds = lax.div(count + UNROLL - 1, UNROLL)
    lane = lax.broadcasted_iota(jnp.int32, (BLK, PAIR), 1)
    zero = jnp.zeros((BLK, PAIR), jnp.bfloat16)
    for block in range(blocks):
        pair = own_ref[block * BLK : (block + 1) * BLK, PAIR:]
        rhs[block, :BLK] = jnp.where(lane < HEAD, pair, zero)
        rhs[block, BLK:] = jnp.where(lane < HEAD, zero, pair)
    top[...] = jnp.full_like(top, -jnp.inf)
    total[...] = jnp.zeros_like(total)
    mixed[...] = jnp.zeros_like(mixed)
    query[...] = jnp.zeros_like(query)

    def tiles(step):
        return [(step * UNROLL + u, own_list[step * UNROLL + u], far_list[step * UNROLL + u]) for u in range(UNROLL)]

    def score_step(step, carry):
        now = tiles(step)
        both = [
            lax.dot_general(
                rhs[own], kv_ref[far], (((1,), (1,)), ((), ())), preferred_element_type=jnp.float32
            )
            for _, own, far in now
        ]
        scaled = []
        for (tile, _, _), product in zip(now, both):
            masked = product[:BLK] * EXP2_SCALE + jnp.where(tile < count, 0.0, -jnp.inf)
            score[tile] = masked
            slope[tile] = product[BLK:]
            scaled.append(masked)
        for (_, own, _), masked in zip(now, scaled):
            top[own] = jnp.maximum(top[own], masked)
        return carry

    lax.fori_loop(0, rounds, score_step, 0)
    for block in range(blocks):
        top[block] = jnp.broadcast_to(jnp.max(top[block], axis=1, keepdims=True), (BLK, PAIR))

    def weight_step(step, carry):
        now = tiles(step)
        weights = []
        for tile, own, _ in now:
            weight = jnp.exp2(score[tile] - top[own])
            weights.append(weight)
        sums = [
            jnp.dot(weight.astype(jnp.bfloat16), kv_ref[far], preferred_element_type=jnp.float32)
            for weight, (_, _, far) in zip(weights, now)
        ]
        for (tile, own, _), weight, part in zip(now, weights, sums):
            score[tile] = weight
            total[own] += weight
            mixed[own] += part
        return carry

    lax.fori_loop(0, rounds, weight_step, 0)
    column = jnp.zeros((BLK, PAIR), jnp.float32)
    for block in range(blocks):
        inverse = 1.0 / jnp.sum(total[block], axis=1, keepdims=True)
        output = mixed[block] * inverse
        mixed[block] = output
        pair = own_ref[block * BLK : (block + 1) * BLK, PAIR:].astype(jnp.float32)
        drift = jnp.sum(jnp.where(lane < HEAD, 0.0, pair * output), axis=1, keepdims=True)
        column = jnp.where(lane == block, top[block], column)
        column = jnp.where(lane == blocks + block, inverse, column)
        column = jnp.where(lane == 2 * blocks + block, drift, column)
        total[block] = jnp.broadcast_to(inverse, (BLK, PAIR))
        top[block] = jnp.broadcast_to(drift, (BLK, PAIR))
    stats_ref[...] = jnp.transpose(column)[: stats_ref.shape[0]]

    def slope_step(step, carry):
        now = tiles(step)
        slopes = []
        for tile, own, _ in now:
            prob = score[tile] * total[own]
            slopes.append((prob * (slope[tile] - top[own])).astype(jnp.bfloat16))
        parts = [
            jnp.dot(value, kv_ref[far], preferred_element_type=jnp.float32)
            for value, (_, _, far) in zip(slopes, now)
        ]
        for (_, own, _), part in zip(now, parts):
            query[own] += part
        return carry

    lax.fori_loop(0, rounds, slope_step, 0)
    for block in range(blocks):
        out_ref[block * BLK : (block + 1) * BLK] = jnp.where(
            lane < HEAD, query[block] * SCALE, mixed[block]
        ).astype(jnp.bfloat16)


def attend_queries(turns, projected, kv):
    peers = lax.axis_size("seq")
    rows = projected.shape[0]
    blocks = rows // BLK
    most = most_pairs(peers, blocks, turns.shape[1])
    square = pltpu.VMEM((blocks, BLK, PAIR), jnp.float32)
    flops = most * 4 * 2 * 2 * BLK * BLK * PAIR // 2
    return pl.pallas_call(
        functools.partial(query_kernel, peers),
        out_shape=(
            jax.ShapeDtypeStruct((rows, PAIR), jnp.bfloat16),
            jax.ShapeDtypeStruct((4 * blocks, BLK), jnp.float32),
        ),
        in_specs=[SMEM, VMEM, VMEM],
        out_specs=(VMEM, VMEM),
        scratch_shapes=[
            pltpu.SMEM((most,), jnp.int32),
            pltpu.SMEM((most,), jnp.int32),
            pltpu.VMEM((blocks, 2 * BLK, PAIR), jnp.bfloat16),
            pltpu.VMEM((most, BLK, BLK), jnp.float32),
            pltpu.VMEM((most, BLK, BLK), jnp.float32),
            square,
            square,
            square,
            square,
        ],
        compiler_params=pltpu.CompilerParams(vmem_limit_bytes=LIMIT),
        cost_estimate=pl.CostEstimate(flops=flops, bytes_accessed=kv.size * 2, transcendentals=most * BLK * BLK),
        name="attend_queries",
    )(turns, projected, kv.reshape(-1, BLK, PAIR))


def key_kernel(peers, turn_ref, own_ref, qg_ref, stats_ref, out_ref, own_list, far_list, lhs, grads):
    blocks = own_ref.shape[0] // BLK
    count = list_pairs(peers, blocks, lax.axis_index("seq"), turn_ref, own_list, far_list)
    rounds = lax.div(count + UNROLL - 1, UNROLL)
    lane = lax.broadcasted_iota(jnp.int32, (BLK, PAIR), 1)
    zero = jnp.zeros((BLK, PAIR), jnp.bfloat16)
    for block in range(blocks):
        pair = own_ref[block * BLK : (block + 1) * BLK, :PAIR]
        lhs[block, :BLK] = jnp.where(lane < HEAD, pair, zero)
        lhs[block, BLK:] = jnp.where(lane < HEAD, zero, pair)
    grads[...] = jnp.zeros_like(grads)

    def step_of(step, carry):
        now = []
        for u in range(UNROLL):
            tile = step * UNROLL + u
            now.append((tile, own_list[tile], far_list[tile]))
        both = [
            lax.dot_general(
                lhs[own], qg_ref[far], (((1,), (1,)), ((), ())), preferred_element_type=jnp.float32
            )
            for _, own, far in now
        ]
        factors = []
        for (tile, _, far), product in zip(now, both):
            peer, block = lax.div(far, blocks), lax.rem(far, blocks)
            top, inverse, drift = (
                stats_ref[peer, pl.ds(kind * blocks + block, 1), :] for kind in range(3)
            )
            masked = product[:BLK] * EXP2_SCALE + jnp.where(tile < count, 0.0, -jnp.inf)
            prob = jnp.exp2(masked - top) * inverse
            factors.append(
                jnp.concatenate([prob * (product[BLK:] - drift), prob], axis=0).astype(jnp.bfloat16)
            )
        parts = [
            jnp.dot(factor, qg_ref[far], preferred_element_type=jnp.float32)
            for factor, (_, _, far) in zip(factors, now)
        ]
        for (_, own, _), part in zip(now, parts):
            grads[own] += part
        return carry

    lax.fori_loop(0, rounds, step_of, 0)
    for block in range(blocks):
        out_ref[block * BLK : (block + 1) * BLK] = jnp.where(
            lane < HEAD, grads[block, :BLK] * SCALE, grads[block, BLK:]
        ).astype(jnp.bfloat16)


def attend_keys(turns, projected, qg, stats):
    peers = lax.axis_size("seq")
    rows = projected.shape[0]
    blocks = rows // BLK
    most = most_pairs(peers, blocks, turns.shape[1])
    flops = most * 4 * 2 * 2 * BLK * BLK * PAIR // 2
    return pl.pallas_call(
        functools.partial(key_kernel, peers),
        out_shape=jax.ShapeDtypeStruct((rows, PAIR), jnp.bfloat16),
        in_specs=[SMEM, VMEM, VMEM, VMEM],
        out_specs=VMEM,
        scratch_shapes=[
            pltpu.SMEM((most,), jnp.int32),
            pltpu.SMEM((most,), jnp.int32),
            pltpu.VMEM((blocks, 2 * BLK, PAIR), jnp.bfloat16),
            pltpu.VMEM((blocks, 2 * BLK, PAIR), jnp.float32),
        ],
        compiler_params=pltpu.CompilerParams(vmem_limit_bytes=LIMIT),
        cost_estimate=pl.CostEstimate(flops=flops, bytes_accessed=qg.size * 2, transcendentals=most * BLK * BLK),
        name="attend_keys",
    )(turns, projected, qg.reshape(-1, BLK, PAIR), stats)


def sum_over_seq(grads, sums_ref, from_x, x_sum, from_y, piece, totals, sems):
    _, _, at_y, at_x, _, count_y = places()
    along_x, along_y = seq_partners(at_y, at_x, count_y)
    width = totals.shape[1]
    xs, ys = range(len(along_x)), range(len(along_y))

    def weight(index):
        column = pl.multiple_of(jnp.where(index == RING_X - 1, width, 0), PAIR)
        return grads.at[pl.ds(pl.multiple_of(index * HEAD, HEAD), HEAD), pl.ds(column, width)]

    def columns(index):
        return pl.ds(pl.multiple_of(index * PAIR, PAIR), PAIR)

    def rows(index):
        return pl.ds(pl.multiple_of(index * HEAD, HEAD), HEAD)

    def in_x(step):
        source = weight(lax.rem(at_x + step + 1, RING_X))
        return remote(source, from_x.at[step], sems[0].at[step], sems[1].at[step], along_x[step])

    def in_y(step):
        source = x_sum.at[:, columns(lax.rem(at_y + step + 1, count_y))]
        return remote(source, from_y.at[step], sems[2].at[step], sems[3].at[step], along_y[step])

    def out_y(step, owner):
        target = totals.at[rows(at_x), columns(owner)]
        return remote(piece, target, sems[4].at[step], sems[5].at[step], along_y[step])

    def out_x(step, owner):
        part = totals.at[rows(owner)]
        return remote(part, part, sems[6].at[step], sems[7].at[step], along_x[step])

    for step in xs:
        in_x(step).start()
    yield
    total = weight(at_x)[...].astype(jnp.float32)
    for step in xs:
        in_x(step).wait_recv()
        total += from_x[step].astype(jnp.float32)
    x_sum[...] = total.astype(jnp.bfloat16)
    for step in ys:
        in_y(step).start()
    yield
    total = x_sum[:, columns(at_y)].astype(jnp.float32)
    for step in ys:
        in_y(step).wait_recv()
        total += from_y[step].astype(jnp.float32)
    piece[...] = total.astype(jnp.bfloat16)
    for step in ys:
        out_y(step, at_y).start()
    totals[rows(at_x), columns(at_y)] = piece[...]
    yield
    for step in ys:
        out_y(step, wrap(at_y - step - 1, count_y)).wait_recv()
    for step in xs:
        out_x(step, at_x).start()
    yield
    for step in xs:
        out_x(step, wrap(at_x - step - 1, RING_X)).wait_recv()
    sums_ref[...] = totals[...].astype(jnp.float32)
    for step in xs:
        in_x(step).wait_send()
        out_x(step, at_x).wait_send()
    for step in ys:
        in_y(step).wait_send()
        out_y(step, at_y).wait_send()


def finish_kernel(
    key_side,
    query_side,
    grads,
    key_w,
    value_w,
    query_w,
    out_w,
    grad_frames,
    sums_ref,
    lhs,
    weights,
    filled,
    from_x,
    x_sum,
    from_y,
    piece,
    totals,
    *refs,
):
    chip, core, at_y, at_x, chips, count_y = places()
    along_x, along_y = seq_partners(at_y, at_x, count_y)
    fill = stack_rows((key_w, value_w, query_w, out_w), weights, filled)
    for copy in fill:
        copy.start()
    greet(along_x + along_y + mp_partners(chip, core, chips))
    over_seq = sum_over_seq(grads, sums_ref, from_x, x_sum, from_y, piece, totals, refs[:8])
    take(over_seq, 1)
    for copy in fill:
        copy.wait()
    lane = lax.broadcasted_iota(jnp.int32, query_side.shape, 1)
    lhs[:, :PAIR] = key_side[...]
    lhs[:, PAIR:] = jnp.where(lane < HEAD, query_side[...], jnp.zeros_like(query_side[...]))

    def partial(tile, half):
        columns = pl.ds(pl.multiple_of(tile * PAIR, PAIR), PAIR)
        return jnp.dot(half_rows_of(lhs, half), weights[:, columns], preferred_element_type=jnp.float32)

    over_mp = sum_over_mp(partial, grad_frames, *refs[8:])
    take(over_mp, 2 * chips)
    take(over_seq, 2)
    take(over_mp, 1)
    finish(over_seq)
    finish(over_mp)


def finish_sums(key_side, query_side, grads, weights):
    peers = lax.axis_size("seq")
    rows = key_side.shape[0]
    height, width = 4 * HEAD, D
    dma = pltpu.SemaphoreType.DMA
    x_sems, y_sems = dma((RING_X - 1,)), dma((peers // RING_X - 1,))
    return pl.pallas_call(
        finish_kernel,
        out_shape=(
            jax.ShapeDtypeStruct((HEAD, rows), jnp.bfloat16),
            jax.ShapeDtypeStruct((height, width), jnp.float32),
        ),
        in_specs=[VMEM] * 3 + [ANY] * 4,
        out_specs=(VMEM, VMEM),
        scratch_shapes=[
            pltpu.VMEM((rows, 2 * PAIR), jnp.bfloat16),
            pltpu.VMEM((height, width), jnp.bfloat16),
            dma((4,)),
            pltpu.VMEM((RING_X - 1, HEAD, width), jnp.bfloat16),
            pltpu.VMEM((HEAD, width), jnp.bfloat16),
            pltpu.VMEM((peers // RING_X - 1, HEAD, PAIR), jnp.bfloat16),
            pltpu.VMEM((HEAD, PAIR), jnp.bfloat16),
            pltpu.VMEM((height, width), jnp.bfloat16),
            x_sems,
            x_sems,
            y_sems,
            y_sems,
            y_sems,
            y_sems,
            x_sems,
            x_sems,
        ]
        + sum_scratch(rows),
        compiler_params=pltpu.CompilerParams(
            collective_id=2, has_side_effects=True, vmem_limit_bytes=LIMIT
        ),
        name="finish_sums",
    )(key_side, query_side, grads, *weights)


def on_device(frames, cotangent, query_weight, key_weight, value_weight, out_weight, turn_blocks):
    turns = jnp.transpose(turn_blocks, (0, 2, 1))
    weights = (key_weight, value_weight, query_weight, out_weight)
    features, projected, kv = project(frames, cotangent, weights)
    query_side, stats = attend_queries(turns, projected, kv)
    qg, all_stats, attended = share(projected, stats, query_side, weights)
    key_side = attend_keys(turns, projected, qg, all_stats)
    joint = jnp.concatenate([key_side, query_side], axis=1)
    products = lax.dot_general(
        joint, features, (((0,), (0,)), ((), ())), preferred_element_type=jnp.float32
    )
    grad_frames, sums = finish_sums(key_side, query_side, products.astype(jnp.bfloat16), weights)
    grad_key, grad_value, grad_query, grad_out = (
        sums[index * HEAD : (index + 1) * HEAD] for index in range(4)
    )
    return attended.T, grad_frames.T, grad_query, grad_key, grad_value, grad_out


def solution(mesh):
    return jax.shard_map(
        on_device,
        mesh=mesh,
        in_specs=(
            P("seq", "mp"),
            P("seq", "mp"),
            P("mp", None),
            P("mp", None),
            P("mp", None),
            P("mp", None),
            P(),
        ),
        out_specs=(
            P("seq", "mp"),
            P("seq", "mp"),
            P("mp", None),
            P("mp", None),
            P("mp", None),
            P("mp", None),
        ),
        check_vma=False,
    )
```

```python
import functools
import math

import jax
import jax.numpy as jnp
from jax import lax
from jax.experimental import pallas as pl
from jax.experimental.pallas import tpu as pltpu
from jax.sharding import PartitionSpec as P

D = 1024
HEADS = 16
BLK = 128
BAND = 2
RING_X = 4
ROWS = 4
LEAST = -3e38
HEAD = D // HEADS
PAIR = 2 * HEAD
UNROLL = 4
SCALE = 1.0 / math.sqrt(HEAD)
EXP2_SCALE = SCALE * math.log2(math.e)
MESH = pl.DeviceIdType.MESH
VMEM = pl.BlockSpec(memory_space=pltpu.VMEM)
SMEM = pl.BlockSpec(memory_space=pltpu.SMEM)
ANY = pl.BlockSpec(memory_space=pl.ANY)
LIMIT = 48 * 1024 * 1024


def wrap(index, count):
    return lax.rem(index + count, count)


def greet(devices):
    barrier = pltpu.get_barrier_semaphore()
    for device in devices:
        pl.semaphore_signal(barrier, inc=1, device_id=device, device_id_type=MESH)
    pl.semaphore_wait(barrier, len(devices))


def remote(source, target, send, recv, device):
    return pltpu.make_async_remote_copy(
        source, target, send, recv, device_id=device, device_id_type=MESH
    )


def take(process, count):
    for _ in range(count):
        next(process, None)


def finish(process):
    for _ in process:
        pass


def stack_rows(refs, whole, sems):
    copies = []
    for index, ref in enumerate(refs):
        target = whole.at[pl.ds(index * HEAD, HEAD)]
        copies.append(pltpu.make_async_copy(ref, target, sems.at[index]))
    return copies


def places():
    me_mp, me = lax.axis_index("mp"), lax.axis_index("seq")
    chips, count_y = lax.axis_size("mp") // 2, lax.axis_size("seq") // RING_X
    return lax.div(me_mp, 2), lax.rem(me_mp, 2), lax.div(me, RING_X), lax.rem(me, RING_X), chips, count_y


def neighbours(at_y, at_x, count_y):
    return {
        ("x", 1): {"seq": at_y * RING_X + wrap(at_x + 1, RING_X)},
        ("x", -1): {"seq": at_y * RING_X + wrap(at_x - 1, RING_X)},
        ("y", 1): {"seq": wrap(at_y + 1, count_y) * RING_X + at_x},
        ("y", -1): {"seq": wrap(at_y - 1, count_y) * RING_X + at_x},
    }


def ring_gather(store, at, count, devices, send, recv):
    half_rows = store.shape[1] // 2
    last = count // 2

    def copy_of(hop, way, part, arriving):
        moved = hop if arriving else hop - 1
        slot = wrap(at + (-moved if way == 0 else moved), count)
        spot = store.at[slot, pl.ds(part * half_rows, half_rows)]
        index = (hop - 1, way, part)
        return remote(spot, spot, send.at[index], recv.at[index], devices[way])

    messages = [
        (hop, way, part)
        for hop in range(1, last + 1)
        for part in (0, 1)
        for way in (0, 1)
        if hop < last or part == way
    ]
    for hop, way, part in messages:
        if hop > 1:
            copy_of(hop - 1, way, part, True).wait_recv()
        copy_of(hop, way, part, False).start()
        yield
    for hop, way, part in messages:
        if (hop + 1, way, part) not in messages:
            copy_of(hop, way, part, True).wait_recv()
    yield
    for hop, way, part in messages:
        copy_of(hop, way, part, False).wait_send()


def ring_sum(parts, out, arrived, leaving, at, count, devices, send, recv):
    half_rows = parts.shape[1] // 2
    last = count // 2

    def rows(part):
        return pl.ds(part * half_rows, half_rows)

    def copy_of(hop, way, part):
        index = (hop - 1, way, part)
        if hop == 1:
            source = parts.at[wrap(at + last, count), rows(part)]
        else:
            source = leaving.at[hop - 2, way, rows(part)]
        target = arrived.at[hop - 1, way, rows(part)]
        return remote(source, target, send.at[index], recv.at[index], devices[way])

    def summed(hop, way, part):
        slot = wrap(at + (last + 1 - hop if way == 0 else hop - 1 - last), count)
        value = parts[slot, rows(part)].astype(jnp.float32)
        if hop > 2 or part == way:
            copy_of(hop - 1, way, part).wait_recv()
            value += arrived[hop - 2, way, rows(part)].astype(jnp.float32)
        return value

    messages = [(1, way, way) for way in (0, 1)] + [
        (hop, way, part) for hop in range(2, last + 1) for part in (0, 1) for way in (0, 1)
    ]
    for hop, way, part in messages:
        if hop > 1:
            leaving[hop - 2, way, rows(part)] = summed(hop, way, part).astype(jnp.bfloat16)
        copy_of(hop, way, part).start()
        yield
    for part in (0, 1):
        value = parts[at, rows(part)].astype(jnp.float32)
        for way in (0, 1):
            copy_of(last, way, part).wait_recv()
            value += arrived[last - 1, way, rows(part)].astype(jnp.float32)
        out[rows(part)] = value.astype(jnp.bfloat16)
    yield
    for message in messages:
        copy_of(*message).wait_send()


def sum_over_mp(partial, out_ref, mine, gift, theirs, chip_sum, tiles, done, pair_send, pair_recv, z_send, z_recv, swap_send, swap_recv):
    chip, core, _, _, chips, _ = places()
    sibling = {"mp": 2 * chip + 1 - core}
    half = mine.shape[1]

    def give(step):
        return remote(gift.at[step], theirs.at[step], pair_send.at[step], pair_recv.at[step], sibling)

    def post(step):
        target = {"mp": 2 * lax.rem(chip + step, chips) + core}
        return remote(chip_sum.at[step], tiles.at[step], z_send.at[step - 1], z_recv.at[step - 1], target)

    order = sorted(range(1, chips), key=lambda step: -min(step, chips - step)) + [0]
    for step in order:
        tile = lax.rem(chip + step, chips)
        gift[step] = partial(tile, 1 - core).astype(jnp.bfloat16)
        give(step).start()
        mine[step] = partial(tile, core)
        yield
    for step in order:
        give(step).wait_recv()
        mine[step] += theirs[step].astype(jnp.float32)
        if step:
            chip_sum[step] = mine[step].astype(jnp.bfloat16)
            post(step).start()
        yield
    total = mine[0]
    for step in reversed(order[:-1]):
        post(step).wait_recv()
        total += tiles[step].astype(jnp.float32)
    done[...] = jnp.transpose(total).astype(jnp.bfloat16)
    columns = pl.ds(pl.multiple_of(core * half, half), half)
    other_columns = pl.ds(pl.multiple_of((1 - core) * half, half), half)
    own_rows = pl.ds(pl.multiple_of(core * HEAD, HEAD), HEAD)
    swap = remote(
        done.at[pl.ds(pl.multiple_of((1 - core) * HEAD, HEAD), HEAD)],
        out_ref.at[:, columns],
        swap_send,
        swap_recv,
        sibling,
    )
    swap.start()
    out_ref[:, columns] = done[own_rows]
    yield
    remote(done.at[own_rows], out_ref.at[:, other_columns], swap_send, swap_recv, sibling).wait_recv()
    swap.wait_send()
    for step in order:
        give(step).wait_send()
        if step:
            post(step).wait_send()


def sum_scratch(rows):
    chips = lax.axis_size("mp") // 2
    half = rows // 2
    dma = pltpu.SemaphoreType.DMA
    some = pltpu.VMEM((chips, half, PAIR), jnp.bfloat16)
    return [
        pltpu.VMEM((chips, half, PAIR), jnp.float32),
        some,
        some,
        some,
        some,
        pltpu.VMEM((PAIR, half), jnp.bfloat16),
        dma((chips,)),
        dma((chips,)),
        dma((chips - 1,)),
        dma((chips - 1,)),
        dma,
        dma,
    ]


def mp_partners(chip, core, chips):
    return [{"mp": 2 * chip + 1 - core}] + [
        {"mp": 2 * lax.rem(chip + step, chips) + core} for step in range(1, chips)
    ]


def seq_partners(at_y, at_x, count_y):
    along_x = [{"seq": at_y * RING_X + lax.rem(at_x + step, RING_X)} for step in range(1, RING_X)]
    along_y = [{"seq": lax.rem(at_y + step, count_y) * RING_X + at_x} for step in range(1, count_y)]
    return along_x, along_y


def half_rows_of(ref, half):
    rows = ref.shape[0] // 2
    return ref[pl.ds(pl.multiple_of(half * rows, rows), rows)]


def project_kernel(
    frames_ref,
    grad_ref,
    key_w,
    value_w,
    query_w,
    out_w,
    features,
    kv_ref,
    qg_ref,
    weights,
    mine,
    other,
    loaded,
    filled,
    pair_send,
    pair_recv,
    z_send,
    z_recv,
    share_send,
    share_recv,
    y_send,
    y_recv,
    x_send,
    x_recv,
):
    chip, core, at_y, at_x, chips, count_y = places()
    hops = chips // 2
    rows = features.shape[0]
    half, width = rows // 2, chips * PAIR
    sibling = {"mp": 2 * chip + 1 - core}
    right = {"mp": 2 * wrap(chip + 1, chips) + core}
    left = {"mp": 2 * wrap(chip - 1, chips) + core}
    inputs = stack_rows((frames_ref, grad_ref), mine, loaded)
    fill = stack_rows((key_w, value_w, query_w, out_w), weights, filled)
    for copy in inputs + fill:
        copy.start()
    greet([sibling, right, left] + list(neighbours(at_y, at_x, count_y).values()))
    for copy in inputs:
        copy.wait()

    def side(whose):
        return pl.ds(pl.multiple_of(whose * half, half), half)

    swap = remote(mine.at[:, side(1 - core)], other, pair_send, pair_recv, sibling)
    swap.start()
    swap.wait_recv()
    here, there = mine[:, side(core)].astype(jnp.float32), other[...].astype(jnp.float32)
    even = jnp.where(core == 0, here, there)
    odd = jnp.where(core == 0, there, here)
    for kind in (0, 1):
        part = slice(kind * HEAD, (kind + 1) * HEAD)
        tile = jnp.transpose(jnp.concatenate([even[part], odd[part]], axis=0))
        column = pl.multiple_of(kind * width + chip * PAIR, PAIR)
        features[side(core), pl.ds(column, PAIR)] = tile.astype(jnp.bfloat16)

    def place(kind, tile, way, hop):
        start = pl.multiple_of(kind * width + wrap(tile, chips) * PAIR, PAIR)
        count = half if hop < hops else half // 2
        first = core * half + (0 if hop < hops else way * count)
        return features.at[pl.ds(pl.multiple_of(first, count), count), pl.ds(start, PAIR)]

    def along_z(kind, way, hop, moved):
        spot = place(kind, chip + (-moved if way == 0 else moved), way, hop)
        at = (kind, way, hop - 1)
        return remote(spot, spot, z_send.at[at], z_recv.at[at], right if way == 0 else left)

    def sent(kind, way, hop):
        return along_z(kind, way, hop, hop - 1)

    def landed(kind, way, hop):
        return along_z(kind, way, hop, hop)

    def shared(kind, whose):
        spot = features.at[side(whose), pl.ds(kind * width, width)]
        return remote(spot, spot, share_send.at[kind], share_recv.at[kind], sibling)

    def advance(kind, hop):
        for way in (0, 1):
            landed(kind, way, hop).wait_recv()
            if hop < hops:
                sent(kind, way, hop + 1).start()
        if hop == hops:
            shared(kind, core).start()

    def begin(kind):
        for way in (0, 1):
            sent(kind, way, 1).start()

    begin(0)
    for hop in range(1, hops + 1):
        advance(0, hop)
        if hop == hops - 2:
            begin(1)
        if hop > hops - 2:
            advance(1, hop - hops + 2)
    for copy in fill:
        copy.wait()
    shared(0, 1 - core).wait_recv()

    lane = lax.broadcasted_iota(jnp.int32, (BLK, PAIR), 1)
    blocks = [slice(start, start + BLK) for start in range(0, rows, BLK)]
    against = (((1,), (1,)), ((), ()))
    for block in blocks:
        product = lax.dot_general(
            features[block, :width], weights[...], against, preferred_element_type=jnp.float32
        )
        kv_ref[at_y, block] = product[:, :PAIR].astype(jnp.bfloat16)
        qg_ref[at_x, block] = product[:, PAIR:].astype(jnp.bfloat16)
    near = neighbours(at_y, at_x, count_y)
    over_y = ring_gather(kv_ref, at_y, count_y, (near["y", 1], near["y", -1]), y_send, y_recv)
    take(over_y, 4)
    for hop in range(3, hops + 1):
        advance(1, hop)
    shared(1, 1 - core).wait_recv()
    for block in blocks:
        product = lax.dot_general(
            features[block, width:], weights[PAIR:], against, preferred_element_type=jnp.float32
        )
        pair = jnp.where(lane < HEAD, qg_ref[at_x, block], product.astype(jnp.bfloat16))
        qg_ref[at_x, block] = pair
    over_x = ring_gather(qg_ref, at_x, RING_X, (near["x", 1], near["x", -1]), x_send, x_recv)
    take(over_x, 4)
    take(over_y, 4)
    take(over_x, 2)
    finish(over_y)
    finish(over_x)
    swap.wait_send()
    for kind in (0, 1):
        shared(kind, core).wait_send()
        for hop in range(1, hops + 1):
            for way in (0, 1):
                sent(kind, way, hop).wait_send()


def project(frames, cotangent, weights):
    cores, peers = lax.axis_size("mp"), lax.axis_size("seq")
    rows = frames.shape[0]
    dma = pltpu.SemaphoreType.DMA
    sems = dma((2, 2, cores // 4))
    x_sems, y_sems = dma((RING_X // 2, 2, 2)), dma((peers // RING_X // 2, 2, 2))
    return pl.pallas_call(
        project_kernel,
        out_shape=(
            jax.ShapeDtypeStruct((rows, cores * PAIR), jnp.bfloat16),
            jax.ShapeDtypeStruct((peers // RING_X, rows, PAIR), jnp.bfloat16),
            jax.ShapeDtypeStruct((RING_X, rows, PAIR), jnp.bfloat16),
        ),
        in_specs=[ANY] * 6,
        out_specs=(VMEM, VMEM, VMEM),
        scratch_shapes=[
            pltpu.VMEM((4 * HEAD, D), jnp.bfloat16),
            pltpu.VMEM((PAIR, rows), jnp.bfloat16),
            pltpu.VMEM((PAIR, rows // 2), jnp.bfloat16),
            dma((2,)),
            dma((4,)),
            dma,
            dma,
            sems,
            sems,
            dma((2,)),
            dma((2,)),
            y_sems,
            y_sems,
            x_sems,
            x_sems,
        ],
        compiler_params=pltpu.CompilerParams(
            collective_id=0, has_side_effects=True, vmem_limit_bytes=60 * 1024 * 1024
        ),
        name="project",
    )(frames.T, cotangent.T, *weights)


def list_pairs(turn_ref, own_ref, far_ref):
    _, _, at_y, at_x, _, count_y = places()
    count = jnp.int32(0)
    spread = RING_X * ROWS

    def add(count, own, far, ok):
        own_ref[count] = jnp.clip(own, 0, spread - 1)
        far_ref[count] = jnp.clip(far, 0, count_y * ROWS - 1)
        return count + ok.astype(jnp.int32)

    for block in range(ROWS):
        for offset in range(-BAND, BAND + 1):
            own = at_x * ROWS + block + offset
            count = add(count, own, at_y * ROWS + block, (own >= 0) & (own < spread))
    first, final = at_x == 0, at_x == RING_X - 1
    crosses = (first & (at_y + 1 < count_y)) | (final & (at_y > 0))
    for ahead in range(BAND):
        for back in range(BAND - ahead):
            own = jnp.where(first, spread - 1 - back, back)
            far = jnp.where(first, (at_y + 1) * ROWS + ahead, at_y * ROWS - 1 - ahead)
            count = add(count, own, far, crosses)

    def visit(index, count):
        row, column = lax.div(index, RING_X), lax.rem(index, RING_X)
        holder, partner = at_y * RING_X + column, row * RING_X + at_x
        for slot in range(turn_ref.shape[1]):
            own = turn_ref[holder, slot, partner]
            far = turn_ref[partner, slot, holder]
            ok = (own >= 0) & (jnp.abs(own - far) > BAND)
            count = add(count, own - at_y * spread, far + (row - partner) * ROWS, ok)
        return count

    count = lax.fori_loop(0, count_y * RING_X, visit, count)
    for pad in range(UNROLL):
        own_ref[count + pad] = 0
        far_ref[count + pad] = 0
    return count


def most_pairs(turns):
    return ROWS * (2 * BAND + 1) + BAND * (BAND + 1) // 2 + turns.shape[0] * turns.shape[1] + UNROLL


def forward_kernel(turn_ref, qg_ref, kv_ref, out_ref, own_list, far_list, lhs, score, top, total, mixed):
    count = list_pairs(turn_ref, own_list, far_list)
    rounds = lax.div(count + UNROLL - 1, UNROLL)
    lane = lax.broadcasted_iota(jnp.int32, (BLK, PAIR), 1)
    blocks = qg_ref.shape[0]
    zero = jnp.zeros((BLK, PAIR), jnp.bfloat16)
    for block in range(blocks):
        lhs[block] = jnp.where(lane < HEAD, qg_ref[block], zero)
    top[...] = jnp.full_like(top, LEAST)
    total[...] = jnp.zeros_like(total)
    mixed[...] = jnp.zeros_like(mixed)

    def tiles(step):
        at = [step * UNROLL + u for u in range(UNROLL)]
        return [(tile, own_list[tile], far_list[tile]) for tile in at]

    def score_step(step, carry):
        now = tiles(step)
        products = [
            lax.dot_general(
                lhs[own], kv_ref[far], (((1,), (1,)), ((), ())), preferred_element_type=jnp.float32
            )
            for _, own, far in now
        ]
        scaled = []
        for (tile, _, _), product in zip(now, products):
            masked = product * EXP2_SCALE + jnp.where(tile < count, 0.0, -jnp.inf)
            score[tile] = masked
            scaled.append(masked)
        for (_, own, _), masked in zip(now, scaled):
            top[own] = jnp.maximum(top[own], masked)
        return carry

    lax.fori_loop(0, rounds, score_step, 0)
    for block in range(blocks):
        top[block] = jnp.broadcast_to(jnp.max(top[block], axis=1, keepdims=True), (BLK, PAIR))

    def weight_step(step, carry):
        now = tiles(step)
        weights = [jnp.exp2(score[tile] - top[own]) for tile, own, _ in now]
        sums = [
            jnp.dot(weight.astype(jnp.bfloat16), kv_ref[far], preferred_element_type=jnp.float32)
            for weight, (_, _, far) in zip(weights, now)
        ]
        for (_, own, _), weight, part in zip(now, weights, sums):
            total[own] += weight
            mixed[own] += part
        return carry

    lax.fori_loop(0, rounds, weight_step, 0)
    for device in range(RING_X):
        column = jnp.zeros((BLK, PAIR), jnp.float32)
        for block in range(ROWS):
            at = device * ROWS + block
            column = jnp.where(lane == block, top[at], column)
            column = jnp.where(lane == ROWS + block, jnp.sum(total[at], axis=1, keepdims=True), column)
        for pair in range(ROWS // 2):
            even, odd = mixed[device * ROWS + 2 * pair], mixed[device * ROWS + 2 * pair + 1]
            out_ref[device, pair * BLK : (pair + 1) * BLK] = jnp.where(
                lane < HEAD, pltpu.roll(even, HEAD, 1), odd
            )
        out_ref[device, ROWS // 2 * BLK :] = jnp.transpose(column)[: 2 * ROWS]


def attend_forward(turns, qg, kv):
    most = most_pairs(turns)
    blocks = RING_X * ROWS
    square = pltpu.VMEM((blocks, BLK, PAIR), jnp.float32)
    return pl.pallas_call(
        forward_kernel,
        out_shape=jax.ShapeDtypeStruct((RING_X, ROWS // 2 * BLK + 2 * ROWS, PAIR), jnp.float32),
        in_specs=[SMEM, VMEM, VMEM],
        out_specs=VMEM,
        scratch_shapes=[
            pltpu.SMEM((most,), jnp.int32),
            pltpu.SMEM((most,), jnp.int32),
            pltpu.VMEM((blocks, BLK, PAIR), jnp.bfloat16),
            pltpu.VMEM((most, BLK, BLK), jnp.float32),
            square,
            square,
            square,
        ],
        compiler_params=pltpu.CompilerParams(vmem_limit_bytes=LIMIT),
        cost_estimate=pl.CostEstimate(
            flops=most * 4 * BLK * BLK * PAIR, bytes_accessed=kv.size * 4, transcendentals=most * BLK * BLK
        ),
        name="attend_forward",
    )(turns, qg.reshape(-1, BLK, PAIR), kv.reshape(-1, BLK, PAIR))


def backward_kernel(
    turn_ref, qg_ref, kv_ref, stats_ref, query_ref, key_ref, own_list, far_list, rhs, query, key
):
    count = list_pairs(turn_ref, own_list, far_list)
    rounds = lax.div(count + UNROLL - 1, UNROLL)
    lane = lax.broadcasted_iota(jnp.int32, (BLK, PAIR), 1)
    zero = jnp.zeros((BLK, PAIR), jnp.bfloat16)
    for block in range(qg_ref.shape[0]):
        pair = qg_ref[block]
        rhs[block, :BLK] = jnp.where(lane < HEAD, pair, zero)
        rhs[block, BLK:] = jnp.where(lane < HEAD, zero, pair)
    query[...] = jnp.zeros_like(query)
    key[...] = jnp.zeros_like(key)

    def step_of(step, carry):
        now = []
        for u in range(UNROLL):
            tile = step * UNROLL + u
            now.append((tile, own_list[tile], far_list[tile]))
        both = [
            lax.dot_general(
                kv_ref[far], rhs[own], (((1,), (1,)), ((), ())), preferred_element_type=jnp.float32
            )
            for _, own, far in now
        ]
        factors = []
        for (tile, own, _), product in zip(now, both):
            device, block = lax.div(own, ROWS), lax.rem(own, ROWS)
            top, inverse, drift = (
                stats_ref[device, pl.ds(kind * ROWS + block, 1), :] for kind in range(3)
            )
            masked = product[:, :BLK] * EXP2_SCALE + jnp.where(tile < count, 0.0, -jnp.inf)
            prob = jnp.exp2(masked - top) * inverse
            slope = prob * (product[:, BLK:] - drift)
            factors.append((slope.astype(jnp.bfloat16), prob.astype(jnp.bfloat16)))
        to_keys = [
            jnp.dot(jnp.concatenate(factor, axis=1), rhs[own], preferred_element_type=jnp.float32)
            for factor, (_, own, _) in zip(factors, now)
        ]
        to_queries = [
            lax.dot_general(
                slope, kv_ref[far], (((0,), (0,)), ((), ())), preferred_element_type=jnp.float32
            )
            for (slope, _), (_, _, far) in zip(factors, now)
        ]
        for (_, own, far), to_key, to_query in zip(now, to_keys, to_queries):
            key[far] += to_key
            query[own] += to_query
        return carry

    lax.fori_loop(0, rounds, step_of, 0)
    for block in range(key.shape[0]):
        key_ref[block] = jnp.where(lane < HEAD, key[block] * SCALE, key[block]).astype(jnp.bfloat16)
    for device in range(RING_X):
        for pair in range(ROWS // 2):
            even, odd = query[device * ROWS + 2 * pair], query[device * ROWS + 2 * pair + 1]
            query_ref[device, pair * BLK : (pair + 1) * BLK] = (
                jnp.where(lane < HEAD, even, pltpu.roll(odd, HEAD, 1)) * SCALE
            )


def attend_backward(turns, qg, kv, stats):
    most = most_pairs(turns)
    blocks, keys = RING_X * ROWS, kv.shape[0] * ROWS
    return pl.pallas_call(
        backward_kernel,
        out_shape=(
            jax.ShapeDtypeStruct((RING_X, ROWS // 2 * BLK, PAIR), jnp.float32),
            jax.ShapeDtypeStruct((keys, BLK, PAIR), jnp.bfloat16),
        ),
        in_specs=[SMEM, VMEM, VMEM, VMEM],
        out_specs=(VMEM, VMEM),
        scratch_shapes=[
            pltpu.SMEM((most,), jnp.int32),
            pltpu.SMEM((most,), jnp.int32),
            pltpu.VMEM((blocks, 2 * BLK, PAIR), jnp.bfloat16),
            pltpu.VMEM((blocks, BLK, PAIR), jnp.float32),
            pltpu.VMEM((keys, BLK, PAIR), jnp.float32),
        ],
        compiler_params=pltpu.CompilerParams(vmem_limit_bytes=LIMIT),
        cost_estimate=pl.CostEstimate(
            flops=most * 10 * BLK * BLK * PAIR, bytes_accessed=kv.size * 4, transcendentals=most * BLK * BLK
        ),
        name="attend_backward",
    )(turns, qg.reshape(-1, BLK, PAIR), kv.reshape(-1, BLK, PAIR), stats)


def combine_kernel(parts, qg_ref, context, stats_ref, got, send, recv, s_send, s_recv):
    _, _, at_y, at_x, _, count_y = places()
    along_x, _ = seq_partners(at_y, at_x, count_y)
    greet(along_x)
    steps = range(len(along_x))

    def give(step):
        target = lax.rem(at_x + step + 1, RING_X)
        return remote(parts.at[target], got.at[step], send.at[step], recv.at[step], along_x[step])

    def tell(step, slot):
        part = stats_ref.at[slot]
        return remote(part, part, s_send.at[step], s_recv.at[step], along_x[step])

    for step in steps:
        give(step).start()
    for step in steps:
        give(step).wait_recv()
    packed = ROWS // 2 * BLK
    lane = lax.broadcasted_iota(jnp.int32, (BLK, PAIR), 1)

    def values(start, count):
        rows = slice(start, start + count)
        return [parts[at_x, rows]] + [got[step, rows] for step in steps]

    tops, totals = values(packed, ROWS), values(packed + ROWS, ROWS)
    top = functools.reduce(jnp.maximum, tops)
    factors = [jnp.exp2(part - top) for part in tops]
    inverse = 1.0 / sum(factor * part for factor, part in zip(factors, totals))
    shares = [factor * inverse for factor in factors]
    blank = jnp.zeros((BLK - ROWS * RING_X, PAIR), jnp.float32)
    columns = jnp.transpose(jnp.concatenate(shares + [blank], axis=0))
    drifts = jnp.zeros((BLK, PAIR), jnp.float32)
    for block in range(ROWS):
        output = jnp.zeros((BLK, PAIR), jnp.float32)
        for index, part in enumerate(values(block // 2 * BLK, BLK)):
            at = index * ROWS + block
            output += (part if block % 2 else pltpu.roll(part, HEAD, 1)) * columns[:, at : at + 1]
        output = jnp.where(lane < HEAD, 0.0, output)
        rows = slice(block * BLK, (block + 1) * BLK)
        context[rows] = output.astype(jnp.bfloat16)
        drift = jnp.sum(qg_ref[at_x, rows].astype(jnp.float32) * output, axis=1, keepdims=True)
        drifts = jnp.where(lane == block, drift, drifts)
    drift_rows = jnp.transpose(drifts)[: 2 * ROWS]
    stats_ref[at_x] = jnp.concatenate([top, inverse, drift_rows], axis=0)
    for step in steps:
        tell(step, at_x).start()
    for step in steps:
        tell(step, wrap(at_x - step - 1, RING_X)).wait_recv()
    for step in steps:
        give(step).wait_send()
        tell(step, at_x).wait_send()


def combine(parts, qg):
    sems = pltpu.SemaphoreType.DMA((RING_X - 1,))
    return pl.pallas_call(
        combine_kernel,
        out_shape=(
            jax.ShapeDtypeStruct((ROWS * BLK, PAIR), jnp.bfloat16),
            jax.ShapeDtypeStruct((RING_X, 4 * ROWS, PAIR), jnp.float32),
        ),
        in_specs=[VMEM, VMEM],
        out_specs=(VMEM, VMEM),
        scratch_shapes=[pltpu.VMEM((RING_X - 1,) + parts.shape[1:], jnp.float32), sems, sems, sems, sems],
        compiler_params=pltpu.CompilerParams(
            collective_id=1, has_side_effects=True, vmem_limit_bytes=LIMIT
        ),
        name="combine",
    )(parts, qg)


def sum_over_seq(parts, sums_ref, x_sum, arrived, leaving, from_y, piece, totals, sems):
    _, _, at_y, at_x, _, count_y = places()
    near = neighbours(at_y, at_x, count_y)
    around = (near["x", 1], near["x", -1])
    _, along_y = seq_partners(at_y, at_x, count_y)
    ys = range(len(along_y))

    def columns(index):
        return pl.ds(pl.multiple_of(index * PAIR, PAIR), PAIR)

    def in_y(step):
        source = x_sum.at[:, columns(lax.rem(at_y + step + 1, count_y))]
        return remote(source, from_y.at[step], sems[2].at[step], sems[3].at[step], along_y[step])

    def out_y(step, owner):
        target = totals.at[at_x, :, columns(owner)]
        return remote(piece, target, sems[4].at[step], sems[5].at[step], along_y[step])

    over_x = ring_sum(parts, x_sum, arrived, leaving, at_x, RING_X, around, sems[0], sems[1])
    take(over_x, 2)
    yield
    take(over_x, 4)
    yield
    take(over_x, 1)
    for step in ys:
        in_y(step).start()
    yield
    total = x_sum[:, columns(at_y)].astype(jnp.float32)
    for step in ys:
        in_y(step).wait_recv()
        total += from_y[step].astype(jnp.float32)
    piece[...] = total.astype(jnp.bfloat16)
    for step in ys:
        out_y(step, at_y).start()
    totals[at_x, :, columns(at_y)] = piece[...]
    yield
    for step in ys:
        out_y(step, wrap(at_y - step - 1, count_y)).wait_recv()
    back = ring_gather(totals, at_x, RING_X, around, sems[6], sems[7])
    take(back, 4)
    yield
    finish(back)
    for index in range(RING_X):
        sums_ref[index * HEAD : (index + 1) * HEAD] = totals[index].astype(jnp.float32)
    finish(over_x)
    for step in ys:
        in_y(step).wait_send()
        out_y(step, at_y).wait_send()


def gradient_kernel(
    query_parts,
    key_parts,
    context,
    features_ref,
    key_w,
    value_w,
    query_w,
    out_w,
    attended,
    grad_frames,
    sums_ref,
    features,
    weights,
    filled,
    loaded,
    joint,
    lhs,
    got,
    key_sum,
    arrived,
    leaving,
    x_send,
    x_recv,
    y_send,
    y_recv,
    products,
    x_sum,
    w_arrived,
    w_leaving,
    from_y,
    piece,
    totals,
    *refs,
):
    chip, core, at_y, at_x, chips, count_y = places()
    along_x, along_y = seq_partners(at_y, at_x, count_y)
    near = neighbours(at_y, at_x, count_y)
    fill = stack_rows((key_w, value_w, query_w, out_w), weights, filled)
    load = pltpu.make_async_copy(features_ref, features, loaded)
    for copy in fill + [load]:
        copy.start()
    greet(along_x + along_y + mp_partners(chip, core, chips))
    steps = range(len(along_x))

    def give(step):
        target = lax.rem(at_x + step + 1, RING_X)
        return remote(query_parts.at[target], got.at[step], x_send.at[step], x_recv.at[step], along_x[step])

    over_y = ring_sum(
        key_parts, key_sum, arrived, leaving, at_y, count_y, (near["y", 1], near["y", -1]), y_send, y_recv
    )
    take(over_y, 4)
    for step in steps:
        give(step).start()
    for copy in fill:
        copy.wait()

    def columns(tile):
        return pl.ds(pl.multiple_of(tile * PAIR, PAIR), PAIR)

    def output_part(tile, half):
        return jnp.dot(
            half_rows_of(context, half), weights[PAIR:, columns(tile)], preferred_element_type=jnp.float32
        )

    def input_part(tile, half):
        return jnp.dot(half_rows_of(lhs, half), weights[:, columns(tile)], preferred_element_type=jnp.float32)

    half_refs = len(refs[8:]) // 2
    outputs = sum_over_mp(output_part, attended, *refs[8 : 8 + half_refs])
    inputs = sum_over_mp(input_part, grad_frames, *refs[8 + half_refs :])
    for _ in range(chips):
        take(outputs, 2)
        take(over_y, 1)
    lane = lax.broadcasted_iota(jnp.int32, (BLK, PAIR), 1)
    for step in steps:
        give(step).wait_recv()
    for pair in range(ROWS // 2):
        part = slice(pair * BLK, (pair + 1) * BLK)
        total = query_parts[at_x, part]
        for step in steps:
            total += got[step, part]
        for block, value in ((2 * pair, total), (2 * pair + 1, pltpu.roll(total, HEAD, 1))):
            rows = slice(block * BLK, (block + 1) * BLK)
            value = value.astype(jnp.bfloat16)
            joint[rows] = jnp.where(lane < HEAD, value, context[rows])
            lhs[rows, PAIR:] = jnp.where(lane < HEAD, value, jnp.zeros_like(value))
    load.wait()
    width = products.shape[2]
    along_rows = (((0,), (0,)), ((), ()))
    for index, at in ((2, 0), (3, 1)):
        product = lax.dot_general(
            joint[...],
            features[:, at * width : (at + 1) * width],
            along_rows,
            preferred_element_type=jnp.float32,
        )
        products[index] = product[at * HEAD : (at + 1) * HEAD].astype(jnp.bfloat16)
    take(over_y, 3)
    lhs[:, :PAIR] = key_sum[...]
    product = lax.dot_general(
        key_sum[...], features[:, :width], along_rows, preferred_element_type=jnp.float32
    )
    products[0] = product[:HEAD].astype(jnp.bfloat16)
    products[1] = product[HEAD:].astype(jnp.bfloat16)
    over_seq = sum_over_seq(products, sums_ref, x_sum, w_arrived, w_leaving, from_y, piece, totals, refs[:8])
    take(over_seq, 1)
    take(inputs, chips)
    take(over_seq, 1)
    take(inputs, chips)
    take(over_seq, 1)
    take(outputs, 1)
    take(over_seq, 2)
    take(inputs, 1)
    finish(over_seq)
    finish(outputs)
    finish(inputs)
    finish(over_y)
    for step in steps:
        give(step).wait_send()


def sum_gradients(query_parts, key_parts, context, features, weights):
    peers = lax.axis_size("seq")
    rows = context.shape[0]
    count_y = peers // RING_X
    dma = pltpu.SemaphoreType.DMA
    x_sems, y_sems = dma((RING_X - 1,)), dma((count_y - 1,))
    x_ring, y_ring = dma((RING_X // 2, 2, 2)), dma((count_y // 2, 2, 2))
    out = jax.ShapeDtypeStruct((HEAD, rows), jnp.bfloat16)
    stack = (RING_X, HEAD, D)

    def rounded(*shape):
        return pltpu.VMEM(shape, jnp.bfloat16)

    return pl.pallas_call(
        gradient_kernel,
        out_shape=(out, out, jax.ShapeDtypeStruct((RING_X * HEAD, D), jnp.float32)),
        in_specs=[VMEM] * 3 + [ANY] * 5,
        out_specs=(VMEM, VMEM, VMEM),
        scratch_shapes=[
            rounded(*features.shape),
            rounded(RING_X * HEAD, D),
            dma((4,)),
            dma,
            rounded(rows, PAIR),
            rounded(rows, 2 * PAIR),
            pltpu.VMEM((RING_X - 1,) + query_parts.shape[1:], jnp.float32),
            rounded(rows, PAIR),
            rounded(count_y // 2, 2, rows, PAIR),
            rounded(count_y // 2 - 1, 2, rows, PAIR),
            x_sems,
            x_sems,
            y_ring,
            y_ring,
            rounded(*stack),
            rounded(HEAD, D),
            rounded(RING_X // 2, 2, HEAD, D),
            rounded(RING_X // 2 - 1, 2, HEAD, D),
            rounded(count_y - 1, HEAD, PAIR),
            rounded(HEAD, PAIR),
            rounded(*stack),
            x_ring,
            x_ring,
            y_sems,
            y_sems,
            y_sems,
            y_sems,
            x_ring,
            x_ring,
        ]
        + sum_scratch(rows)
        + sum_scratch(rows),
        compiler_params=pltpu.CompilerParams(
            collective_id=2, has_side_effects=True, vmem_limit_bytes=LIMIT
        ),
        name="sum_gradients",
    )(query_parts, key_parts.reshape(count_y, rows, PAIR), context, features, *weights)


def on_device(frames, cotangent, query_weight, key_weight, value_weight, out_weight, turn_blocks):
    turns = jnp.transpose(turn_blocks, (0, 2, 1))
    weights = (key_weight, value_weight, query_weight, out_weight)
    features, kv, qg = project(frames, cotangent, weights)
    context, stats = combine(attend_forward(turns, qg, kv), qg)
    query_parts, key_parts = attend_backward(turns, qg, kv, stats)
    attended, grad_frames, sums = sum_gradients(query_parts, key_parts, context, features, weights)
    grad_key, grad_value, grad_query, grad_out = (
        sums[index * HEAD : (index + 1) * HEAD] for index in range(4)
    )
    return attended.T, grad_frames.T, grad_query, grad_key, grad_value, grad_out


def solution(mesh):
    return jax.shard_map(
        on_device,
        mesh=mesh,
        in_specs=(
            P("seq", "mp"),
            P("seq", "mp"),
            P("mp", None),
            P("mp", None),
            P("mp", None),
            P("mp", None),
            P(),
        ),
        out_specs=(
            P("seq", "mp"),
            P("seq", "mp"),
            P("mp", None),
            P("mp", None),
            P("mp", None),
            P("mp", None),
        ),
        check_vma=False,
    )
```

```python
import functools
import math

import jax
import jax.numpy as jnp
from jax import lax
from jax.experimental import pallas as pl
from jax.experimental.pallas import tpu as pltpu
from jax.sharding import PartitionSpec as P

D = 1024
HEADS = 16
BLK = 128
BAND = 2
RING_X = 4
ROWS = 4
LEAST = -3e38
HEAD = D // HEADS
PAIR = 2 * HEAD
UNROLL = 8
SCALE = 1.0 / math.sqrt(HEAD)
EXP2_SCALE = SCALE * math.log2(math.e)
MESH = pl.DeviceIdType.MESH
VMEM = pl.BlockSpec(memory_space=pltpu.VMEM)
SMEM = pl.BlockSpec(memory_space=pltpu.SMEM)
ANY = pl.BlockSpec(memory_space=pl.ANY)
LIMIT = 48 * 1024 * 1024


def wrap(index, count):
    return lax.rem(index + count, count)


def greet(devices):
    barrier = pltpu.get_barrier_semaphore()
    for device in devices:
        pl.semaphore_signal(barrier, inc=1, device_id=device, device_id_type=MESH)
    pl.semaphore_wait(barrier, len(devices))


def remote(source, target, send, recv, device):
    return pltpu.make_async_remote_copy(
        source, target, send, recv, device_id=device, device_id_type=MESH
    )


def take(process, count):
    for _ in range(count):
        next(process, None)


def finish(process):
    for _ in process:
        pass


def stack_rows(refs, whole, sems):
    copies = []
    for index, ref in enumerate(refs):
        target = whole.at[pl.ds(index * HEAD, HEAD)]
        copies.append(pltpu.make_async_copy(ref, target, sems.at[index]))
    return copies


def places():
    me_mp, me = lax.axis_index("mp"), lax.axis_index("seq")
    chips, count_y = lax.axis_size("mp") // 2, lax.axis_size("seq") // RING_X
    return lax.div(me_mp, 2), lax.rem(me_mp, 2), lax.div(me, RING_X), lax.rem(me, RING_X), chips, count_y


def neighbours(at_y, at_x, count_y):
    return {
        ("x", 1): {"seq": at_y * RING_X + wrap(at_x + 1, RING_X)},
        ("x", -1): {"seq": at_y * RING_X + wrap(at_x - 1, RING_X)},
        ("y", 1): {"seq": wrap(at_y + 1, count_y) * RING_X + at_x},
        ("y", -1): {"seq": wrap(at_y - 1, count_y) * RING_X + at_x},
    }


def ring_messages(count, parts):
    return [
        (hop, way, part)
        for hop in range(1, count // 2 + 1)
        for part in range(parts)
        for way in (0, 1)
        if hop < count // 2 or part // (parts // 2) == way
    ]


def ring_gather(store, at, count, devices, send, recv):
    parts = send.shape[2]
    part_rows = store.shape[1] // parts

    def copy_of(hop, way, part, arriving):
        moved = hop if arriving else hop - 1
        slot = wrap(at + (-moved if way == 0 else moved), count)
        spot = store.at[slot, pl.ds(part * part_rows, part_rows)]
        index = (hop - 1, way, part)
        return remote(spot, spot, send.at[index], recv.at[index], devices[way])

    messages = ring_messages(count, parts)
    for hop, way, part in messages:
        if hop > 1:
            copy_of(hop - 1, way, part, True).wait_recv()
        copy_of(hop, way, part, False).start()
        yield
    for hop, way, part in messages:
        if (hop + 1, way, part) not in messages:
            copy_of(hop, way, part, True).wait_recv()
    yield
    for hop, way, part in messages:
        copy_of(hop, way, part, False).wait_send()


def ring_sum(values, out, arrived, leaving, at, count, devices, send, recv):
    parts = send.shape[2]
    part_rows = values.shape[1] // parts
    last = count // 2

    def rows(part):
        return pl.ds(part * part_rows, part_rows)

    def copy_of(hop, way, part):
        index = (hop - 1, way, part)
        if hop == 1:
            source = values.at[wrap(at + last, count), rows(part)]
        else:
            source = leaving.at[hop - 2, way, rows(part)]
        target = arrived.at[hop - 1, way, rows(part)]
        return remote(source, target, send.at[index], recv.at[index], devices[way])

    messages = [
        (hop, way, part)
        for hop in range(1, last + 1)
        for part in range(parts)
        for way in (0, 1)
        if hop > 1 or part // (parts // 2) == way
    ]

    def summed(hop, way, part):
        slot = wrap(at + (last + 1 - hop if way == 0 else hop - 1 - last), count)
        value = values[slot, rows(part)].astype(jnp.float32)
        if (hop - 1, way, part) in messages:
            copy_of(hop - 1, way, part).wait_recv()
            value += arrived[hop - 2, way, rows(part)].astype(jnp.float32)
        return value

    for hop, way, part in messages:
        if hop > 1:
            leaving[hop - 2, way, rows(part)] = summed(hop, way, part).astype(jnp.bfloat16)
        copy_of(hop, way, part).start()
        yield
    for part in range(parts):
        value = values[at, rows(part)].astype(jnp.float32)
        for way in (0, 1):
            copy_of(last, way, part).wait_recv()
            value += arrived[last - 1, way, rows(part)].astype(jnp.float32)
        out[rows(part)] = value.astype(jnp.bfloat16)
    yield
    for message in messages:
        copy_of(*message).wait_send()


def sum_over_mp(partial, out_ref, mine, gift, theirs, chip_sum, tiles, done, pair_send, pair_recv, z_send, z_recv, swap_send, swap_recv):
    chip, core, _, _, chips, _ = places()
    sibling = {"mp": 2 * chip + 1 - core}
    half = mine.shape[1]

    def give(step):
        return remote(gift.at[step], theirs.at[step], pair_send.at[step], pair_recv.at[step], sibling)

    def post(step):
        target = {"mp": 2 * lax.rem(chip + step, chips) + core}
        return remote(chip_sum.at[step], tiles.at[step], z_send.at[step - 1], z_recv.at[step - 1], target)

    order = sorted(range(1, chips), key=lambda step: -min(step, chips - step)) + [0]
    for step in order:
        tile = lax.rem(chip + step, chips)
        gift[step] = partial(tile, 1 - core).astype(jnp.bfloat16)
        give(step).start()
        mine[step] = partial(tile, core)
        yield
    for step in order:
        give(step).wait_recv()
        mine[step] += theirs[step].astype(jnp.float32)
        if step:
            chip_sum[step] = mine[step].astype(jnp.bfloat16)
            post(step).start()
        yield
    total = mine[0]
    for step in reversed(order[:-1]):
        post(step).wait_recv()
        total += tiles[step].astype(jnp.float32)
    done[...] = jnp.transpose(total).astype(jnp.bfloat16)
    columns = pl.ds(pl.multiple_of(core * half, half), half)
    other_columns = pl.ds(pl.multiple_of((1 - core) * half, half), half)
    own_rows = pl.ds(pl.multiple_of(core * HEAD, HEAD), HEAD)
    swap = remote(
        done.at[pl.ds(pl.multiple_of((1 - core) * HEAD, HEAD), HEAD)],
        out_ref.at[:, columns],
        swap_send,
        swap_recv,
        sibling,
    )
    swap.start()
    out_ref[:, columns] = done[own_rows]
    yield
    remote(done.at[own_rows], out_ref.at[:, other_columns], swap_send, swap_recv, sibling).wait_recv()
    swap.wait_send()
    for step in order:
        give(step).wait_send()
        if step:
            post(step).wait_send()


def sum_scratch(rows):
    chips = lax.axis_size("mp") // 2
    half = rows // 2
    dma = pltpu.SemaphoreType.DMA
    some = pltpu.VMEM((chips, half, PAIR), jnp.bfloat16)
    return [
        pltpu.VMEM((chips, half, PAIR), jnp.float32),
        some,
        some,
        some,
        some,
        pltpu.VMEM((PAIR, half), jnp.bfloat16),
        dma((chips,)),
        dma((chips,)),
        dma((chips - 1,)),
        dma((chips - 1,)),
        dma,
        dma,
    ]


def mp_partners(chip, core, chips):
    return [{"mp": 2 * chip + 1 - core}] + [
        {"mp": 2 * lax.rem(chip + step, chips) + core} for step in range(1, chips)
    ]


def seq_partners(at_y, at_x, count_y):
    along_x = [{"seq": at_y * RING_X + lax.rem(at_x + step, RING_X)} for step in range(1, RING_X)]
    along_y = [{"seq": lax.rem(at_y + step, count_y) * RING_X + at_x} for step in range(1, count_y)]
    return along_x, along_y


def half_rows_of(ref, half):
    rows = ref.shape[0] // 2
    return ref[pl.ds(pl.multiple_of(half * rows, rows), rows)]


def project_kernel(
    frames_ref,
    grad_ref,
    key_w,
    value_w,
    query_w,
    out_w,
    features,
    kv_ref,
    qg_ref,
    weights,
    mine,
    other,
    loaded,
    filled,
    pair_send,
    pair_recv,
    z_send,
    z_recv,
    share_send,
    share_recv,
    y_send,
    y_recv,
    x_send,
    x_recv,
):
    chip, core, at_y, at_x, chips, count_y = places()
    hops = chips // 2
    rows = features.shape[0]
    half, width = rows // 2, chips * PAIR
    sibling = {"mp": 2 * chip + 1 - core}
    right = {"mp": 2 * wrap(chip + 1, chips) + core}
    left = {"mp": 2 * wrap(chip - 1, chips) + core}
    inputs = stack_rows((frames_ref, grad_ref), mine, loaded)
    fill = stack_rows((key_w, value_w, query_w, out_w), weights, filled)
    for copy in inputs + fill:
        copy.start()
    greet([sibling, right, left] + list(neighbours(at_y, at_x, count_y).values()))
    for copy in inputs:
        copy.wait()

    def side(whose):
        return pl.ds(pl.multiple_of(whose * half, half), half)

    swap = remote(mine.at[:, side(1 - core)], other, pair_send, pair_recv, sibling)
    swap.start()
    swap.wait_recv()
    here, there = mine[:, side(core)].astype(jnp.float32), other[...].astype(jnp.float32)
    even = jnp.where(core == 0, here, there)
    odd = jnp.where(core == 0, there, here)
    for kind in (0, 1):
        part = slice(kind * HEAD, (kind + 1) * HEAD)
        tile = jnp.transpose(jnp.concatenate([even[part], odd[part]], axis=0))
        column = pl.multiple_of(kind * width + chip * PAIR, PAIR)
        features[side(core), pl.ds(column, PAIR)] = tile.astype(jnp.bfloat16)

    def along_z(kind, way, hop, part, moved):
        tile = wrap(chip + (-moved if way == 0 else moved), chips)
        start = pl.multiple_of(kind * width + tile * PAIR, PAIR)
        first = pl.multiple_of(core * half + part * (half // 2), half // 2)
        spot = features.at[pl.ds(first, half // 2), pl.ds(start, PAIR)]
        at = (kind, way, hop - 1, part)
        return remote(spot, spot, z_send.at[at], z_recv.at[at], right if way == 0 else left)

    def sent(kind, way, hop, part):
        return along_z(kind, way, hop, part, hop - 1)

    def landed(kind, way, hop, part):
        return along_z(kind, way, hop, part, hop)

    def shared(kind, whose):
        spot = features.at[side(whose), pl.ds(kind * width, width)]
        return remote(spot, spot, share_send.at[kind], share_recv.at[kind], sibling)

    z_messages = ring_messages(chips, 2)

    def advance(kind, hop):
        for _, way, part in [message for message in z_messages if message[0] == hop]:
            landed(kind, way, hop, part).wait_recv()
            if (hop + 1, way, part) in z_messages:
                sent(kind, way, hop + 1, part).start()
        if hop == hops:
            shared(kind, core).start()

    def begin(kind):
        for _, way, part in [message for message in z_messages if message[0] == 1]:
            sent(kind, way, 1, part).start()

    begin(0)
    for hop in range(1, hops + 1):
        advance(0, hop)
        if hop == hops - 2:
            begin(1)
        if hop > hops - 2:
            advance(1, hop - hops + 2)
    for copy in fill:
        copy.wait()
    shared(0, 1 - core).wait_recv()

    lane = lax.broadcasted_iota(jnp.int32, (BLK, PAIR), 1)
    blocks = [slice(start, start + BLK) for start in range(0, rows, BLK)]
    against = (((1,), (1,)), ((), ()))
    for block in blocks:
        product = lax.dot_general(
            features[block, :width], weights[...], against, preferred_element_type=jnp.float32
        )
        kv_ref[at_y, block] = product[:, :PAIR].astype(jnp.bfloat16)
        qg_ref[at_x, block] = product[:, PAIR:].astype(jnp.bfloat16)
    near = neighbours(at_y, at_x, count_y)
    over_y = ring_gather(kv_ref, at_y, count_y, (near["y", 1], near["y", -1]), y_send, y_recv)
    take(over_y, 8)
    for hop in range(3, hops + 1):
        advance(1, hop)
        take(over_y, 4)
    shared(1, 1 - core).wait_recv()
    for block in blocks:
        product = lax.dot_general(
            features[block, width:], weights[PAIR:], against, preferred_element_type=jnp.float32
        )
        pair = jnp.where(lane < HEAD, qg_ref[at_x, block], product.astype(jnp.bfloat16))
        qg_ref[at_x, block] = pair
    over_x = ring_gather(qg_ref, at_x, RING_X, (near["x", 1], near["x", -1]), x_send, x_recv)
    take(over_x, 4)
    take(over_y, 6)
    take(over_x, 2)
    finish(over_y)
    finish(over_x)
    swap.wait_send()
    for kind in (0, 1):
        shared(kind, core).wait_send()
        for hop, way, part in z_messages:
            sent(kind, way, hop, part).wait_send()


def project(frames, cotangent, weights):
    cores, peers = lax.axis_size("mp"), lax.axis_size("seq")
    rows = frames.shape[0]
    dma = pltpu.SemaphoreType.DMA
    sems = dma((2, 2, cores // 4, 2))
    x_sems, y_sems = dma((RING_X // 2, 2, 2)), dma((peers // RING_X // 2, 2, 4))
    return pl.pallas_call(
        project_kernel,
        out_shape=(
            jax.ShapeDtypeStruct((rows, cores * PAIR), jnp.bfloat16),
            jax.ShapeDtypeStruct((peers // RING_X, rows, PAIR), jnp.bfloat16),
            jax.ShapeDtypeStruct((RING_X, rows, PAIR), jnp.bfloat16),
        ),
        in_specs=[ANY] * 6,
        out_specs=(VMEM, VMEM, VMEM),
        scratch_shapes=[
            pltpu.VMEM((4 * HEAD, D), jnp.bfloat16),
            pltpu.VMEM((PAIR, rows), jnp.bfloat16),
            pltpu.VMEM((PAIR, rows // 2), jnp.bfloat16),
            dma((2,)),
            dma((4,)),
            dma,
            dma,
            sems,
            sems,
            dma((2,)),
            dma((2,)),
            y_sems,
            y_sems,
            x_sems,
            x_sems,
        ],
        compiler_params=pltpu.CompilerParams(
            collective_id=0, has_side_effects=True, vmem_limit_bytes=60 * 1024 * 1024
        ),
        name="project",
    )(frames.T, cotangent.T, *weights)


def list_pairs(turn_ref, own_ref, far_ref):
    _, _, at_y, at_x, _, count_y = places()
    count = jnp.int32(0)
    spread = RING_X * ROWS

    def add(count, own, far, ok):
        own_ref[count] = jnp.clip(own, 0, spread - 1)
        far_ref[count] = jnp.clip(far, 0, count_y * ROWS - 1)
        return count + ok.astype(jnp.int32)

    for block in range(ROWS):
        for offset in range(-BAND, BAND + 1):
            own = at_x * ROWS + block + offset
            count = add(count, own, at_y * ROWS + block, (own >= 0) & (own < spread))
    first, final = at_x == 0, at_x == RING_X - 1
    crosses = (first & (at_y + 1 < count_y)) | (final & (at_y > 0))
    for ahead in range(BAND):
        for back in range(BAND - ahead):
            own = jnp.where(first, spread - 1 - back, back)
            far = jnp.where(first, (at_y + 1) * ROWS + ahead, at_y * ROWS - 1 - ahead)
            count = add(count, own, far, crosses)

    def visit(index, count):
        row, column = lax.div(index, RING_X), lax.rem(index, RING_X)
        holder, partner = at_y * RING_X + column, row * RING_X + at_x
        for slot in range(turn_ref.shape[1]):
            own = turn_ref[holder, slot, partner]
            far = turn_ref[partner, slot, holder]
            ok = (own >= 0) & (jnp.abs(own - far) > BAND)
            count = add(count, own - at_y * spread, far + (row - partner) * ROWS, ok)
        return count

    count = lax.fori_loop(0, count_y * RING_X, visit, count)
    for pad in range(UNROLL):
        own_ref[count + pad] = 0
        far_ref[count + pad] = 0
    return count


def most_pairs(turns):
    return ROWS * (2 * BAND + 1) + BAND * (BAND + 1) // 2 + turns.shape[0] * turns.shape[1] + UNROLL


def forward_kernel(turn_ref, qg_ref, kv_ref, out_ref, own_list, far_list, lhs, score, top, total, mixed):
    count = list_pairs(turn_ref, own_list, far_list)
    rounds = lax.div(count + UNROLL - 1, UNROLL)
    lane = lax.broadcasted_iota(jnp.int32, (BLK, PAIR), 1)
    blocks = qg_ref.shape[0]
    zero = jnp.zeros((BLK, PAIR), jnp.bfloat16)
    for block in range(blocks):
        lhs[block] = jnp.where(lane < HEAD, qg_ref[block], zero)
    top[...] = jnp.full_like(top, LEAST)
    total[...] = jnp.zeros_like(total)
    mixed[...] = jnp.zeros_like(mixed)

    def tiles(step):
        at = [step * UNROLL + u for u in range(UNROLL)]
        return [(tile, own_list[tile], far_list[tile]) for tile in at]

    def score_step(step, carry):
        now = tiles(step)
        products = [
            lax.dot_general(
                lhs[own], kv_ref[far], (((1,), (1,)), ((), ())), preferred_element_type=jnp.float32
            )
            for _, own, far in now
        ]
        scaled = []
        for (tile, _, _), product in zip(now, products):
            masked = product * EXP2_SCALE + jnp.where(tile < count, 0.0, -jnp.inf)
            score[tile] = masked
            scaled.append(masked)
        for (_, own, _), masked in zip(now, scaled):
            top[own] = jnp.maximum(top[own], masked)
        return carry

    lax.fori_loop(0, rounds, score_step, 0)
    for block in range(blocks):
        top[block] = jnp.broadcast_to(jnp.max(top[block], axis=1, keepdims=True), (BLK, PAIR))

    def weight_step(step, carry):
        now = tiles(step)
        weights = [jnp.exp2(score[tile] - top[own]) for tile, own, _ in now]
        sums = [
            jnp.dot(weight.astype(jnp.bfloat16), kv_ref[far], preferred_element_type=jnp.float32)
            for weight, (_, _, far) in zip(weights, now)
        ]
        for (_, own, _), weight, part in zip(now, weights, sums):
            total[own] += weight
            mixed[own] += part
        return carry

    lax.fori_loop(0, rounds, weight_step, 0)
    for device in range(RING_X):
        column = jnp.zeros((BLK, PAIR), jnp.float32)
        for block in range(ROWS):
            at = device * ROWS + block
            column = jnp.where(lane == block, top[at], column)
            column = jnp.where(lane == ROWS + block, jnp.sum(total[at], axis=1, keepdims=True), column)
        for pair in range(ROWS // 2):
            even, odd = mixed[device * ROWS + 2 * pair], mixed[device * ROWS + 2 * pair + 1]
            out_ref[device, pair * BLK : (pair + 1) * BLK] = jnp.where(
                lane < HEAD, pltpu.roll(even, HEAD, 1), odd
            )
        out_ref[device, ROWS // 2 * BLK :] = jnp.transpose(column)[: 2 * ROWS]


def attend_forward(turns, qg, kv):
    most = most_pairs(turns)
    blocks = RING_X * ROWS
    square = pltpu.VMEM((blocks, BLK, PAIR), jnp.float32)
    return pl.pallas_call(
        forward_kernel,
        out_shape=jax.ShapeDtypeStruct((RING_X, ROWS // 2 * BLK + 2 * ROWS, PAIR), jnp.float32),
        in_specs=[SMEM, VMEM, VMEM],
        out_specs=VMEM,
        scratch_shapes=[
            pltpu.SMEM((most,), jnp.int32),
            pltpu.SMEM((most,), jnp.int32),
            pltpu.VMEM((blocks, BLK, PAIR), jnp.bfloat16),
            pltpu.VMEM((most, BLK, BLK), jnp.float32),
            square,
            square,
            square,
        ],
        compiler_params=pltpu.CompilerParams(vmem_limit_bytes=LIMIT),
        cost_estimate=pl.CostEstimate(
            flops=most * 4 * BLK * BLK * PAIR, bytes_accessed=kv.size * 4, transcendentals=most * BLK * BLK
        ),
        name="attend_forward",
    )(turns, qg.reshape(-1, BLK, PAIR), kv.reshape(-1, BLK, PAIR))


def backward_kernel(
    turn_ref, qg_ref, kv_ref, stats_ref, query_ref, key_ref, own_list, far_list, rhs, query, key
):
    count = list_pairs(turn_ref, own_list, far_list)
    rounds = lax.div(count + UNROLL - 1, UNROLL)
    lane = lax.broadcasted_iota(jnp.int32, (BLK, PAIR), 1)
    zero = jnp.zeros((BLK, PAIR), jnp.bfloat16)
    for block in range(qg_ref.shape[0]):
        pair = qg_ref[block]
        rhs[block, :BLK] = jnp.where(lane < HEAD, pair, zero)
        rhs[block, BLK:] = jnp.where(lane < HEAD, zero, pair)
    query[...] = jnp.zeros_like(query)
    key[...] = jnp.zeros_like(key)

    def step_of(step, carry):
        now = []
        for u in range(UNROLL):
            tile = step * UNROLL + u
            now.append((tile, own_list[tile], far_list[tile]))
        both = [
            lax.dot_general(
                kv_ref[far], rhs[own], (((1,), (1,)), ((), ())), preferred_element_type=jnp.float32
            )
            for _, own, far in now
        ]
        factors = []
        for (tile, own, _), product in zip(now, both):
            device, block = lax.div(own, ROWS), lax.rem(own, ROWS)
            top, inverse, drift = (
                stats_ref[device, pl.ds(kind * ROWS + block, 1), :] for kind in range(3)
            )
            masked = product[:, :BLK] * EXP2_SCALE + jnp.where(tile < count, 0.0, -jnp.inf)
            prob = jnp.exp2(masked - top) * inverse
            slope = prob * (product[:, BLK:] - drift)
            factors.append((slope.astype(jnp.bfloat16), prob.astype(jnp.bfloat16)))
        to_keys = [
            jnp.dot(jnp.concatenate(factor, axis=1), rhs[own], preferred_element_type=jnp.float32)
            for factor, (_, own, _) in zip(factors, now)
        ]
        to_queries = [
            lax.dot_general(
                slope, kv_ref[far], (((0,), (0,)), ((), ())), preferred_element_type=jnp.float32
            )
            for (slope, _), (_, _, far) in zip(factors, now)
        ]
        for (_, own, far), to_key, to_query in zip(now, to_keys, to_queries):
            key[far] += to_key
            query[own] += to_query
        return carry

    lax.fori_loop(0, rounds, step_of, 0)
    for block in range(key.shape[0]):
        key_ref[block] = jnp.where(lane < HEAD, key[block] * SCALE, key[block]).astype(jnp.bfloat16)
    for device in range(RING_X):
        for pair in range(ROWS // 2):
            even, odd = query[device * ROWS + 2 * pair], query[device * ROWS + 2 * pair + 1]
            query_ref[device, pair * BLK : (pair + 1) * BLK] = (
                jnp.where(lane < HEAD, even, pltpu.roll(odd, HEAD, 1)) * SCALE
            )


def attend_backward(turns, qg, kv, stats):
    most = most_pairs(turns)
    blocks, keys = RING_X * ROWS, kv.shape[0] * ROWS
    return pl.pallas_call(
        backward_kernel,
        out_shape=(
            jax.ShapeDtypeStruct((RING_X, ROWS // 2 * BLK, PAIR), jnp.float32),
            jax.ShapeDtypeStruct((keys, BLK, PAIR), jnp.bfloat16),
        ),
        in_specs=[SMEM, VMEM, VMEM, VMEM],
        out_specs=(VMEM, VMEM),
        scratch_shapes=[
            pltpu.SMEM((most,), jnp.int32),
            pltpu.SMEM((most,), jnp.int32),
            pltpu.VMEM((blocks, 2 * BLK, PAIR), jnp.bfloat16),
            pltpu.VMEM((blocks, BLK, PAIR), jnp.float32),
            pltpu.VMEM((keys, BLK, PAIR), jnp.float32),
        ],
        compiler_params=pltpu.CompilerParams(vmem_limit_bytes=LIMIT),
        cost_estimate=pl.CostEstimate(
            flops=most * 10 * BLK * BLK * PAIR, bytes_accessed=kv.size * 4, transcendentals=most * BLK * BLK
        ),
        name="attend_backward",
    )(turns, qg.reshape(-1, BLK, PAIR), kv.reshape(-1, BLK, PAIR), stats)


def combine_kernel(parts, qg_ref, context, stats_ref, got, send, recv, s_send, s_recv):
    _, _, at_y, at_x, _, count_y = places()
    along_x, _ = seq_partners(at_y, at_x, count_y)
    greet(along_x)
    steps = range(len(along_x))

    def give(step):
        target = lax.rem(at_x + step + 1, RING_X)
        return remote(parts.at[target], got.at[step], send.at[step], recv.at[step], along_x[step])

    def tell(step, slot):
        part = stats_ref.at[slot]
        return remote(part, part, s_send.at[step], s_recv.at[step], along_x[step])

    for step in steps:
        give(step).start()
    for step in steps:
        give(step).wait_recv()
    packed = ROWS // 2 * BLK
    lane = lax.broadcasted_iota(jnp.int32, (BLK, PAIR), 1)

    def values(start, count):
        rows = slice(start, start + count)
        return [parts[at_x, rows]] + [got[step, rows] for step in steps]

    tops, totals = values(packed, ROWS), values(packed + ROWS, ROWS)
    top = functools.reduce(jnp.maximum, tops)
    factors = [jnp.exp2(part - top) for part in tops]
    inverse = 1.0 / sum(factor * part for factor, part in zip(factors, totals))
    shares = [factor * inverse for factor in factors]
    blank = jnp.zeros((BLK - ROWS * RING_X, PAIR), jnp.float32)
    columns = jnp.transpose(jnp.concatenate(shares + [blank], axis=0))
    drifts = jnp.zeros((BLK, PAIR), jnp.float32)
    for block in range(ROWS):
        output = jnp.zeros((BLK, PAIR), jnp.float32)
        for index, part in enumerate(values(block // 2 * BLK, BLK)):
            at = index * ROWS + block
            output += (part if block % 2 else pltpu.roll(part, HEAD, 1)) * columns[:, at : at + 1]
        output = jnp.where(lane < HEAD, 0.0, output)
        rows = slice(block * BLK, (block + 1) * BLK)
        context[rows] = output.astype(jnp.bfloat16)
        drift = jnp.sum(qg_ref[at_x, rows].astype(jnp.float32) * output, axis=1, keepdims=True)
        drifts = jnp.where(lane == block, drift, drifts)
    drift_rows = jnp.transpose(drifts)[: 2 * ROWS]
    stats_ref[at_x] = jnp.concatenate([top, inverse, drift_rows], axis=0)
    for step in steps:
        tell(step, at_x).start()
    for step in steps:
        tell(step, wrap(at_x - step - 1, RING_X)).wait_recv()
    for step in steps:
        give(step).wait_send()
        tell(step, at_x).wait_send()


def combine(parts, qg):
    sems = pltpu.SemaphoreType.DMA((RING_X - 1,))
    return pl.pallas_call(
        combine_kernel,
        out_shape=(
            jax.ShapeDtypeStruct((ROWS * BLK, PAIR), jnp.bfloat16),
            jax.ShapeDtypeStruct((RING_X, 4 * ROWS, PAIR), jnp.float32),
        ),
        in_specs=[VMEM, VMEM],
        out_specs=(VMEM, VMEM),
        scratch_shapes=[pltpu.VMEM((RING_X - 1,) + parts.shape[1:], jnp.float32), sems, sems, sems, sems],
        compiler_params=pltpu.CompilerParams(
            collective_id=1, has_side_effects=True, vmem_limit_bytes=LIMIT
        ),
        name="combine",
    )(parts, qg)


def sum_over_seq(parts, sums_refs, x_sum, arrived, leaving, from_y, piece, totals, *sems):
    _, _, at_y, at_x, _, count_y = places()
    near = neighbours(at_y, at_x, count_y)
    around = (near["x", 1], near["x", -1])
    _, along_y = seq_partners(at_y, at_x, count_y)
    ys = range(len(along_y))

    def columns(index):
        return pl.ds(pl.multiple_of(index * PAIR, PAIR), PAIR)

    def in_y(step):
        source = x_sum.at[:, columns(lax.rem(at_y + step + 1, count_y))]
        return remote(source, from_y.at[step], sems[2].at[step], sems[3].at[step], along_y[step])

    def out_y(step, owner):
        target = totals.at[at_x, :, columns(owner)]
        return remote(piece, target, sems[4].at[step], sems[5].at[step], along_y[step])

    over_x = ring_sum(parts, x_sum, arrived, leaving, at_x, RING_X, around, sems[0], sems[1])
    take(over_x, 2)
    yield
    take(over_x, 4)
    yield
    take(over_x, 1)
    for step in ys:
        in_y(step).start()
    yield
    total = x_sum[:, columns(at_y)].astype(jnp.float32)
    for step in ys:
        in_y(step).wait_recv()
        total += from_y[step].astype(jnp.float32)
    piece[...] = total.astype(jnp.bfloat16)
    for step in ys:
        out_y(step, at_y).start()
    totals[at_x, :, columns(at_y)] = piece[...]
    yield
    for step in ys:
        out_y(step, wrap(at_y - step - 1, count_y)).wait_recv()
    back = ring_gather(totals, at_x, RING_X, around, sems[6], sems[7])
    take(back, 4)
    yield
    finish(back)
    count = RING_X // len(sums_refs)
    for index in range(RING_X):
        height = totals.shape[1]
        rows = pl.ds(index % count * height, height)
        sums_refs[index // count][rows] = totals[index].astype(jnp.float32)
    finish(over_x)
    for step in ys:
        in_y(step).wait_send()
        out_y(step, at_y).wait_send()


def gradient_kernel(
    query_parts,
    key_parts,
    context,
    features_ref,
    key_w,
    value_w,
    query_w,
    out_w,
    attended,
    grad_frames,
    sums_ref,
    features,
    weights,
    filled,
    loaded,
    joint,
    lhs,
    got,
    key_sum,
    arrived,
    leaving,
    x_send,
    x_recv,
    y_send,
    y_recv,
    *refs,
):
    chip, core, at_y, at_x, chips, count_y = places()
    along_x, along_y = seq_partners(at_y, at_x, count_y)
    near = neighbours(at_y, at_x, count_y)
    fill = stack_rows((key_w, value_w, query_w, out_w), weights, filled)
    load = pltpu.make_async_copy(features_ref, features, loaded)
    for copy in fill + [load]:
        copy.start()
    greet(along_x + along_y + mp_partners(chip, core, chips))
    steps = range(len(along_x))

    def give(step):
        target = lax.rem(at_x + step + 1, RING_X)
        return remote(query_parts.at[target], got.at[step], x_send.at[step], x_recv.at[step], along_x[step])

    over_y = ring_sum(
        key_parts, key_sum, arrived, leaving, at_y, count_y, (near["y", 1], near["y", -1]), y_send, y_recv
    )
    take(over_y, 4)
    for step in steps:
        give(step).start()
    for copy in fill:
        copy.wait()

    def columns(tile):
        return pl.ds(pl.multiple_of(tile * PAIR, PAIR), PAIR)

    def output_part(tile, half):
        return jnp.dot(
            half_rows_of(context, half), weights[PAIR:, columns(tile)], preferred_element_type=jnp.float32
        )

    def input_part(tile, half):
        return jnp.dot(half_rows_of(lhs, half), weights[:, columns(tile)], preferred_element_type=jnp.float32)

    seq_refs = len(seq_scratch(count_y))
    mp_refs = (len(refs) - 2 * seq_refs) // 2
    early, late = refs[:seq_refs], refs[seq_refs : 2 * seq_refs]
    outputs = sum_over_mp(output_part, attended, *refs[2 * seq_refs : 2 * seq_refs + mp_refs])
    inputs = sum_over_mp(input_part, grad_frames, *refs[2 * seq_refs + mp_refs :])
    sums = [sums_ref.at[pl.ds(index * HEAD, HEAD)] for index in range(4)]
    over_seq = [
        sum_over_seq(early[0], sums[2:], *early[1:]),
        sum_over_seq(late[0], sums[:2], *late[1:]),
    ]
    width = D
    along_rows = (((0,), (0,)), ((), ()))

    def store_product(target, first, values, at, lower, upper):
        product = lax.dot_general(
            values, features[:, at * width : (at + 1) * width], along_rows, preferred_element_type=jnp.float32
        )
        height = target.shape[1]
        for index in range((upper - lower) // height):
            start = lower + index * height
            target[first + index] = product[start : start + height].astype(jnp.bfloat16)

    lane = lax.broadcasted_iota(jnp.int32, (BLK, PAIR), 1)
    for turn in range(chips):
        take(outputs, 2)
        take(over_y, 3)
        if turn == chips // 2:
            for step in steps:
                give(step).wait_recv()
            for pair in range(ROWS // 2):
                part = slice(pair * BLK, (pair + 1) * BLK)
                total = query_parts[at_x, part]
                for step in steps:
                    total += got[step, part]
                for block, value in ((2 * pair, total), (2 * pair + 1, pltpu.roll(total, HEAD, 1))):
                    rows = slice(block * BLK, (block + 1) * BLK)
                    value = value.astype(jnp.bfloat16)
                    joint[rows] = jnp.where(lane < HEAD, value, context[rows])
                    lhs[rows, PAIR:] = jnp.where(lane < HEAD, value, jnp.zeros_like(value))
            load.wait()
            store_product(early[0], 0, joint[...], 0, 0, HEAD)
            store_product(early[0], RING_X // 2, joint[...], 1, HEAD, PAIR)
            take(over_seq[0], 1)
    take(over_seq[0], 1)
    take(over_y, 1)
    lhs[:, :PAIR] = key_sum[...]
    store_product(late[0], 0, key_sum[...], 0, 0, PAIR)
    take(over_seq[1], 1)
    take(over_seq[0], 1)
    take(inputs, chips)
    take(over_seq[1], 1)
    take(over_seq[0], 1)
    take(inputs, chips)
    take(over_seq[1], 1)
    take(over_seq[0], 1)
    take(outputs, 1)
    take(over_seq[1], 2)
    take(inputs, 1)
    finish(over_seq[0])
    finish(over_seq[1])
    finish(outputs)
    finish(inputs)
    finish(over_y)
    for step in steps:
        give(step).wait_send()


def seq_scratch(count_y):
    dma = pltpu.SemaphoreType.DMA
    x_ring, y_sems = dma((RING_X // 2, 2, 2)), dma((count_y - 1,))
    height = 2 * HEAD // RING_X
    stack = pltpu.VMEM((RING_X, height, D), jnp.bfloat16)
    return [
        stack,
        pltpu.VMEM((height, D), jnp.bfloat16),
        pltpu.VMEM((RING_X // 2, 2, height, D), jnp.bfloat16),
        pltpu.VMEM((RING_X // 2 - 1, 2, height, D), jnp.bfloat16),
        pltpu.VMEM((count_y - 1, height, PAIR), jnp.bfloat16),
        pltpu.VMEM((height, PAIR), jnp.bfloat16),
        stack,
        x_ring,
        x_ring,
        y_sems,
        y_sems,
        y_sems,
        y_sems,
        x_ring,
        x_ring,
    ]


def sum_gradients(query_parts, key_parts, context, features, weights):
    peers = lax.axis_size("seq")
    rows = context.shape[0]
    count_y = peers // RING_X
    dma = pltpu.SemaphoreType.DMA
    x_sems, y_ring = dma((RING_X - 1,)), dma((count_y // 2, 2, 4))
    out = jax.ShapeDtypeStruct((HEAD, rows), jnp.bfloat16)

    def rounded(*shape):
        return pltpu.VMEM(shape, jnp.bfloat16)

    return pl.pallas_call(
        gradient_kernel,
        out_shape=(out, out, jax.ShapeDtypeStruct((RING_X * HEAD, D), jnp.float32)),
        in_specs=[VMEM] * 3 + [ANY] * 5,
        out_specs=(VMEM, VMEM, VMEM),
        scratch_shapes=[
            rounded(*features.shape),
            rounded(RING_X * HEAD, D),
            dma((4,)),
            dma,
            rounded(rows, PAIR),
            rounded(rows, 2 * PAIR),
            pltpu.VMEM((RING_X - 1,) + query_parts.shape[1:], jnp.float32),
            rounded(rows, PAIR),
            rounded(count_y // 2, 2, rows, PAIR),
            rounded(count_y // 2 - 1, 2, rows, PAIR),
            x_sems,
            x_sems,
            y_ring,
            y_ring,
        ]
        + seq_scratch(count_y)
        + seq_scratch(count_y)
        + sum_scratch(rows)
        + sum_scratch(rows),
        compiler_params=pltpu.CompilerParams(
            collective_id=2, has_side_effects=True, vmem_limit_bytes=LIMIT
        ),
        name="sum_gradients",
    )(query_parts, key_parts.reshape(count_y, rows, PAIR), context, features, *weights)


def on_device(frames, cotangent, query_weight, key_weight, value_weight, out_weight, turn_blocks):
    turns = jnp.transpose(turn_blocks, (0, 2, 1))
    weights = (key_weight, value_weight, query_weight, out_weight)
    features, kv, qg = project(frames, cotangent, weights)
    context, stats = combine(attend_forward(turns, qg, kv), qg)
    query_parts, key_parts = attend_backward(turns, qg, kv, stats)
    attended, grad_frames, sums = sum_gradients(query_parts, key_parts, context, features, weights)
    grad_key, grad_value, grad_query, grad_out = (
        sums[index * HEAD : (index + 1) * HEAD] for index in range(4)
    )
    return attended.T, grad_frames.T, grad_query, grad_key, grad_value, grad_out


def solution(mesh):
    return jax.shard_map(
        on_device,
        mesh=mesh,
        in_specs=(
            P("seq", "mp"),
            P("seq", "mp"),
            P("mp", None),
            P("mp", None),
            P("mp", None),
            P("mp", None),
            P(),
        ),
        out_specs=(
            P("seq", "mp"),
            P("seq", "mp"),
            P("mp", None),
            P("mp", None),
            P("mp", None),
            P("mp", None),
        ),
        check_vma=False,
    )
```

```python
import functools
import math

import jax
import jax.numpy as jnp
from jax import lax
from jax.experimental import pallas as pl
from jax.experimental.pallas import tpu as pltpu
from jax.sharding import PartitionSpec as P

D = 1024
HEADS = 16
BLK = 128
BAND = 2
RING_X = 4
ROWS = 4
LEAST = -3e38
HEAD = D // HEADS
PAIR = 2 * HEAD
UNROLL = 8
SCALE = 1.0 / math.sqrt(HEAD)
EXP2_SCALE = SCALE * math.log2(math.e)
MESH = pl.DeviceIdType.MESH
VMEM = pl.BlockSpec(memory_space=pltpu.VMEM)
SMEM = pl.BlockSpec(memory_space=pltpu.SMEM)
ANY = pl.BlockSpec(memory_space=pl.ANY)
LIMIT = 48 * 1024 * 1024


def wrap(index, count):
    return lax.rem(index + count, count)


def greet(devices):
    barrier = pltpu.get_barrier_semaphore()
    for device in devices:
        pl.semaphore_signal(barrier, inc=1, device_id=device, device_id_type=MESH)
    pl.semaphore_wait(barrier, len(devices))


def remote(source, target, send, recv, device):
    return pltpu.make_async_remote_copy(
        source, target, send, recv, device_id=device, device_id_type=MESH
    )


def take(process, count):
    for _ in range(count):
        next(process, None)


def finish(process):
    for _ in process:
        pass


def stack_rows(refs, whole, sems):
    copies = []
    for index, ref in enumerate(refs):
        target = whole.at[pl.ds(index * HEAD, HEAD)]
        copies.append(pltpu.make_async_copy(ref, target, sems.at[index]))
    return copies


def places():
    me_mp, me = lax.axis_index("mp"), lax.axis_index("seq")
    chips, count_y = lax.axis_size("mp") // 2, lax.axis_size("seq") // RING_X
    return lax.div(me_mp, 2), lax.rem(me_mp, 2), lax.div(me, RING_X), lax.rem(me, RING_X), chips, count_y


def neighbours(at_y, at_x, count_y):
    return {
        ("x", 1): {"seq": at_y * RING_X + wrap(at_x + 1, RING_X)},
        ("x", -1): {"seq": at_y * RING_X + wrap(at_x - 1, RING_X)},
        ("y", 1): {"seq": wrap(at_y + 1, count_y) * RING_X + at_x},
        ("y", -1): {"seq": wrap(at_y - 1, count_y) * RING_X + at_x},
    }


def ring_messages(count, parts):
    return [
        (hop, way, part)
        for hop in range(1, count // 2 + 1)
        for part in range(parts)
        for way in (0, 1)
        if hop < count // 2 or part // (parts // 2) == way
    ]


def ring_gather(store, at, count, devices, send, recv):
    parts = send.shape[2]
    part_rows = store.shape[1] // parts

    def copy_of(hop, way, part, arriving):
        moved = hop if arriving else hop - 1
        slot = wrap(at + (-moved if way == 0 else moved), count)
        spot = store.at[slot, pl.ds(part * part_rows, part_rows)]
        index = (hop - 1, way, part)
        return remote(spot, spot, send.at[index], recv.at[index], devices[way])

    messages = ring_messages(count, parts)
    for hop, way, part in messages:
        if hop > 1:
            copy_of(hop - 1, way, part, True).wait_recv()
        copy_of(hop, way, part, False).start()
        yield
    for hop, way, part in messages:
        if (hop + 1, way, part) not in messages:
            copy_of(hop, way, part, True).wait_recv()
    yield
    for hop, way, part in messages:
        copy_of(hop, way, part, False).wait_send()


def ring_sum(values, out, arrived, leaving, at, count, devices, send, recv):
    parts = send.shape[2]
    part_rows = values.shape[1] // parts
    last = count // 2

    def rows(part):
        return pl.ds(part * part_rows, part_rows)

    def copy_of(hop, way, part):
        index = (hop - 1, way, part)
        if hop == 1:
            source = values.at[wrap(at + last, count), rows(part)]
        else:
            source = leaving.at[hop - 2, way, rows(part)]
        target = arrived.at[hop - 1, way, rows(part)]
        return remote(source, target, send.at[index], recv.at[index], devices[way])

    messages = [
        (hop, way, part)
        for hop in range(1, last + 1)
        for part in range(parts)
        for way in (0, 1)
        if hop > 1 or part // (parts // 2) == way
    ]

    def summed(hop, way, part):
        slot = wrap(at + (last + 1 - hop if way == 0 else hop - 1 - last), count)
        value = values[slot, rows(part)].astype(jnp.float32)
        if (hop - 1, way, part) in messages:
            copy_of(hop - 1, way, part).wait_recv()
            value += arrived[hop - 2, way, rows(part)].astype(jnp.float32)
        return value

    for hop, way, part in messages:
        if hop > 1:
            leaving[hop - 2, way, rows(part)] = summed(hop, way, part).astype(jnp.bfloat16)
        copy_of(hop, way, part).start()
        yield
    for part in range(parts):
        value = values[at, rows(part)].astype(jnp.float32)
        for way in (0, 1):
            copy_of(last, way, part).wait_recv()
            value += arrived[last - 1, way, rows(part)].astype(jnp.float32)
        out[rows(part)] = value.astype(jnp.bfloat16)
    yield
    for message in messages:
        copy_of(*message).wait_send()


def sum_over_mp(partial, out_ref, mine, gift, theirs, chip_sum, tiles, done, pair_send, pair_recv, z_send, z_recv, swap_send, swap_recv):
    chip, core, _, _, chips, _ = places()
    sibling = {"mp": 2 * chip + 1 - core}
    half = mine.shape[1]

    def give(step):
        return remote(gift.at[step], theirs.at[step], pair_send.at[step], pair_recv.at[step], sibling)

    def post(step):
        target = {"mp": 2 * lax.rem(chip + step, chips) + core}
        return remote(chip_sum.at[step], tiles.at[step], z_send.at[step - 1], z_recv.at[step - 1], target)

    order = sorted(range(1, chips), key=lambda step: -min(step, chips - step)) + [0]
    for step in order:
        tile = lax.rem(chip + step, chips)
        product = partial(tile)
        gift[step] = product[:half].astype(jnp.bfloat16)
        give(step).start()
        mine[step] = product[half:]
        yield
    for step in order:
        give(step).wait_recv()
        mine[step] += theirs[step].astype(jnp.float32)
        if step:
            chip_sum[step] = mine[step].astype(jnp.bfloat16)
            post(step).start()
        yield
    total = mine[0]
    for step in reversed(order[:-1]):
        post(step).wait_recv()
        total += tiles[step].astype(jnp.float32)
    done[...] = jnp.transpose(total).astype(jnp.bfloat16)
    columns = pl.ds(pl.multiple_of(core * half, half), half)
    other_columns = pl.ds(pl.multiple_of((1 - core) * half, half), half)
    own_rows = pl.ds(pl.multiple_of(core * HEAD, HEAD), HEAD)
    swap = remote(
        done.at[pl.ds(pl.multiple_of((1 - core) * HEAD, HEAD), HEAD)],
        out_ref.at[:, columns],
        swap_send,
        swap_recv,
        sibling,
    )
    swap.start()
    out_ref[:, columns] = done[own_rows]
    yield
    remote(done.at[own_rows], out_ref.at[:, other_columns], swap_send, swap_recv, sibling).wait_recv()
    swap.wait_send()
    for step in order:
        give(step).wait_send()
        if step:
            post(step).wait_send()


def sum_scratch(rows):
    chips = lax.axis_size("mp") // 2
    half = rows // 2
    dma = pltpu.SemaphoreType.DMA
    some = pltpu.VMEM((chips, half, PAIR), jnp.bfloat16)
    return [
        pltpu.VMEM((chips, half, PAIR), jnp.float32),
        some,
        some,
        some,
        some,
        pltpu.VMEM((PAIR, half), jnp.bfloat16),
        dma((chips,)),
        dma((chips,)),
        dma((chips - 1,)),
        dma((chips - 1,)),
        dma,
        dma,
    ]


def mp_partners(chip, core, chips):
    return [{"mp": 2 * chip + 1 - core}] + [
        {"mp": 2 * lax.rem(chip + step, chips) + core} for step in range(1, chips)
    ]


def seq_partners(at_y, at_x, count_y):
    along_x = [{"seq": at_y * RING_X + lax.rem(at_x + step, RING_X)} for step in range(1, RING_X)]
    along_y = [{"seq": lax.rem(at_y + step, count_y) * RING_X + at_x} for step in range(1, count_y)]
    return along_x, along_y


def half_rows_of(ref, half):
    rows = ref.shape[0] // 2
    return ref[pl.ds(pl.multiple_of(half * rows, rows), rows)]


def project_kernel(
    frames_ref,
    grad_ref,
    key_w,
    value_w,
    query_w,
    out_w,
    features,
    kv_ref,
    qg_ref,
    weights,
    loaded,
    filled,
    z_send,
    z_recv,
    share_send,
    share_recv,
    y_send,
    y_recv,
    x_send,
    x_recv,
):
    chip, core, at_y, at_x, chips, count_y = places()
    hops = chips // 2
    rows = features.shape[-1]
    half = rows // 2
    sibling = {"mp": 2 * chip + 1 - core}
    right = {"mp": 2 * wrap(chip + 1, chips) + core}
    left = {"mp": 2 * wrap(chip - 1, chips) + core}
    inputs = [
        pltpu.make_async_copy(ref, features.at[kind, chip, core], loaded.at[kind])
        for kind, ref in enumerate((frames_ref, grad_ref))
    ]
    fill = stack_rows((key_w, value_w, query_w, out_w), weights, filled)
    for copy in inputs + fill:
        copy.start()
    greet([sibling, right, left] + list(neighbours(at_y, at_x, count_y).values()))
    for copy in inputs:
        copy.wait()

    def along_z(kind, way, hop, part, moved):
        tile = wrap(chip + (-moved if way == 0 else moved), chips)
        spot = features.at[kind, tile, core, :, pl.ds(part * half, half)]
        at = (kind, way, hop - 1, part)
        return remote(spot, spot, z_send.at[at], z_recv.at[at], right if way == 0 else left)

    def sent(kind, way, hop, part):
        return along_z(kind, way, hop, part, hop - 1)

    def landed(kind, way, hop, part):
        return along_z(kind, way, hop, part, hop)

    def shared(kind, whose):
        spot = features.at[kind, :, whose]
        return remote(spot, spot, share_send.at[kind], share_recv.at[kind], sibling)

    z_messages = ring_messages(chips, 2)

    def advance(kind, hop):
        for _, way, part in [message for message in z_messages if message[0] == hop]:
            landed(kind, way, hop, part).wait_recv()
            if (hop + 1, way, part) in z_messages:
                sent(kind, way, hop + 1, part).start()
        if hop == hops:
            shared(kind, core).start()

    def begin(kind):
        for _, way, part in [message for message in z_messages if message[0] == 1]:
            sent(kind, way, 1, part).start()

    begin(0)
    for hop in range(1, hops + 1):
        advance(0, hop)
        if hop == hops - 2:
            begin(1)
        if hop > hops - 2:
            advance(1, hop - hops + 2)
    for copy in fill:
        copy.wait()
    shared(0, 1 - core).wait_recv()

    def products(rows_of_weights, kind):
        whole = features[kind].reshape(chips * PAIR, rows)
        product = jnp.dot(weights[rows_of_weights], whole, preferred_element_type=jnp.float32)
        return jnp.transpose(product).astype(jnp.bfloat16)

    joined = products(slice(None), 0)
    kv_ref[at_y] = joined[:, :PAIR]
    queries = joined[:, PAIR:]
    near = neighbours(at_y, at_x, count_y)
    over_y = ring_gather(kv_ref, at_y, count_y, (near["y", 1], near["y", -1]), y_send, y_recv)
    take(over_y, 8)
    for hop in range(3, hops + 1):
        advance(1, hop)
        take(over_y, 4)
    shared(1, 1 - core).wait_recv()
    lane = lax.broadcasted_iota(jnp.int32, queries.shape, 1)
    qg_ref[at_x] = jnp.where(lane < HEAD, queries, products(slice(PAIR, None), 1))
    over_x = ring_gather(qg_ref, at_x, RING_X, (near["x", 1], near["x", -1]), x_send, x_recv)
    take(over_x, 4)
    take(over_y, 6)
    take(over_x, 2)
    finish(over_y)
    finish(over_x)
    for kind in (0, 1):
        shared(kind, core).wait_send()
        for hop, way, part in z_messages:
            sent(kind, way, hop, part).wait_send()


def project(frames, cotangent, weights):
    cores, peers = lax.axis_size("mp"), lax.axis_size("seq")
    rows = frames.shape[0]
    dma = pltpu.SemaphoreType.DMA
    sems = dma((2, 2, cores // 4, 2))
    x_sems, y_sems = dma((RING_X // 2, 2, 2)), dma((peers // RING_X // 2, 2, 4))
    return pl.pallas_call(
        project_kernel,
        out_shape=(
            jax.ShapeDtypeStruct((2, cores // 2, 2, HEAD, rows), jnp.bfloat16),
            jax.ShapeDtypeStruct((peers // RING_X, rows, PAIR), jnp.bfloat16),
            jax.ShapeDtypeStruct((RING_X, rows, PAIR), jnp.bfloat16),
        ),
        in_specs=[ANY] * 6,
        out_specs=(VMEM, VMEM, VMEM),
        scratch_shapes=[
            pltpu.VMEM((4 * HEAD, D), jnp.bfloat16),
            dma((2,)),
            dma((4,)),
            sems,
            sems,
            dma((2,)),
            dma((2,)),
            y_sems,
            y_sems,
            x_sems,
            x_sems,
        ],
        compiler_params=pltpu.CompilerParams(
            collective_id=0, has_side_effects=True, vmem_limit_bytes=60 * 1024 * 1024
        ),
        name="project",
    )(frames.T, cotangent.T, *weights)


def list_pairs(turn_ref, own_ref, far_ref):
    _, _, at_y, at_x, _, count_y = places()
    count = jnp.int32(0)
    spread = RING_X * ROWS

    def add(count, own, far, ok):
        own_ref[count] = jnp.clip(own, 0, spread - 1)
        far_ref[count] = jnp.clip(far, 0, count_y * ROWS - 1)
        return count + ok.astype(jnp.int32)

    for block in range(ROWS):
        for offset in range(-BAND, BAND + 1):
            own = at_x * ROWS + block + offset
            count = add(count, own, at_y * ROWS + block, (own >= 0) & (own < spread))
    first, final = at_x == 0, at_x == RING_X - 1
    crosses = (first & (at_y + 1 < count_y)) | (final & (at_y > 0))
    for ahead in range(BAND):
        for back in range(BAND - ahead):
            own = jnp.where(first, spread - 1 - back, back)
            far = jnp.where(first, (at_y + 1) * ROWS + ahead, at_y * ROWS - 1 - ahead)
            count = add(count, own, far, crosses)

    def visit(index, count):
        row, column = lax.div(index, RING_X), lax.rem(index, RING_X)
        holder, partner = at_y * RING_X + column, row * RING_X + at_x
        for slot in range(turn_ref.shape[1]):
            own = turn_ref[holder, slot, partner]
            far = turn_ref[partner, slot, holder]
            ok = (own >= 0) & (jnp.abs(own - far) > BAND)
            count = add(count, own - at_y * spread, far + (row - partner) * ROWS, ok)
        return count

    count = lax.fori_loop(0, count_y * RING_X, visit, count)
    for pad in range(UNROLL):
        own_ref[count + pad] = 0
        far_ref[count + pad] = 0
    return count


def most_pairs(turns):
    return ROWS * (2 * BAND + 1) + BAND * (BAND + 1) // 2 + turns.shape[0] * turns.shape[1] + UNROLL


def forward_kernel(turn_ref, qg_ref, kv_ref, out_ref, table_ref, own_list, far_list, lhs, score, top, total, mixed):
    count = list_pairs(turn_ref, own_list, far_list)
    rounds = lax.div(count + UNROLL - 1, UNROLL)
    lane = lax.broadcasted_iota(jnp.int32, (BLK, PAIR), 1)
    blocks = qg_ref.shape[0]
    zero = jnp.zeros((BLK, PAIR), jnp.bfloat16)
    for block in range(blocks):
        lhs[block] = jnp.where(lane < HEAD, qg_ref[block], zero)
    top[...] = jnp.full_like(top, LEAST)
    total[...] = jnp.zeros_like(total)
    mixed[...] = jnp.zeros_like(mixed)

    def tiles(step):
        at = [step * UNROLL + u for u in range(UNROLL)]
        return [(tile, own_list[tile], far_list[tile]) for tile in at]

    def score_step(step, carry):
        now = tiles(step)
        products = [
            lax.dot_general(
                lhs[own], kv_ref[far], (((1,), (1,)), ((), ())), preferred_element_type=jnp.float32
            )
            for _, own, far in now
        ]
        scaled = []
        for (tile, _, _), product in zip(now, products):
            masked = product * EXP2_SCALE + jnp.where(tile < count, 0.0, -jnp.inf)
            score[tile] = masked
            scaled.append(masked)
        for (_, own, _), masked in zip(now, scaled):
            top[own] = jnp.maximum(top[own], masked)
        return carry

    lax.fori_loop(0, rounds, score_step, 0)
    for block in range(blocks):
        top[block] = jnp.broadcast_to(jnp.max(top[block], axis=1, keepdims=True), (BLK, PAIR))

    def weight_step(step, carry):
        now = tiles(step)
        weights = [jnp.exp2(score[tile] - top[own]) for tile, own, _ in now]
        sums = [
            jnp.dot(weight.astype(jnp.bfloat16), kv_ref[far], preferred_element_type=jnp.float32)
            for weight, (_, _, far) in zip(weights, now)
        ]
        for (_, own, _), weight, part in zip(now, weights, sums):
            total[own] += weight
            mixed[own] += part
        return carry

    lax.fori_loop(0, rounds, weight_step, 0)
    for device in range(RING_X):
        column = jnp.zeros((BLK, PAIR), jnp.float32)
        for block in range(ROWS):
            at = device * ROWS + block
            column = jnp.where(lane == block, top[at], column)
            column = jnp.where(lane == ROWS + block, jnp.sum(total[at], axis=1, keepdims=True), column)
        for pair in range(ROWS // 2):
            even, odd = mixed[device * ROWS + 2 * pair], mixed[device * ROWS + 2 * pair + 1]
            out_ref[device, pair * BLK : (pair + 1) * BLK] = jnp.where(
                lane < HEAD, pltpu.roll(even, HEAD, 1), odd
            ).astype(jnp.bfloat16)
        table_ref[device] = jnp.transpose(column)[: 2 * ROWS]


def attend_forward(turns, qg, kv):
    most = most_pairs(turns)
    blocks = RING_X * ROWS
    square = pltpu.VMEM((blocks, BLK, PAIR), jnp.float32)
    return pl.pallas_call(
        forward_kernel,
        out_shape=(
            jax.ShapeDtypeStruct((RING_X, ROWS // 2 * BLK, PAIR), jnp.bfloat16),
            jax.ShapeDtypeStruct((RING_X, 2 * ROWS, PAIR), jnp.float32),
        ),
        in_specs=[SMEM, VMEM, VMEM],
        out_specs=(VMEM, VMEM),
        scratch_shapes=[
            pltpu.SMEM((most,), jnp.int32),
            pltpu.SMEM((most,), jnp.int32),
            pltpu.VMEM((blocks, BLK, PAIR), jnp.bfloat16),
            pltpu.VMEM((most, BLK, BLK), jnp.float32),
            square,
            square,
            square,
        ],
        compiler_params=pltpu.CompilerParams(vmem_limit_bytes=LIMIT),
        cost_estimate=pl.CostEstimate(
            flops=most * 4 * BLK * BLK * PAIR, bytes_accessed=kv.size * 4, transcendentals=most * BLK * BLK
        ),
        name="attend_forward",
    )(turns, qg.reshape(-1, BLK, PAIR), kv.reshape(-1, BLK, PAIR))


def backward_kernel(
    turn_ref, qg_ref, kv_ref, stats_ref, query_ref, key_ref, own_list, far_list, rhs, query, key
):
    count = list_pairs(turn_ref, own_list, far_list)
    rounds = lax.div(count + UNROLL - 1, UNROLL)
    lane = lax.broadcasted_iota(jnp.int32, (BLK, PAIR), 1)
    zero = jnp.zeros((BLK, PAIR), jnp.bfloat16)
    for block in range(qg_ref.shape[0]):
        pair = qg_ref[block]
        rhs[block, :BLK] = jnp.where(lane < HEAD, pair, zero)
        rhs[block, BLK:] = jnp.where(lane < HEAD, zero, pair)
    query[...] = jnp.zeros_like(query)
    key[...] = jnp.zeros_like(key)

    def step_of(step, carry):
        now = []
        for u in range(UNROLL):
            tile = step * UNROLL + u
            now.append((tile, own_list[tile], far_list[tile]))
        both = [
            lax.dot_general(
                kv_ref[far], rhs[own], (((1,), (1,)), ((), ())), preferred_element_type=jnp.float32
            )
            for _, own, far in now
        ]
        factors = []
        for (tile, own, _), product in zip(now, both):
            device, block = lax.div(own, ROWS), lax.rem(own, ROWS)
            top, inverse, drift = (
                stats_ref[device, pl.ds(kind * ROWS + block, 1), :] for kind in range(3)
            )
            masked = product[:, :BLK] * EXP2_SCALE + jnp.where(tile < count, 0.0, -jnp.inf)
            prob = jnp.exp2(masked - top) * inverse
            slope = prob * (product[:, BLK:] - drift)
            factors.append((slope.astype(jnp.bfloat16), prob.astype(jnp.bfloat16)))
        to_keys = [
            jnp.dot(jnp.concatenate(factor, axis=1), rhs[own], preferred_element_type=jnp.float32)
            for factor, (_, own, _) in zip(factors, now)
        ]
        to_queries = [
            lax.dot_general(
                slope, kv_ref[far], (((0,), (0,)), ((), ())), preferred_element_type=jnp.float32
            )
            for (slope, _), (_, _, far) in zip(factors, now)
        ]
        for (_, own, far), to_key, to_query in zip(now, to_keys, to_queries):
            key[far] += to_key
            query[own] += to_query
        return carry

    lax.fori_loop(0, rounds, step_of, 0)
    for block in range(key.shape[0]):
        key_ref[block] = jnp.where(lane < HEAD, key[block] * SCALE, key[block]).astype(jnp.bfloat16)
    for device in range(RING_X):
        for pair in range(ROWS // 2):
            even, odd = query[device * ROWS + 2 * pair], query[device * ROWS + 2 * pair + 1]
            query_ref[device, pair * BLK : (pair + 1) * BLK] = (
                jnp.where(lane < HEAD, even, pltpu.roll(odd, HEAD, 1)) * SCALE
            )


def attend_backward(turns, qg, kv, stats):
    most = most_pairs(turns)
    blocks, keys = RING_X * ROWS, kv.shape[0] * ROWS
    return pl.pallas_call(
        backward_kernel,
        out_shape=(
            jax.ShapeDtypeStruct((RING_X, ROWS // 2 * BLK, PAIR), jnp.float32),
            jax.ShapeDtypeStruct((keys, BLK, PAIR), jnp.bfloat16),
        ),
        in_specs=[SMEM, VMEM, VMEM, VMEM],
        out_specs=(VMEM, VMEM),
        scratch_shapes=[
            pltpu.SMEM((most,), jnp.int32),
            pltpu.SMEM((most,), jnp.int32),
            pltpu.VMEM((blocks, 2 * BLK, PAIR), jnp.bfloat16),
            pltpu.VMEM((blocks, BLK, PAIR), jnp.float32),
            pltpu.VMEM((keys, BLK, PAIR), jnp.float32),
        ],
        compiler_params=pltpu.CompilerParams(vmem_limit_bytes=LIMIT),
        cost_estimate=pl.CostEstimate(
            flops=most * 10 * BLK * BLK * PAIR, bytes_accessed=kv.size * 4, transcendentals=most * BLK * BLK
        ),
        name="attend_backward",
    )(turns, qg.reshape(-1, BLK, PAIR), kv.reshape(-1, BLK, PAIR), stats)


def combine_kernel(
    parts, tables, qg_ref, context, stats_ref, got, got_tables, send, recv, t_send, t_recv, s_send, s_recv
):
    _, _, at_y, at_x, _, count_y = places()
    along_x, _ = seq_partners(at_y, at_x, count_y)
    greet(along_x)
    steps = range(len(along_x))

    def give(step):
        target = lax.rem(at_x + step + 1, RING_X)
        return remote(parts.at[target], got.at[step], send.at[step], recv.at[step], along_x[step])

    def give_table(step):
        target = lax.rem(at_x + step + 1, RING_X)
        return remote(
            tables.at[target], got_tables.at[step], t_send.at[step], t_recv.at[step], along_x[step]
        )

    def tell(step, slot):
        part = stats_ref.at[slot]
        return remote(part, part, s_send.at[step], s_recv.at[step], along_x[step])

    for step in steps:
        give_table(step).start()
    for step in steps:
        give(step).start()
    for step in steps:
        give_table(step).wait_recv()
    lane = lax.broadcasted_iota(jnp.int32, (BLK, PAIR), 1)

    def values(start):
        rows = slice(start, start + BLK)
        found = [parts[at_x, rows]] + [got[step, rows] for step in steps]
        return [part.astype(jnp.float32) for part in found]

    both = [tables[at_x]] + [got_tables[step] for step in steps]
    tops, totals = [table[:ROWS] for table in both], [table[ROWS:] for table in both]
    top = functools.reduce(jnp.maximum, tops)
    factors = [jnp.exp2(part - top) for part in tops]
    inverse = 1.0 / sum(factor * part for factor, part in zip(factors, totals))
    shares = [factor * inverse for factor in factors]
    blank = jnp.zeros((BLK - ROWS * RING_X, PAIR), jnp.float32)
    columns = jnp.transpose(jnp.concatenate(shares + [blank], axis=0))
    drifts = jnp.zeros((BLK, PAIR), jnp.float32)
    for step in steps:
        give(step).wait_recv()
    for block in range(ROWS):
        output = jnp.zeros((BLK, PAIR), jnp.float32)
        for index, part in enumerate(values(block // 2 * BLK)):
            at = index * ROWS + block
            output += (part if block % 2 else pltpu.roll(part, HEAD, 1)) * columns[:, at : at + 1]
        output = jnp.where(lane < HEAD, 0.0, output)
        rows = slice(block * BLK, (block + 1) * BLK)
        context[rows] = output.astype(jnp.bfloat16)
        drift = jnp.sum(qg_ref[at_x, rows].astype(jnp.float32) * output, axis=1, keepdims=True)
        drifts = jnp.where(lane == block, drift, drifts)
    drift_rows = jnp.transpose(drifts)[: 2 * ROWS]
    stats_ref[at_x] = jnp.concatenate([top, inverse, drift_rows], axis=0)
    for step in steps:
        tell(step, at_x).start()
    for step in steps:
        tell(step, wrap(at_x - step - 1, RING_X)).wait_recv()
    for step in steps:
        give(step).wait_send()
        give_table(step).wait_send()
        tell(step, at_x).wait_send()


def combine(parts, tables, qg):
    sems = pltpu.SemaphoreType.DMA((RING_X - 1,))
    return pl.pallas_call(
        combine_kernel,
        out_shape=(
            jax.ShapeDtypeStruct((ROWS * BLK, PAIR), jnp.bfloat16),
            jax.ShapeDtypeStruct((RING_X, 4 * ROWS, PAIR), jnp.float32),
        ),
        in_specs=[VMEM, VMEM, VMEM],
        out_specs=(VMEM, VMEM),
        scratch_shapes=[
            pltpu.VMEM((RING_X - 1,) + parts.shape[1:], jnp.bfloat16),
            pltpu.VMEM((RING_X - 1,) + tables.shape[1:], jnp.float32),
        ]
        + [sems] * 6,
        compiler_params=pltpu.CompilerParams(
            collective_id=1, has_side_effects=True, vmem_limit_bytes=LIMIT
        ),
        name="combine",
    )(parts, tables, qg)


def sum_over_seq(parts, sums_refs, x_sum, arrived, leaving, from_y, piece, totals, *sems):
    _, _, at_y, at_x, _, count_y = places()
    near = neighbours(at_y, at_x, count_y)
    around = (near["x", 1], near["x", -1])
    _, along_y = seq_partners(at_y, at_x, count_y)
    ys = range(len(along_y))

    def columns(index):
        return pl.ds(pl.multiple_of(index * PAIR, PAIR), PAIR)

    def in_y(step):
        source = x_sum.at[:, columns(lax.rem(at_y + step + 1, count_y))]
        return remote(source, from_y.at[step], sems[2].at[step], sems[3].at[step], along_y[step])

    def out_y(step, owner):
        target = totals.at[at_x, :, columns(owner)]
        return remote(piece, target, sems[4].at[step], sems[5].at[step], along_y[step])

    over_x = ring_sum(parts, x_sum, arrived, leaving, at_x, RING_X, around, sems[0], sems[1])
    take(over_x, 2)
    yield
    take(over_x, 4)
    yield
    take(over_x, 1)
    for step in ys:
        in_y(step).start()
    yield
    total = x_sum[:, columns(at_y)].astype(jnp.float32)
    for step in ys:
        in_y(step).wait_recv()
        total += from_y[step].astype(jnp.float32)
    piece[...] = total.astype(jnp.bfloat16)
    for step in ys:
        out_y(step, at_y).start()
    totals[at_x, :, columns(at_y)] = piece[...]
    yield
    for step in ys:
        out_y(step, wrap(at_y - step - 1, count_y)).wait_recv()
    back = ring_gather(totals, at_x, RING_X, around, sems[6], sems[7])
    take(back, 4)
    yield
    finish(back)
    count = RING_X // len(sums_refs)
    for index in range(RING_X):
        height = totals.shape[1]
        rows = pl.ds(index % count * height, height)
        sums_refs[index // count][rows] = totals[index].astype(jnp.float32)
    finish(over_x)
    for step in ys:
        in_y(step).wait_send()
        out_y(step, at_y).wait_send()


def gradient_kernel(
    query_parts,
    key_parts,
    context,
    features_ref,
    key_w,
    value_w,
    query_w,
    out_w,
    attended,
    grad_frames,
    sums_ref,
    features,
    weights,
    filled,
    loaded,
    joint,
    lhs,
    turned,
    got,
    key_sum,
    arrived,
    leaving,
    x_send,
    x_recv,
    y_send,
    y_recv,
    *refs,
):
    chip, core, at_y, at_x, chips, count_y = places()
    along_x, along_y = seq_partners(at_y, at_x, count_y)
    near = neighbours(at_y, at_x, count_y)
    fill = stack_rows((key_w, value_w, query_w, out_w), weights, filled)
    load = pltpu.make_async_copy(features_ref, features, loaded)
    for copy in fill + [load]:
        copy.start()
    greet(along_x + along_y + mp_partners(chip, core, chips))
    steps = range(len(along_x))

    def give(step):
        target = lax.rem(at_x + step + 1, RING_X)
        return remote(query_parts.at[target], got.at[step], x_send.at[step], x_recv.at[step], along_x[step])

    over_y = ring_sum(
        key_parts, key_sum, arrived, leaving, at_y, count_y, (near["y", 1], near["y", -1]), y_send, y_recv
    )
    take(over_y, 4)
    for step in steps:
        give(step).start()
    for copy in fill:
        copy.wait()

    def columns(tile):
        return pl.ds(pl.multiple_of(tile * PAIR, PAIR), PAIR)

    half = context.shape[0] // 2

    def turned_rows(target, source):
        target[:half] = half_rows_of(source, 1 - core)
        target[half:] = half_rows_of(source, core)

    def output_part(tile):
        return jnp.dot(turned[:, :PAIR], weights[PAIR:, columns(tile)], preferred_element_type=jnp.float32)

    def input_part(tile):
        return jnp.dot(turned[...], weights[:, columns(tile)], preferred_element_type=jnp.float32)

    turned_rows(turned.at[:, pl.ds(0, PAIR)], context)
    seq_refs = len(seq_scratch(count_y))
    mp_refs = (len(refs) - 2 * seq_refs) // 2
    early, late = refs[:seq_refs], refs[seq_refs : 2 * seq_refs]
    outputs = sum_over_mp(output_part, attended, *refs[2 * seq_refs : 2 * seq_refs + mp_refs])
    inputs = sum_over_mp(input_part, grad_frames, *refs[2 * seq_refs + mp_refs :])
    sums = [sums_ref.at[pl.ds(index * HEAD, HEAD)] for index in range(4)]
    over_seq = [
        sum_over_seq(early[0], sums[2:], *early[1:]),
        sum_over_seq(late[0], sums[:2], *late[1:]),
    ]
    width = D

    def store_product(target, first, values, at, lower, upper):
        turned = jnp.transpose(values.astype(jnp.float32)).astype(jnp.bfloat16)
        product = lax.dot_general(
            turned,
            features[at].reshape(width, values.shape[0]),
            (((1,), (1,)), ((), ())),
            preferred_element_type=jnp.float32,
        )
        height = target.shape[1]
        for index in range((upper - lower) // height):
            start = lower + index * height
            target[first + index] = product[start : start + height].astype(jnp.bfloat16)

    lane = lax.broadcasted_iota(jnp.int32, (BLK, PAIR), 1)
    for turn in range(chips):
        take(outputs, 2)
        take(over_y, 3)
        if turn == chips // 2:
            for step in steps:
                give(step).wait_recv()
            for pair in range(ROWS // 2):
                part = slice(pair * BLK, (pair + 1) * BLK)
                total = query_parts[at_x, part]
                for step in steps:
                    total += got[step, part]
                for block, value in ((2 * pair, total), (2 * pair + 1, pltpu.roll(total, HEAD, 1))):
                    rows = slice(block * BLK, (block + 1) * BLK)
                    value = value.astype(jnp.bfloat16)
                    joint[rows] = jnp.where(lane < HEAD, value, context[rows])
                    lhs[rows, PAIR:] = jnp.where(lane < HEAD, value, jnp.zeros_like(value))
            load.wait()
            store_product(early[0], 0, joint[...], 0, 0, HEAD)
            store_product(early[0], RING_X // 2, joint[...], 1, HEAD, PAIR)
            take(over_seq[0], 1)
    take(over_seq[0], 1)
    take(over_y, 1)
    lhs[:, :PAIR] = key_sum[...]
    turned_rows(turned, lhs)
    store_product(late[0], 0, key_sum[...], 0, 0, PAIR)
    take(over_seq[1], 1)
    take(over_seq[0], 1)
    take(inputs, chips)
    take(over_seq[1], 1)
    take(over_seq[0], 1)
    take(inputs, chips)
    take(over_seq[1], 1)
    take(over_seq[0], 1)
    take(outputs, 1)
    take(over_seq[1], 2)
    take(inputs, 1)
    finish(over_seq[0])
    finish(over_seq[1])
    finish(outputs)
    finish(inputs)
    finish(over_y)
    for step in steps:
        give(step).wait_send()


def seq_scratch(count_y):
    dma = pltpu.SemaphoreType.DMA
    x_ring, y_sems = dma((RING_X // 2, 2, 2)), dma((count_y - 1,))
    height = 2 * HEAD // RING_X
    stack = pltpu.VMEM((RING_X, height, D), jnp.bfloat16)
    return [
        stack,
        pltpu.VMEM((height, D), jnp.bfloat16),
        pltpu.VMEM((RING_X // 2, 2, height, D), jnp.bfloat16),
        pltpu.VMEM((RING_X // 2 - 1, 2, height, D), jnp.bfloat16),
        pltpu.VMEM((count_y - 1, height, PAIR), jnp.bfloat16),
        pltpu.VMEM((height, PAIR), jnp.bfloat16),
        stack,
        x_ring,
        x_ring,
        y_sems,
        y_sems,
        y_sems,
        y_sems,
        x_ring,
        x_ring,
    ]


def sum_gradients(query_parts, key_parts, context, features, weights):
    peers = lax.axis_size("seq")
    rows = context.shape[0]
    count_y = peers // RING_X
    dma = pltpu.SemaphoreType.DMA
    x_sems, y_ring = dma((RING_X - 1,)), dma((count_y // 2, 2, 4))
    out = jax.ShapeDtypeStruct((HEAD, rows), jnp.bfloat16)

    def rounded(*shape):
        return pltpu.VMEM(shape, jnp.bfloat16)

    return pl.pallas_call(
        gradient_kernel,
        out_shape=(out, out, jax.ShapeDtypeStruct((RING_X * HEAD, D), jnp.float32)),
        in_specs=[VMEM] * 3 + [ANY] * 5,
        out_specs=(VMEM, VMEM, VMEM),
        scratch_shapes=[
            rounded(*features.shape),
            rounded(RING_X * HEAD, D),
            dma((4,)),
            dma,
            rounded(rows, PAIR),
            rounded(rows, 2 * PAIR),
            rounded(rows, 2 * PAIR),
            pltpu.VMEM((RING_X - 1,) + query_parts.shape[1:], jnp.float32),
            rounded(rows, PAIR),
            rounded(count_y // 2, 2, rows, PAIR),
            rounded(count_y // 2 - 1, 2, rows, PAIR),
            x_sems,
            x_sems,
            y_ring,
            y_ring,
        ]
        + seq_scratch(count_y)
        + seq_scratch(count_y)
        + sum_scratch(rows)
        + sum_scratch(rows),
        compiler_params=pltpu.CompilerParams(
            collective_id=2, has_side_effects=True, vmem_limit_bytes=LIMIT
        ),
        name="sum_gradients",
    )(query_parts, key_parts.reshape(count_y, rows, PAIR), context, features, *weights)


def on_device(frames, cotangent, query_weight, key_weight, value_weight, out_weight, turn_blocks):
    turns = jnp.transpose(turn_blocks, (0, 2, 1))
    weights = (key_weight, value_weight, query_weight, out_weight)
    features, kv, qg = project(frames, cotangent, weights)
    context, stats = combine(*attend_forward(turns, qg, kv), qg)
    query_parts, key_parts = attend_backward(turns, qg, kv, stats)
    attended, grad_frames, sums = sum_gradients(query_parts, key_parts, context, features, weights)
    grad_key, grad_value, grad_query, grad_out = (
        sums[index * HEAD : (index + 1) * HEAD] for index in range(4)
    )
    return attended.T, grad_frames.T, grad_query, grad_key, grad_value, grad_out


def solution(mesh):
    return jax.shard_map(
        on_device,
        mesh=mesh,
        in_specs=(
            P("seq", "mp"),
            P("seq", "mp"),
            P("mp", None),
            P("mp", None),
            P("mp", None),
            P("mp", None),
            P(),
        ),
        out_specs=(
            P("seq", "mp"),
            P("seq", "mp"),
            P("mp", None),
            P("mp", None),
            P("mp", None),
            P("mp", None),
        ),
        check_vma=False,
    )
```

```python
import functools
import math

import jax
import jax.numpy as jnp
from jax import lax
from jax.experimental import pallas as pl
from jax.experimental.pallas import tpu as pltpu
from jax.sharding import PartitionSpec as P

D = 1024
HEADS = 16
BLK = 128
BAND = 2
RING_X = 4
ROWS = 4
LEAST = -3e38
HEAD = D // HEADS
PAIR = 2 * HEAD
UNROLL = 8
SCALE = 1.0 / math.sqrt(HEAD)
EXP2_SCALE = SCALE * math.log2(math.e)
MESH = pl.DeviceIdType.MESH
VMEM = pl.BlockSpec(memory_space=pltpu.VMEM)
SMEM = pl.BlockSpec(memory_space=pltpu.SMEM)
ANY = pl.BlockSpec(memory_space=pl.ANY)
LIMIT = 48 * 1024 * 1024


def wrap(index, count):
    return lax.rem(index + count, count)


def greet(devices):
    barrier = pltpu.get_barrier_semaphore()
    for device in devices:
        pl.semaphore_signal(barrier, inc=1, device_id=device, device_id_type=MESH)
    pl.semaphore_wait(barrier, len(devices))


def remote(source, target, send, recv, device):
    return pltpu.make_async_remote_copy(
        source, target, send, recv, device_id=device, device_id_type=MESH
    )


def take(process, count):
    for _ in range(count):
        next(process, None)


def finish(process):
    for _ in process:
        pass


def stack_rows(refs, whole, sems):
    copies = []
    for index, ref in enumerate(refs):
        target = whole.at[pl.ds(index * HEAD, HEAD)]
        copies.append(pltpu.make_async_copy(ref, target, sems.at[index]))
    return copies


def places():
    me_mp, me = lax.axis_index("mp"), lax.axis_index("seq")
    chips, count_y = lax.axis_size("mp") // 2, lax.axis_size("seq") // RING_X
    return lax.div(me_mp, 2), lax.rem(me_mp, 2), lax.div(me, RING_X), lax.rem(me, RING_X), chips, count_y


def neighbours(at_y, at_x, count_y):
    return {
        ("x", 1): {"seq": at_y * RING_X + wrap(at_x + 1, RING_X)},
        ("x", -1): {"seq": at_y * RING_X + wrap(at_x - 1, RING_X)},
        ("y", 1): {"seq": wrap(at_y + 1, count_y) * RING_X + at_x},
        ("y", -1): {"seq": wrap(at_y - 1, count_y) * RING_X + at_x},
    }


def ring_messages(count, parts):
    return [
        (hop, way, part)
        for hop in range(1, count // 2 + 1)
        for part in range(parts)
        for way in (0, 1)
        if hop < count // 2 or part // (parts // 2) == way
    ]


def ring_gather(store, at, count, devices, send, recv):
    parts = send.shape[2]
    part_rows = store.shape[1] // parts

    def copy_of(hop, way, part, arriving):
        moved = hop if arriving else hop - 1
        slot = wrap(at + (-moved if way == 0 else moved), count)
        spot = store.at[slot, pl.ds(part * part_rows, part_rows)]
        index = (hop - 1, way, part)
        return remote(spot, spot, send.at[index], recv.at[index], devices[way])

    messages = ring_messages(count, parts)
    for hop, way, part in messages:
        if hop > 1:
            copy_of(hop - 1, way, part, True).wait_recv()
        copy_of(hop, way, part, False).start()
        yield
    for hop, way, part in messages:
        if (hop + 1, way, part) not in messages:
            copy_of(hop, way, part, True).wait_recv()
    yield
    for hop, way, part in messages:
        copy_of(hop, way, part, False).wait_send()


def ring_sum(values, out, arrived, leaving, at, count, devices, send, recv):
    parts = send.shape[2]
    part_rows = values.shape[1] // parts
    last = count // 2

    def rows(part):
        return pl.ds(part * part_rows, part_rows)

    def copy_of(hop, way, part):
        index = (hop - 1, way, part)
        if hop == 1:
            source = values.at[wrap(at + last, count), rows(part)]
        else:
            source = leaving.at[hop - 2, way, rows(part)]
        target = arrived.at[hop - 1, way, rows(part)]
        return remote(source, target, send.at[index], recv.at[index], devices[way])

    messages = [
        (hop, way, part)
        for hop in range(1, last + 1)
        for part in range(parts)
        for way in (0, 1)
        if hop > 1 or part // (parts // 2) == way
    ]

    def summed(hop, way, part):
        slot = wrap(at + (last + 1 - hop if way == 0 else hop - 1 - last), count)
        value = values[slot, rows(part)].astype(jnp.float32)
        if (hop - 1, way, part) in messages:
            copy_of(hop - 1, way, part).wait_recv()
            value += arrived[hop - 2, way, rows(part)].astype(jnp.float32)
        return value

    for hop, way, part in messages:
        if hop > 1:
            leaving[hop - 2, way, rows(part)] = summed(hop, way, part).astype(jnp.bfloat16)
        copy_of(hop, way, part).start()
        yield
    for part in range(parts):
        value = values[at, rows(part)].astype(jnp.float32)
        for way in (0, 1):
            copy_of(last, way, part).wait_recv()
            value += arrived[last - 1, way, rows(part)].astype(jnp.float32)
        out[rows(part)] = value.astype(jnp.bfloat16)
    yield
    for message in messages:
        copy_of(*message).wait_send()


def sum_over_mp(partial, out_ref, mine, gift, theirs, chip_sum, tiles, done, pair_send, pair_recv, z_send, z_recv, swap_send, swap_recv):
    chip, core, _, _, chips, _ = places()
    sibling = {"mp": 2 * chip + 1 - core}
    half = mine.shape[1]

    def give(step):
        return remote(gift.at[step], theirs.at[step], pair_send.at[step], pair_recv.at[step], sibling)

    def post(step):
        target = {"mp": 2 * lax.rem(chip + step, chips) + core}
        return remote(chip_sum.at[step], tiles.at[step], z_send.at[step - 1], z_recv.at[step - 1], target)

    order = sorted(range(1, chips), key=lambda step: -min(step, chips - step)) + [0]
    for step in order:
        tile = lax.rem(chip + step, chips)
        product = partial(tile)
        gift[step] = product[:half].astype(jnp.bfloat16)
        give(step).start()
        mine[step] = product[half:]
        yield
    for step in order:
        give(step).wait_recv()
        mine[step] += theirs[step].astype(jnp.float32)
        if step:
            chip_sum[step] = mine[step].astype(jnp.bfloat16)
            post(step).start()
        yield
    total = mine[0]
    for step in reversed(order[:-1]):
        post(step).wait_recv()
        total += tiles[step].astype(jnp.float32)
    done[...] = jnp.transpose(total).astype(jnp.bfloat16)
    columns = pl.ds(pl.multiple_of(core * half, half), half)
    other_columns = pl.ds(pl.multiple_of((1 - core) * half, half), half)
    own_rows = pl.ds(pl.multiple_of(core * HEAD, HEAD), HEAD)
    swap = remote(
        done.at[pl.ds(pl.multiple_of((1 - core) * HEAD, HEAD), HEAD)],
        out_ref.at[:, columns],
        swap_send,
        swap_recv,
        sibling,
    )
    swap.start()
    out_ref[:, columns] = done[own_rows]
    yield
    remote(done.at[own_rows], out_ref.at[:, other_columns], swap_send, swap_recv, sibling).wait_recv()
    swap.wait_send()
    for step in order:
        give(step).wait_send()
        if step:
            post(step).wait_send()


def sum_scratch(rows):
    chips = lax.axis_size("mp") // 2
    half = rows // 2
    dma = pltpu.SemaphoreType.DMA
    some = pltpu.VMEM((chips, half, PAIR), jnp.bfloat16)
    return [
        pltpu.VMEM((chips, half, PAIR), jnp.float32),
        some,
        some,
        some,
        some,
        pltpu.VMEM((PAIR, half), jnp.bfloat16),
        dma((chips,)),
        dma((chips,)),
        dma((chips - 1,)),
        dma((chips - 1,)),
        dma,
        dma,
    ]


def mp_partners(chip, core, chips):
    return [{"mp": 2 * chip + 1 - core}] + [
        {"mp": 2 * lax.rem(chip + step, chips) + core} for step in range(1, chips)
    ]


def seq_partners(at_y, at_x, count_y):
    along_x = [{"seq": at_y * RING_X + lax.rem(at_x + step, RING_X)} for step in range(1, RING_X)]
    along_y = [{"seq": lax.rem(at_y + step, count_y) * RING_X + at_x} for step in range(1, count_y)]
    return along_x, along_y


def half_rows_of(ref, half):
    rows = ref.shape[0] // 2
    return ref[pl.ds(pl.multiple_of(half * rows, rows), rows)]


def project_kernel(
    frames_ref,
    grad_ref,
    key_w,
    value_w,
    query_w,
    out_w,
    features,
    kv_ref,
    qg_ref,
    weights,
    loaded,
    filled,
    z_send,
    z_recv,
    share_send,
    share_recv,
    y_send,
    y_recv,
    x_send,
    x_recv,
):
    chip, core, at_y, at_x, chips, count_y = places()
    hops = chips // 2
    rows = features.shape[-1]
    half = rows // 2
    sibling = {"mp": 2 * chip + 1 - core}
    right = {"mp": 2 * wrap(chip + 1, chips) + core}
    left = {"mp": 2 * wrap(chip - 1, chips) + core}
    inputs = [
        pltpu.make_async_copy(ref, features.at[kind, chip, core], loaded.at[kind])
        for kind, ref in enumerate((frames_ref, grad_ref))
    ]
    fill = stack_rows((key_w, value_w, query_w, out_w), weights, filled)
    for copy in inputs + fill:
        copy.start()
    greet([sibling, right, left] + list(neighbours(at_y, at_x, count_y).values()))
    for copy in inputs:
        copy.wait()

    def along_z(kind, way, hop, part, moved):
        tile = wrap(chip + (-moved if way == 0 else moved), chips)
        spot = features.at[kind, tile, core, :, pl.ds(part * half, half)]
        at = (kind, way, hop - 1, part)
        return remote(spot, spot, z_send.at[at], z_recv.at[at], right if way == 0 else left)

    def sent(kind, way, hop, part):
        return along_z(kind, way, hop, part, hop - 1)

    def landed(kind, way, hop, part):
        return along_z(kind, way, hop, part, hop)

    def shared(kind, whose):
        spot = features.at[kind, :, whose]
        return remote(spot, spot, share_send.at[kind], share_recv.at[kind], sibling)

    z_messages = ring_messages(chips, 2)

    def advance(kind, hop):
        for _, way, part in [message for message in z_messages if message[0] == hop]:
            landed(kind, way, hop, part).wait_recv()
            if (hop + 1, way, part) in z_messages:
                sent(kind, way, hop + 1, part).start()
        if hop == hops:
            shared(kind, core).start()

    def begin(kind):
        for _, way, part in [message for message in z_messages if message[0] == 1]:
            sent(kind, way, 1, part).start()

    begin(0)
    for hop in range(1, hops + 1):
        advance(0, hop)
        if hop == hops - 2:
            begin(1)
        if hop > hops - 2:
            advance(1, hop - hops + 2)
    for copy in fill:
        copy.wait()
    shared(0, 1 - core).wait_recv()

    def products(rows_of_weights, kind):
        whole = features[kind].reshape(chips * PAIR, rows)
        product = jnp.dot(weights[rows_of_weights], whole, preferred_element_type=jnp.float32)
        return jnp.transpose(product).astype(jnp.bfloat16)

    joined = products(slice(None), 0)
    kv_ref[at_y] = joined[:, :PAIR]
    queries = joined[:, PAIR:]
    near = neighbours(at_y, at_x, count_y)
    over_y = ring_gather(kv_ref, at_y, count_y, (near["y", 1], near["y", -1]), y_send, y_recv)
    take(over_y, 8)
    for hop in range(3, hops + 1):
        advance(1, hop)
        take(over_y, 4)
    shared(1, 1 - core).wait_recv()
    lane = lax.broadcasted_iota(jnp.int32, queries.shape, 1)
    qg_ref[at_x] = jnp.where(lane < HEAD, queries, products(slice(PAIR, None), 1))
    over_x = ring_gather(qg_ref, at_x, RING_X, (near["x", 1], near["x", -1]), x_send, x_recv)
    take(over_x, 4)
    take(over_y, 6)
    take(over_x, 2)
    finish(over_y)
    finish(over_x)
    for kind in (0, 1):
        shared(kind, core).wait_send()
        for hop, way, part in z_messages:
            sent(kind, way, hop, part).wait_send()


def project(frames, cotangent, weights):
    cores, peers = lax.axis_size("mp"), lax.axis_size("seq")
    rows = frames.shape[0]
    dma = pltpu.SemaphoreType.DMA
    sems = dma((2, 2, cores // 4, 2))
    x_sems, y_sems = dma((RING_X // 2, 2, 2)), dma((peers // RING_X // 2, 2, 4))
    return pl.pallas_call(
        project_kernel,
        out_shape=(
            jax.ShapeDtypeStruct((2, cores // 2, 2, HEAD, rows), jnp.bfloat16),
            jax.ShapeDtypeStruct((peers // RING_X, rows, PAIR), jnp.bfloat16),
            jax.ShapeDtypeStruct((RING_X, rows, PAIR), jnp.bfloat16),
        ),
        in_specs=[ANY] * 6,
        out_specs=(VMEM, VMEM, VMEM),
        scratch_shapes=[
            pltpu.VMEM((4 * HEAD, D), jnp.bfloat16),
            dma((2,)),
            dma((4,)),
            sems,
            sems,
            dma((2,)),
            dma((2,)),
            y_sems,
            y_sems,
            x_sems,
            x_sems,
        ],
        compiler_params=pltpu.CompilerParams(
            collective_id=0, has_side_effects=True, vmem_limit_bytes=60 * 1024 * 1024
        ),
        name="project",
    )(frames.T, cotangent.T, *weights)


def list_pairs(turn_ref, own_ref, far_ref):
    _, _, at_y, at_x, _, count_y = places()
    count = jnp.int32(0)
    spread = RING_X * ROWS

    def add(count, own, far, ok):
        own_ref[count] = jnp.clip(own, 0, spread - 1)
        far_ref[count] = jnp.clip(far, 0, count_y * ROWS - 1)
        return count + ok.astype(jnp.int32)

    for block in range(ROWS):
        for offset in range(-BAND, BAND + 1):
            own = at_x * ROWS + block + offset
            count = add(count, own, at_y * ROWS + block, (own >= 0) & (own < spread))
    first, final = at_x == 0, at_x == RING_X - 1
    crosses = (first & (at_y + 1 < count_y)) | (final & (at_y > 0))
    for ahead in range(BAND):
        for back in range(BAND - ahead):
            own = jnp.where(first, spread - 1 - back, back)
            far = jnp.where(first, (at_y + 1) * ROWS + ahead, at_y * ROWS - 1 - ahead)
            count = add(count, own, far, crosses)

    def visit(index, count):
        row, column = lax.div(index, RING_X), lax.rem(index, RING_X)
        holder, partner = at_y * RING_X + column, row * RING_X + at_x
        for slot in range(turn_ref.shape[1]):
            own = turn_ref[holder, slot, partner]
            far = turn_ref[partner, slot, holder]
            ok = (own >= 0) & (jnp.abs(own - far) > BAND)
            count = add(count, own - at_y * spread, far + (row - partner) * ROWS, ok)
        return count

    count = lax.fori_loop(0, count_y * RING_X, visit, count)
    for pad in range(UNROLL):
        own_ref[count + pad] = 0
        far_ref[count + pad] = 0
    return count


def most_pairs(turns):
    return ROWS * (2 * BAND + 1) + BAND * (BAND + 1) // 2 + turns.shape[0] * turns.shape[1] + UNROLL


def forward_kernel(turn_ref, qg_ref, kv_ref, out_ref, table_ref, own_list, far_list, lhs, score, top, total, mixed):
    count = list_pairs(turn_ref, own_list, far_list)
    rounds = lax.div(count + UNROLL - 1, UNROLL)
    lane = lax.broadcasted_iota(jnp.int32, (BLK, PAIR), 1)
    blocks = qg_ref.shape[0]
    zero = jnp.zeros((BLK, PAIR), jnp.bfloat16)
    for block in range(blocks):
        lhs[block] = jnp.where(lane < HEAD, qg_ref[block], zero)
    top[...] = jnp.full_like(top, LEAST)
    total[...] = jnp.zeros_like(total)
    mixed[...] = jnp.zeros_like(mixed)

    def tiles(step):
        at = [step * UNROLL + u for u in range(UNROLL)]
        return [(tile, own_list[tile], far_list[tile]) for tile in at]

    def score_step(step, carry):
        now = tiles(step)
        products = [
            lax.dot_general(
                lhs[own], kv_ref[far], (((1,), (1,)), ((), ())), preferred_element_type=jnp.float32
            )
            for _, own, far in now
        ]
        scaled = []
        for (tile, _, _), product in zip(now, products):
            masked = product * EXP2_SCALE + jnp.where(tile < count, 0.0, -jnp.inf)
            score[tile] = masked
            scaled.append(masked)
        for (_, own, _), masked in zip(now, scaled):
            top[own] = jnp.maximum(top[own], masked)
        return carry

    lax.fori_loop(0, rounds, score_step, 0)
    for block in range(blocks):
        top[block] = jnp.broadcast_to(jnp.max(top[block], axis=1, keepdims=True), (BLK, PAIR))

    def weight_step(step, carry):
        now = tiles(step)
        weights = [jnp.exp2(score[tile] - top[own]) for tile, own, _ in now]
        sums = [
            jnp.dot(weight.astype(jnp.bfloat16), kv_ref[far], preferred_element_type=jnp.float32)
            for weight, (_, _, far) in zip(weights, now)
        ]
        for (_, own, _), weight, part in zip(now, weights, sums):
            total[own] += weight
            mixed[own] += part
        return carry

    lax.fori_loop(0, rounds, weight_step, 0)
    for device in range(RING_X):
        column = jnp.zeros((BLK, PAIR), jnp.float32)
        for block in range(ROWS):
            at = device * ROWS + block
            column = jnp.where(lane == block, top[at], column)
            column = jnp.where(lane == ROWS + block, jnp.sum(total[at], axis=1, keepdims=True), column)
        for pair in range(ROWS // 2):
            even, odd = mixed[device * ROWS + 2 * pair], mixed[device * ROWS + 2 * pair + 1]
            out_ref[device, pair * BLK : (pair + 1) * BLK] = jnp.where(
                lane < HEAD, pltpu.roll(even, HEAD, 1), odd
            ).astype(jnp.bfloat16)
        table_ref[device] = jnp.transpose(column)[: 2 * ROWS]


def attend_forward(turns, qg, kv):
    most = most_pairs(turns)
    blocks = RING_X * ROWS
    square = pltpu.VMEM((blocks, BLK, PAIR), jnp.float32)
    return pl.pallas_call(
        forward_kernel,
        out_shape=(
            jax.ShapeDtypeStruct((RING_X, ROWS // 2 * BLK, PAIR), jnp.bfloat16),
            jax.ShapeDtypeStruct((RING_X, 2 * ROWS, PAIR), jnp.float32),
        ),
        in_specs=[SMEM, VMEM, VMEM],
        out_specs=(VMEM, VMEM),
        scratch_shapes=[
            pltpu.SMEM((most,), jnp.int32),
            pltpu.SMEM((most,), jnp.int32),
            pltpu.VMEM((blocks, BLK, PAIR), jnp.bfloat16),
            pltpu.VMEM((most, BLK, BLK), jnp.float32),
            square,
            square,
            square,
        ],
        compiler_params=pltpu.CompilerParams(vmem_limit_bytes=LIMIT),
        cost_estimate=pl.CostEstimate(
            flops=most * 4 * BLK * BLK * PAIR, bytes_accessed=kv.size * 4, transcendentals=most * BLK * BLK
        ),
        name="attend_forward",
    )(turns, qg.reshape(-1, BLK, PAIR), kv.reshape(-1, BLK, PAIR))


def backward_kernel(
    turn_ref, qg_ref, kv_ref, stats_ref, query_ref, key_ref, own_list, far_list, rhs, query, key
):
    count = list_pairs(turn_ref, own_list, far_list)
    rounds = lax.div(count + UNROLL - 1, UNROLL)
    lane = lax.broadcasted_iota(jnp.int32, (BLK, PAIR), 1)
    zero = jnp.zeros((BLK, PAIR), jnp.bfloat16)
    for block in range(qg_ref.shape[0]):
        pair = qg_ref[block]
        rhs[block, :BLK] = jnp.where(lane < HEAD, pair, zero)
        rhs[block, BLK:] = jnp.where(lane < HEAD, zero, pair)
    query[...] = jnp.zeros_like(query)
    key[...] = jnp.zeros_like(key)

    def step_of(step, carry):
        now = []
        for u in range(UNROLL):
            tile = step * UNROLL + u
            now.append((tile, own_list[tile], far_list[tile]))
        both = [
            lax.dot_general(
                kv_ref[far], rhs[own], (((1,), (1,)), ((), ())), preferred_element_type=jnp.float32
            )
            for _, own, far in now
        ]
        factors = []
        for (tile, own, _), product in zip(now, both):
            device, block = lax.div(own, ROWS), lax.rem(own, ROWS)
            top, inverse, drift = (
                stats_ref[device, pl.ds(kind * ROWS + block, 1), :] for kind in range(3)
            )
            masked = product[:, :BLK] * EXP2_SCALE + jnp.where(tile < count, 0.0, -jnp.inf)
            prob = jnp.exp2(masked - top) * inverse
            slope = prob * (product[:, BLK:] - drift)
            factors.append((slope.astype(jnp.bfloat16), prob.astype(jnp.bfloat16)))
        to_keys = [
            jnp.dot(jnp.concatenate(factor, axis=1), rhs[own], preferred_element_type=jnp.float32)
            for factor, (_, own, _) in zip(factors, now)
        ]
        to_queries = [
            lax.dot_general(
                slope, kv_ref[far], (((0,), (0,)), ((), ())), preferred_element_type=jnp.float32
            )
            for (slope, _), (_, _, far) in zip(factors, now)
        ]
        for (_, own, far), to_key, to_query in zip(now, to_keys, to_queries):
            key[far] += to_key
            query[own] += to_query
        return carry

    lax.fori_loop(0, rounds, step_of, 0)
    for block in range(key.shape[0]):
        key_ref[block] = jnp.where(lane < HEAD, key[block] * SCALE, key[block]).astype(jnp.bfloat16)
    for device in range(RING_X):
        for pair in range(ROWS // 2):
            even, odd = query[device * ROWS + 2 * pair], query[device * ROWS + 2 * pair + 1]
            query_ref[device, pair * BLK : (pair + 1) * BLK] = (
                jnp.where(lane < HEAD, even, pltpu.roll(odd, HEAD, 1)) * SCALE
            )


def attend_backward(turns, qg, kv, stats):
    most = most_pairs(turns)
    blocks, keys = RING_X * ROWS, kv.shape[0] * ROWS
    return pl.pallas_call(
        backward_kernel,
        out_shape=(
            jax.ShapeDtypeStruct((RING_X, ROWS // 2 * BLK, PAIR), jnp.float32),
            jax.ShapeDtypeStruct((keys, BLK, PAIR), jnp.bfloat16),
        ),
        in_specs=[SMEM, VMEM, VMEM, VMEM],
        out_specs=(VMEM, VMEM),
        scratch_shapes=[
            pltpu.SMEM((most,), jnp.int32),
            pltpu.SMEM((most,), jnp.int32),
            pltpu.VMEM((blocks, 2 * BLK, PAIR), jnp.bfloat16),
            pltpu.VMEM((blocks, BLK, PAIR), jnp.float32),
            pltpu.VMEM((keys, BLK, PAIR), jnp.float32),
        ],
        compiler_params=pltpu.CompilerParams(vmem_limit_bytes=LIMIT),
        cost_estimate=pl.CostEstimate(
            flops=most * 10 * BLK * BLK * PAIR, bytes_accessed=kv.size * 4, transcendentals=most * BLK * BLK
        ),
        name="attend_backward",
    )(turns, qg.reshape(-1, BLK, PAIR), kv.reshape(-1, BLK, PAIR), stats)


def combine_kernel(
    parts, tables, qg_ref, context, stats_ref, got, got_tables, send, recv, t_send, t_recv, s_send, s_recv
):
    _, _, at_y, at_x, _, count_y = places()
    along_x, _ = seq_partners(at_y, at_x, count_y)
    greet(along_x)
    steps = range(len(along_x))

    def give(step):
        target = lax.rem(at_x + step + 1, RING_X)
        return remote(parts.at[target], got.at[step], send.at[step], recv.at[step], along_x[step])

    def give_table(step):
        target = lax.rem(at_x + step + 1, RING_X)
        return remote(
            tables.at[target], got_tables.at[step], t_send.at[step], t_recv.at[step], along_x[step]
        )

    def tell(step, slot):
        part = stats_ref.at[slot]
        return remote(part, part, s_send.at[step], s_recv.at[step], along_x[step])

    for step in steps:
        give_table(step).start()
    for step in steps:
        give(step).start()
    for step in steps:
        give_table(step).wait_recv()
    lane = lax.broadcasted_iota(jnp.int32, (BLK, PAIR), 1)

    def values(start):
        rows = slice(start, start + BLK)
        found = [parts[at_x, rows]] + [got[step, rows] for step in steps]
        return [part.astype(jnp.float32) for part in found]

    both = [tables[at_x]] + [got_tables[step] for step in steps]
    tops, totals = [table[:ROWS] for table in both], [table[ROWS:] for table in both]
    top = functools.reduce(jnp.maximum, tops)
    factors = [jnp.exp2(part - top) for part in tops]
    inverse = 1.0 / sum(factor * part for factor, part in zip(factors, totals))
    shares = [factor * inverse for factor in factors]
    blank = jnp.zeros((BLK - ROWS * RING_X, PAIR), jnp.float32)
    columns = jnp.transpose(jnp.concatenate(shares + [blank], axis=0))
    drifts = jnp.zeros((BLK, PAIR), jnp.float32)
    for step in steps:
        give(step).wait_recv()
    for block in range(ROWS):
        output = jnp.zeros((BLK, PAIR), jnp.float32)
        for index, part in enumerate(values(block // 2 * BLK)):
            at = index * ROWS + block
            output += (part if block % 2 else pltpu.roll(part, HEAD, 1)) * columns[:, at : at + 1]
        output = jnp.where(lane < HEAD, 0.0, output)
        rows = slice(block * BLK, (block + 1) * BLK)
        context[rows] = output.astype(jnp.bfloat16)
        drift = jnp.sum(qg_ref[at_x, rows].astype(jnp.float32) * output, axis=1, keepdims=True)
        drifts = jnp.where(lane == block, drift, drifts)
    drift_rows = jnp.transpose(drifts)[: 2 * ROWS]
    stats_ref[at_x] = jnp.concatenate([top, inverse, drift_rows], axis=0)
    for step in steps:
        tell(step, at_x).start()
    for step in steps:
        tell(step, wrap(at_x - step - 1, RING_X)).wait_recv()
    for step in steps:
        give(step).wait_send()
        give_table(step).wait_send()
        tell(step, at_x).wait_send()


def combine(parts, tables, qg):
    sems = pltpu.SemaphoreType.DMA((RING_X - 1,))
    return pl.pallas_call(
        combine_kernel,
        out_shape=(
            jax.ShapeDtypeStruct((ROWS * BLK, PAIR), jnp.bfloat16),
            jax.ShapeDtypeStruct((RING_X, 4 * ROWS, PAIR), jnp.float32),
        ),
        in_specs=[VMEM, VMEM, VMEM],
        out_specs=(VMEM, VMEM),
        scratch_shapes=[
            pltpu.VMEM((RING_X - 1,) + parts.shape[1:], jnp.bfloat16),
            pltpu.VMEM((RING_X - 1,) + tables.shape[1:], jnp.float32),
        ]
        + [sems] * 6,
        compiler_params=pltpu.CompilerParams(
            collective_id=1, has_side_effects=True, vmem_limit_bytes=LIMIT
        ),
        name="combine",
    )(parts, tables, qg)


def sum_over_seq(parts, sums_refs, x_sum, arrived, from_y, piece, totals, *sems):
    _, _, at_y, at_x, _, count_y = places()
    along_x, along_y = seq_partners(at_y, at_x, count_y)
    xs, ys = range(len(along_x)), range(len(along_y))

    def in_x(step):
        source = parts.at[lax.rem(at_x + step + 1, RING_X)]
        return remote(source, arrived.at[step], sems[0].at[step], sems[1].at[step], along_x[step])

    def out_x(step, owner):
        part = totals.at[owner]
        return remote(part, part, sems[6].at[step], sems[7].at[step], along_x[step])

    def columns(index):
        return pl.ds(pl.multiple_of(index * PAIR, PAIR), PAIR)

    def in_y(step):
        source = x_sum.at[:, columns(lax.rem(at_y + step + 1, count_y))]
        return remote(source, from_y.at[step], sems[2].at[step], sems[3].at[step], along_y[step])

    def out_y(step, owner):
        target = totals.at[at_x, :, columns(owner)]
        return remote(piece, target, sems[4].at[step], sems[5].at[step], along_y[step])

    for step in xs:
        in_x(step).start()
    yield
    total = parts[at_x].astype(jnp.float32)
    for step in xs:
        in_x(step).wait_recv()
        total += arrived[step].astype(jnp.float32)
    x_sum[...] = total.astype(jnp.bfloat16)
    for step in ys:
        in_y(step).start()
    yield
    total = x_sum[:, columns(at_y)].astype(jnp.float32)
    for step in ys:
        in_y(step).wait_recv()
        total += from_y[step].astype(jnp.float32)
    piece[...] = total.astype(jnp.bfloat16)
    for step in ys:
        out_y(step, at_y).start()
    totals[at_x, :, columns(at_y)] = piece[...]
    yield
    for step in ys:
        out_y(step, wrap(at_y - step - 1, count_y)).wait_recv()
    for step in xs:
        out_x(step, at_x).start()
    yield
    for step in xs:
        out_x(step, wrap(at_x - step - 1, RING_X)).wait_recv()
    count = RING_X // len(sums_refs)
    for index in range(RING_X):
        height = totals.shape[1]
        rows = pl.ds(index % count * height, height)
        sums_refs[index // count][rows] = totals[index].astype(jnp.float32)
    for step in xs:
        in_x(step).wait_send()
        out_x(step, at_x).wait_send()
    for step in ys:
        in_y(step).wait_send()
        out_y(step, at_y).wait_send()


def gradient_kernel(
    query_parts,
    key_parts,
    context,
    features_ref,
    key_w,
    value_w,
    query_w,
    out_w,
    attended,
    grad_frames,
    sums_ref,
    features,
    weights,
    filled,
    loaded,
    joint,
    lhs,
    turned,
    got,
    key_sum,
    arrived,
    leaving,
    x_send,
    x_recv,
    y_send,
    y_recv,
    *refs,
):
    chip, core, at_y, at_x, chips, count_y = places()
    along_x, along_y = seq_partners(at_y, at_x, count_y)
    near = neighbours(at_y, at_x, count_y)
    fill = stack_rows((key_w, value_w, query_w, out_w), weights, filled)
    load = pltpu.make_async_copy(features_ref, features, loaded)
    for copy in fill + [load]:
        copy.start()
    greet(along_x + along_y + mp_partners(chip, core, chips))
    steps = range(len(along_x))

    def give(step):
        target = lax.rem(at_x + step + 1, RING_X)
        return remote(query_parts.at[target], got.at[step], x_send.at[step], x_recv.at[step], along_x[step])

    over_y = ring_sum(
        key_parts, key_sum, arrived, leaving, at_y, count_y, (near["y", 1], near["y", -1]), y_send, y_recv
    )
    take(over_y, 4)
    for step in steps:
        give(step).start()
    for copy in fill:
        copy.wait()

    def columns(tile):
        return pl.ds(pl.multiple_of(tile * PAIR, PAIR), PAIR)

    half = context.shape[0] // 2

    def turned_rows(target, source):
        target[:half] = half_rows_of(source, 1 - core)
        target[half:] = half_rows_of(source, core)

    def output_part(tile):
        return jnp.dot(turned[:, :PAIR], weights[PAIR:, columns(tile)], preferred_element_type=jnp.float32)

    def input_part(tile):
        return jnp.dot(turned[...], weights[:, columns(tile)], preferred_element_type=jnp.float32)

    turned_rows(turned.at[:, pl.ds(0, PAIR)], context)
    seq_refs = len(seq_scratch(count_y))
    mp_refs = (len(refs) - 2 * seq_refs) // 2
    early, late = refs[:seq_refs], refs[seq_refs : 2 * seq_refs]
    outputs = sum_over_mp(output_part, attended, *refs[2 * seq_refs : 2 * seq_refs + mp_refs])
    inputs = sum_over_mp(input_part, grad_frames, *refs[2 * seq_refs + mp_refs :])
    sums = [sums_ref.at[pl.ds(index * HEAD, HEAD)] for index in range(4)]
    over_seq = [
        sum_over_seq(early[0], sums[2:], *early[1:]),
        sum_over_seq(late[0], sums[:2], *late[1:]),
    ]
    width = D

    def store_product(target, first, values, at, lower, upper):
        turned = jnp.transpose(values.astype(jnp.float32)).astype(jnp.bfloat16)
        product = lax.dot_general(
            turned,
            features[at].reshape(width, values.shape[0]),
            (((1,), (1,)), ((), ())),
            preferred_element_type=jnp.float32,
        )
        height = target.shape[1]
        for index in range((upper - lower) // height):
            start = lower + index * height
            target[first + index] = product[start : start + height].astype(jnp.bfloat16)

    lane = lax.broadcasted_iota(jnp.int32, (BLK, PAIR), 1)
    for turn in range(chips):
        take(outputs, 2)
        take(over_y, 3)
        if turn == chips // 2:
            for step in steps:
                give(step).wait_recv()
            for pair in range(ROWS // 2):
                part = slice(pair * BLK, (pair + 1) * BLK)
                total = query_parts[at_x, part]
                for step in steps:
                    total += got[step, part]
                for block, value in ((2 * pair, total), (2 * pair + 1, pltpu.roll(total, HEAD, 1))):
                    rows = slice(block * BLK, (block + 1) * BLK)
                    value = value.astype(jnp.bfloat16)
                    joint[rows] = jnp.where(lane < HEAD, value, context[rows])
                    lhs[rows, PAIR:] = jnp.where(lane < HEAD, value, jnp.zeros_like(value))
            load.wait()
            store_product(early[0], 0, joint[...], 0, 0, HEAD)
            store_product(early[0], RING_X // 2, joint[...], 1, HEAD, PAIR)
            take(over_seq[0], 1)
    take(over_y, 1)
    lhs[:, :PAIR] = key_sum[...]
    turned_rows(turned, lhs)
    store_product(late[0], 0, key_sum[...], 0, 0, PAIR)
    take(over_seq[1], 1)
    take(over_seq[0], 1)
    take(inputs, chips)
    take(over_seq[1], 1)
    take(over_seq[0], 1)
    take(inputs, chips)
    take(over_seq[1], 1)
    take(over_seq[0], 1)
    take(outputs, 1)
    take(over_seq[1], 2)
    take(inputs, 1)
    finish(over_seq[0])
    finish(over_seq[1])
    finish(outputs)
    finish(inputs)
    finish(over_y)
    for step in steps:
        give(step).wait_send()


def seq_scratch(count_y):
    dma = pltpu.SemaphoreType.DMA
    x_ring, y_sems = dma((RING_X - 1,)), dma((count_y - 1,))
    height = 2 * HEAD // RING_X
    stack = pltpu.VMEM((RING_X, height, D), jnp.bfloat16)
    return [
        stack,
        pltpu.VMEM((height, D), jnp.bfloat16),
        pltpu.VMEM((RING_X - 1, height, D), jnp.bfloat16),
        pltpu.VMEM((count_y - 1, height, PAIR), jnp.bfloat16),
        pltpu.VMEM((height, PAIR), jnp.bfloat16),
        stack,
        x_ring,
        x_ring,
        y_sems,
        y_sems,
        y_sems,
        y_sems,
        x_ring,
        x_ring,
    ]


def sum_gradients(query_parts, key_parts, context, features, weights):
    peers = lax.axis_size("seq")
    rows = context.shape[0]
    count_y = peers // RING_X
    dma = pltpu.SemaphoreType.DMA
    x_sems, y_ring = dma((RING_X - 1,)), dma((count_y // 2, 2, 4))
    out = jax.ShapeDtypeStruct((HEAD, rows), jnp.bfloat16)

    def rounded(*shape):
        return pltpu.VMEM(shape, jnp.bfloat16)

    return pl.pallas_call(
        gradient_kernel,
        out_shape=(out, out, jax.ShapeDtypeStruct((RING_X * HEAD, D), jnp.float32)),
        in_specs=[VMEM] * 3 + [ANY] * 5,
        out_specs=(VMEM, VMEM, VMEM),
        scratch_shapes=[
            rounded(*features.shape),
            rounded(RING_X * HEAD, D),
            dma((4,)),
            dma,
            rounded(rows, PAIR),
            rounded(rows, 2 * PAIR),
            rounded(rows, 2 * PAIR),
            pltpu.VMEM((RING_X - 1,) + query_parts.shape[1:], jnp.float32),
            rounded(rows, PAIR),
            rounded(count_y // 2, 2, rows, PAIR),
            rounded(count_y // 2 - 1, 2, rows, PAIR),
            x_sems,
            x_sems,
            y_ring,
            y_ring,
        ]
        + seq_scratch(count_y)
        + seq_scratch(count_y)
        + sum_scratch(rows)
        + sum_scratch(rows),
        compiler_params=pltpu.CompilerParams(
            collective_id=2, has_side_effects=True, vmem_limit_bytes=LIMIT
        ),
        name="sum_gradients",
    )(query_parts, key_parts.reshape(count_y, rows, PAIR), context, features, *weights)


def on_device(frames, cotangent, query_weight, key_weight, value_weight, out_weight, turn_blocks):
    turns = jnp.transpose(turn_blocks, (0, 2, 1))
    weights = (key_weight, value_weight, query_weight, out_weight)
    features, kv, qg = project(frames, cotangent, weights)
    context, stats = combine(*attend_forward(turns, qg, kv), qg)
    query_parts, key_parts = attend_backward(turns, qg, kv, stats)
    attended, grad_frames, sums = sum_gradients(query_parts, key_parts, context, features, weights)
    grad_key, grad_value, grad_query, grad_out = (
        sums[index * HEAD : (index + 1) * HEAD] for index in range(4)
    )
    return attended.T, grad_frames.T, grad_query, grad_key, grad_value, grad_out


def solution(mesh):
    return jax.shard_map(
        on_device,
        mesh=mesh,
        in_specs=(
            P("seq", "mp"),
            P("seq", "mp"),
            P("mp", None),
            P("mp", None),
            P("mp", None),
            P("mp", None),
            P(),
        ),
        out_specs=(
            P("seq", "mp"),
            P("seq", "mp"),
            P("mp", None),
            P("mp", None),
            P("mp", None),
            P("mp", None),
        ),
        check_vma=False,
    )
```
